32 devices in a mesh: lon: 16 (over z, y, core), lat: 2 (over x).
Axes of the slice: x: 2, y: 2, z: 4, core: 2. Of those that a mesh axis runs over, the one named last changes fastest.
Arguments:
- heat_content: float32 [16, 256, 2048], P(None, 'lat', 'lon'), may hold values from -18 to 18
- eastern_current: float32 [16, 256, 2048], P(None, 'lat', 'lon'), may hold values from -12 to 12
- northern_current: float32 [16, 256, 2048], P(None, 'lat', 'lon'), may hold values from -12 to 12
- mixing_coefficient: float32 [16, 256, 2048], P(None, 'lat', 'lon'), may hold values from 0.1 to 1
- friction_coefficient: float32 [256, 2048], P('lat', 'lon'), may hold values from 0.05 to 0.5
- water_indicator: int32 [256, 2048], P('lat', 'lon'), may hold values from 0 to 1
- flooded_strata: int32 [256, 2048], P('lat', 'lon'), may hold values from 12 to 16
Outputs:
- temp_next: float32 [16, 256, 2048], P(None, 'lat', 'lon')
- u_next: float32 [16, 256, 2048], P(None, 'lat', 'lon')
- v_next: float32 [16, 256, 2048], P(None, 'lat', 'lon')
The draws below stay inside these ranges and needn't reach their ends.
All inputs are finite; a program needn't handle non-finite values.
Results may differ from the reference program's by a relative error of at most 0.0003.
Values sent between devices are 32-bit elements; how exact they have to be, the bound alone decides.
No kernel may reach another device: no remote copies, remote signals or barrier semaphores. Data moves between devices by JAX's collectives and lax.ppermute only.
A program may use at most 128 MiB of HBM per device.

```python
import math
import jax
import jax.numpy as jnp

STRATA_NUMBER = 16
CLAT = 128
CLON = 128
PARALLEL_NUMBER = 256
MERIDIAN_NUMBER = 2048


def draw_water_indicator(key, part):
    tile_key, cell_key = jax.random.split(jax.random.fold_in(key, 7))
    tile_rows = PARALLEL_NUMBER // (CLAT // 2)
    tile_cols = MERIDIAN_NUMBER // (CLON // 2)
    tile_land = jax.random.randint(tile_key, (tile_rows, tile_cols), 0, 2)
    tile_full = jnp.repeat(jnp.repeat(tile_land, CLAT // 2, axis=0), CLON // 2, axis=1)
    cell_draw = jax.random.randint(cell_key, (PARALLEL_NUMBER, MERIDIAN_NUMBER), 0, 10)
    return (tile_full * (cell_draw > 0)).astype(jnp.int32)


def with_ends(drawn, key, smallest, high):
    longest = drawn.shape.index(max(drawn.shape))
    spots = []
    for shift in (0, 1):
        where = [jax.random.randint(jax.random.fold_in(key, axis), (), 0, length) for axis, length in enumerate(drawn.shape)]
        where[longest] = (where[longest] + shift) % drawn.shape[longest]
        spots.append(tuple(where))
    return drawn.at[spots[0]].set(smallest).at[spots[1]].set(high)


def level_of(rng, extent, pieces, low, high):
    def one(dim, blocks):
        steps = jax.random.uniform(jax.random.fold_in(jax.random.fold_in(rng, 6), dim), (blocks,), jnp.float32, low / len(pieces), high / len(pieces))
        return jnp.repeat(jnp.exp(steps), extent[dim] // blocks).reshape((-1,) + (1,) * (len(extent) - dim - 1))

    level = one(*pieces[0])
    for cut in pieces[1:]:
        level = level * one(*cut)
    return level


def gaussian(rng, shape, width, most, pieces=(), kind=jnp.bfloat16):
    gain = level_of(rng, shape, pieces, -0.22, 0.18) if pieces else 1.0
    entries = jax.random.normal(rng, shape, jnp.float32) * width * gain
    return jnp.minimum(jnp.maximum(entries, -most), most).astype(kind)


def setup_inputs(seed: int = 0) -> dict:
    splits = jax.random.split(jax.random.key(seed), 8)
    return {
        "heat_content": gaussian(splits[0], (STRATA_NUMBER, PARALLEL_NUMBER, MERIDIAN_NUMBER), 3.0, 18.0, ((1, 2), (2, 16)), jnp.float32),
        "eastern_current": gaussian(splits[1], (STRATA_NUMBER, PARALLEL_NUMBER, MERIDIAN_NUMBER), 2.0, 12.0, ((1, 2), (2, 16)), jnp.float32),
        "northern_current": gaussian(splits[2], (STRATA_NUMBER, PARALLEL_NUMBER, MERIDIAN_NUMBER), 2.0, 12.0, ((1, 2), (2, 16)), jnp.float32),
        "mixing_coefficient": jnp.clip(jnp.exp(math.log(1.0) - 2.3025851 * jax.random.uniform(splits[3], (STRATA_NUMBER, PARALLEL_NUMBER, MERIDIAN_NUMBER), jnp.float32) ** level_of(splits[3], (STRATA_NUMBER, PARALLEL_NUMBER, MERIDIAN_NUMBER), ((1, 2), (2, 16)), -0.2, 0.2)), 0.1, 1.0),
        "friction_coefficient": jnp.clip(jnp.exp(math.log(0.5) - 2.3025851 * jax.random.uniform(splits[4], (PARALLEL_NUMBER, MERIDIAN_NUMBER), jnp.float32) ** level_of(splits[4], (PARALLEL_NUMBER, MERIDIAN_NUMBER), ((0, 2), (1, 16)), -0.2, 0.2)), 0.05, 0.5),
        "water_indicator": draw_water_indicator(jax.random.fold_in(splits[7], 71), 0),
        "flooded_strata": with_ends(jax.random.randint(splits[6], (PARALLEL_NUMBER, MERIDIAN_NUMBER), STRATA_NUMBER - STRATA_NUMBER // 4, STRATA_NUMBER + 1), jax.random.fold_in(splits[6], 1), STRATA_NUMBER - STRATA_NUMBER // 4, STRATA_NUMBER).astype(jnp.int32),
    }


DT = 0.25
GRAV = 0.1


def wet_mask(stratum_plane, stratum_number):
    level_index = jnp.arange(stratum_number, dtype=jnp.float32)[:, None, None]
    return (level_index < stratum_plane[None]).astype(jnp.float32)


def neighbours(field):
    return (field[:, 1:-1, 1:-1], field[:, 1:-1, 2:], field[:, 1:-1, :-2], field[:, 2:, 1:-1], field[:, :-2, 1:-1])


def tracer_step(tracer, u_field, v_field, diffus, wetness):
    t_mid, t_east, t_west, t_north, t_south = neighbours(tracer)
    u_mid, u_east, u_west, u_north, u_south = neighbours(u_field)
    v_mid, v_east, v_west, v_north, v_south = neighbours(v_field)
    k_mid, k_east, k_west, k_north, k_south = neighbours(diffus)
    w_mid, w_east, w_west, w_north, w_south = neighbours(wetness)
    flux_east = w_mid * w_east * (0.25 * (u_mid + u_east) * (t_mid + t_east) - 0.5 * (k_mid + k_east) * (t_east - t_mid))
    flux_west = w_mid * w_west * (0.25 * (u_west + u_mid) * (t_west + t_mid) - 0.5 * (k_west + k_mid) * (t_mid - t_west))
    flux_north = w_mid * w_north * (0.25 * (v_mid + v_north) * (t_mid + t_north) - 0.5 * (k_mid + k_north) * (t_north - t_mid))
    flux_south = w_mid * w_south * (0.25 * (v_south + v_mid) * (t_south + t_mid) - 0.5 * (k_south + k_mid) * (t_mid - t_south))
    flux_up = w_mid[1:] * w_mid[:-1] * 0.5 * (k_mid[1:] + k_mid[:-1]) * (t_mid[1:] - t_mid[:-1])
    zero_level = jnp.zeros_like(t_mid[:1])
    vertical = jnp.concatenate([flux_up, zero_level], 0) - jnp.concatenate([zero_level, flux_up], 0)
    return w_mid * (t_mid + DT * (flux_west - flux_east + flux_south - flux_north + vertical))


def laplace(field, wetness):
    f_mid, f_east, f_west, f_north, f_south = neighbours(field)
    w_mid, w_east, w_west, w_north, w_south = neighbours(wetness)
    return w_mid * (w_east * (f_east - f_mid) + w_west * (f_west - f_mid) + w_north * (f_north - f_mid) + w_south * (f_south - f_mid))


def momentum_step(u_field, v_field, pressure, wetness, friction_coefficient, coriolis):
    p_mid, p_east, p_west, p_north, p_south = neighbours(pressure)
    w_mid = wetness[:, 1:-1, 1:-1]
    u_mid = u_field[:, 1:-1, 1:-1]
    v_mid = v_field[:, 1:-1, 1:-1]
    u_new = w_mid * (u_mid + DT * (coriolis * v_mid - GRAV * 0.5 * (p_east - p_west) + friction_coefficient * laplace(u_field, wetness)))
    v_new = w_mid * (v_mid + DT * (-coriolis * u_mid - GRAV * 0.5 * (p_north - p_south) + friction_coefficient * laplace(v_field, wetness)))
    return u_new, v_new


def border_entire_mesh(field, sign_value):
    lon_wide = jnp.concatenate([field[..., -1:], field, field[..., :1]], -1)
    north_rows = lon_wide[:, -1:, ::-1] * sign_value
    south_rows = jnp.zeros_like(north_rows)
    return jnp.concatenate([south_rows, lon_wide, north_rows], 1)


def reference(heat_content, eastern_current, northern_current, mixing_coefficient, friction_coefficient, water_indicator, flooded_strata):
    stratum_plane = (water_indicator * flooded_strata).astype(jnp.float32)[None]
    depth_wide = border_entire_mesh(stratum_plane, 1.0)
    wetness = wet_mask(depth_wide[0], STRATA_NUMBER)
    scalar_bordered = border_entire_mesh(heat_content, 1.0)
    u_wide = border_entire_mesh(eastern_current, -1.0)
    v_wide = border_entire_mesh(northern_current, -1.0)
    k_wide = border_entire_mesh(mixing_coefficient, 1.0)
    temp_next = tracer_step(scalar_bordered, u_wide, v_wide, k_wide, wetness)
    pressure = jnp.cumsum(temp_next, axis=0)
    p_wide = border_entire_mesh(pressure, 1.0)
    row_index = jnp.arange(PARALLEL_NUMBER, dtype=jnp.float32)
    coriolis = jnp.sin(jnp.pi * ((row_index + 0.5) / PARALLEL_NUMBER - 0.5))[:, None]
    u_next, v_next = momentum_step(u_wide, v_wide, p_wide, wetness, friction_coefficient, coriolis)
    return temp_next, u_next, v_next
```

```python
import functools

import jax
import jax.numpy as jnp
from jax import lax
from jax.experimental import pallas as pl
from jax.experimental.pallas import tpu as pltpu
from jax.sharding import PartitionSpec as P

DT = 0.25
GRAV = 0.1
F32, BF16 = jnp.float32, jnp.bfloat16
PAD = 8
RIM = 128
TAIL = 112
CHUNK = 4


def lanes(x, by):
    by %= x.shape[1]
    return x if by == 0 else pltpu.roll(x, by, 1)


def sublanes(x, by):
    by %= x.shape[0]
    return x if by == 0 else pltpu.roll(x, by, 0)


def iota(shape, dim):
    return lax.broadcasted_iota(jnp.int32, shape, dim)


def halves(x):
    high = x.astype(BF16)
    return jnp.concatenate([high, (x - high.astype(F32)).astype(BF16)], 1)


def across(a, b):
    return lax.dot_general(a, b, (((1,), (1,)), ((), ())), preferred_element_type=F32)


def parity(axis):
    return lax.axis_index(axis) % 2 == 0


def pack_kernel(
    levels, t, u, v, kd, water_hbm, strata_hbm, friction_hbm,
    send_a, send_b, depth, drag, drag_ends, tv, uv, vv, kv,
    water, strata, ends, sem, plane_sem,
):
    rows, cols = depth.shape
    pieces, size = levels // CHUNK, CHUNK * rows
    planes = []
    for n, (src, dst) in enumerate(((water_hbm, water), (strata_hbm, strata), (friction_hbm, drag))):
        planes.append(pltpu.make_async_copy(src, dst, plane_sem.at[n]))
        planes[n].start()
    fields = ((t, tv), (kd, kv), (u, uv), (v, vv))
    for part in range(pieces):
        for f, (src, dst) in enumerate(fields):
            at = pl.ds(part * size, size)
            pltpu.make_async_copy(src.at[at], dst.at[at], sem.at[f, part]).start()

    shape = (8, 2 * cols)
    column = iota(shape, 1) & (cols - 1)
    chosen = (column == ((iota(shape, 0) + (cols - 2)) & (cols - 1))) & (iota(shape, 0) < 4)
    take = jnp.where(chosen, 1.0, 0.0).astype(BF16)

    for copy in planes:
        copy.wait()
    d = (water[...] * strata[...]).astype(F32)
    depth[...] = d
    drag[...] = DT * drag[...]
    drag_ends[...] = across(take, halves(drag[...]))
    d = across(take, halves(d))

    @pl.loop(0, pieces)
    def one_piece(part):
        at = pl.ds(pl.multiple_of(part * size, size), size)
        for f, (src, full) in enumerate(fields):
            pltpu.make_async_copy(src.at[at], full.at[at], sem.at[f, part]).wait()
            found = across(take, halves(full[at, :]))
            for n in range(CHUNK):
                to = pl.multiple_of(8 * (f * levels + part * CHUNK + n), 8)
                ends[pl.ds(to, 8), :] = found[:, n * cols : (n + 1) * cols]


    lon_even = parity("lon")
    for q, (f, near) in enumerate(
        ((0, True), (0, False), (1, True), (1, False), (2, True), (2, False), (3, True))
    ):
        east = ends[pl.ds(8 * levels * f + (1 if near else 0), levels, stride=8), :]
        west = ends[pl.ds(8 * levels * f + (2 if near else 3), levels, stride=8), :]
        at = pl.ds(q * levels, levels)
        send_a[at, :] = jnp.where(lon_even, east, west)
        send_b[at, :] = jnp.where(lon_even, west, east)
    tail = (RIM - TAIL, cols)
    sub = iota(tail, 0)

    def tail_of(near, far):
        near, far = (jnp.broadcast_to(d[r : r + 1], tail) for r in (near, far))
        return jnp.where(sub == 0, near, jnp.where(sub == 1, far, 0.0))

    east, west = tail_of(1, 0), tail_of(2, 3)
    send_a[pl.ds(TAIL, RIM - TAIL), :] = jnp.where(lon_even, east, west)
    send_b[pl.ds(TAIL, RIM - TAIL), :] = jnp.where(lon_even, west, east)


def shift_kernel(
    levels, t, u, v, kd, depth, tv, uv, vv, kv,
    tn, un, vn, kn, lat_a, lat_b, te, ke, ue, uw, ve, vw, coriolis, sem, row_sem, depth_sem,
):
    rows, cols = coriolis.shape
    copies = []
    lat_even = parity("lat")
    for side, message in enumerate((lat_a, lat_b)):
        north = lat_even if side == 0 else jnp.logical_not(lat_even)
        near = jnp.where(north, rows - 1, 0)
        far = jnp.where(north, rows - 2, 1)
        for q, (src, row) in enumerate(
            ((t, near), (t, far), (kd, near), (kd, far), (v, near), (v, far), (u, near))
        ):
            at = message.at[pl.ds(q * levels, levels)]
            copies.append(pltpu.make_async_copy(src.at[:, row], at, row_sem.at[side, q]))
        for n, row in enumerate((near, far)):
            at = message.at[pl.ds(TAIL + n, 1)]
            copies.append(pltpu.make_async_copy(depth.at[pl.ds(row, 1)], at, depth_sem.at[side, n]))
    for n, (src, dst) in enumerate(((t, tn), (v, vn), (kd, kn), (u, un))):
        here, north = pl.ds(0, rows - 1), pl.ds(1, rows - 1)
        copies.append(pltpu.make_async_copy(src.at[:, north], dst.at[:, here], sem.at[n]))
    for copy in copies:
        copy.start()

    row = iota((rows, cols), 0) + lax.axis_index("lat") * rows
    total = rows * lax.axis_size("lat")
    coriolis[...] = DT * jnp.sin(jnp.pi * ((row.astype(F32) + 0.5) / total - 0.5))
    shape = (2 * cols, 2 * cols)
    source, target = iota(shape, 0) & (cols - 1), iota(shape, 1)
    want = jnp.where(target < cols, target + 1, target - cols - 1)
    want = jnp.where(target == cols - 1, -1, want)
    both = jnp.where(source == want, 1.0, 0.0).astype(BF16)

    @pl.loop(0, levels)
    def one_level(k):
        at = pl.ds(pl.multiple_of(k * rows, rows), rows)
        for src, east in ((tv, te), (kv, ke)):
            east[at, :] = jnp.dot(halves(src[at, :]), both[:, :cols], preferred_element_type=F32)
        for src, east, west in ((uv, ue, uw), (vv, ve, vw)):
            moved = jnp.dot(halves(src[at, :]), both, preferred_element_type=F32)
            east[at, :] = moved[:, :cols]
            west[at, :] = moved[:, cols:]

    for copy in copies:
        copy.wait()


def corner_kernel(lat_a, lat_b, recv_a, recv_b, out_a, out_b):
    cols = recv_a.shape[1]
    lon_even, lat_even = parity("lon"), parity("lat")
    a, b = recv_a[...], recv_b[...]
    west, east = jnp.where(lon_even, b, a), jnp.where(lon_even, a, b)
    shape = (8, 2 * cols)
    lane, sub = iota(shape, 1) & (cols - 1), iota(shape, 0)
    chosen = ((sub == 0) & (lane == 0)) | ((sub == 1) & (lane == cols - 1))
    take = jnp.where(chosen, 1.0, 0.0).astype(BF16)
    west, east = across(take, halves(west)), across(take, halves(east))
    tail = (RIM - TAIL, cols)
    sub = iota(tail, 0)
    for n, (main, out) in enumerate(((lat_a, out_a), (lat_b, out_b))):
        north = lat_even if n == 0 else jnp.logical_not(lat_even)
        w = jnp.broadcast_to(jnp.where(north, west[1:2], west[0:1]), tail)
        e = jnp.broadcast_to(jnp.where(north, east[1:2], east[0:1]), tail)
        out[pl.ds(0, TAIL), :] = main[pl.ds(0, TAIL), :]
        end = jnp.where(sub == 2, w, jnp.where(sub == 3, e, 0.0))
        out[pl.ds(TAIL, RIM - TAIL), :] = jnp.where(sub < 2, main[pl.ds(TAIL, RIM - TAIL), :], end)


def inner_kernel(
    levels, strip, t, u, v, kd, tn, un, vn, kn, te, ke, ue, uw, ve, vw, depth, drag, coriolis,
    t_out, u_out, v_out,
    fn, gu, gv, back, de, dw, dn, dragn, p, up,
):
    rows, cols = depth.shape
    zero = jnp.zeros((PAD, cols), F32)
    for ref in (fn, gu, back):
        ref[pl.ds(0, PAD), :] = zero

    shape = (strip, cols)
    lane = iota(shape, 1)
    row = iota(shape, 0)
    starts = range(0, rows, strip)
    for r in starts:
        here = pl.ds(r, strip)
        d, f = depth[here, :], drag[here, :]
        de[here, :] = jnp.where(lane < cols - 1, jnp.minimum(d, lanes(d, -1)), 0.0)
        dw[here, :] = jnp.where(lane > 0, jnp.minimum(d, lanes(d, 1)), 0.0)
        if r + strip < rows:
            north = pl.ds(r + 1, strip)
            dn[here, :] = jnp.minimum(d, depth[north, :])
            dragn[here, :] = drag[north, :]
        else:
            dn[here, :] = jnp.where(row < strip - 1, jnp.minimum(d, sublanes(d, -1)), 0.0)
            dragn[here, :] = sublanes(f, -1)

    shape1 = (2 * cols, cols)
    source, target = iota(shape1, 0) & (cols - 1), iota(shape1, 1)
    slope_of = jnp.where(source == target + 1, 1.0, jnp.where(source == target - 1, -1.0, 0.0)).astype(BF16)

    up[...] = jnp.zeros(up.shape, F32)
    p[...] = jnp.zeros(p.shape, F32)

    @pl.loop(0, levels)
    def one_level(k):
        kf = k.astype(F32)
        base = pl.multiple_of(k * rows, rows)
        above = pl.multiple_of(jnp.minimum(k + 1, levels - 1) * rows, rows)
        for r in starts:
            here = pl.ds(base + r, strip)
            plane, padded, below = pl.ds(r, strip), pl.ds(PAD + r, strip), pl.ds(PAD + r - 1, strip)
            d = depth[plane, :]
            t0, u0, v0, k0 = t[here, :], u[here, :], v[here, :], kd[here, :]
            wet, wet_e, wet_n = d > kf, de[plane, :] > kf, dn[plane, :] > kf

            t1, u1, k1 = te[here, :], ue[here, :], ke[here, :]
            flux = 0.0625 * ((u0 + u1) * (t0 + t1)) - 0.125 * ((k0 + k1) * (t1 - t0))
            flux = jnp.where(wet_e, flux, 0.0)
            change = lanes(flux, 1) - flux
            wet_w = dw[plane, :] > kf
            lap_u = jnp.where(wet_e, u1 - u0, 0.0) + jnp.where(wet_w, uw[here, :] - u0, 0.0)
            lap_v = jnp.where(wet_e, ve[here, :] - v0, 0.0) + jnp.where(wet_w, vw[here, :] - v0, 0.0)

            t1, v1, k1 = tn[here, :], vn[here, :], kn[here, :]
            flux = 0.0625 * ((v0 + v1) * (t0 + t1)) - 0.125 * ((k0 + k1) * (t1 - t0))
            flux = jnp.where(wet_n, flux, 0.0)
            lap = jnp.where(wet_n, un[here, :] - u0, 0.0)
            lap2 = jnp.where(wet_n, v1 - v0, 0.0)
            fn[padded, :] = flux
            gu[padded, :] = lap
            gv[plane, :] = lap2
            change = change + (fn[below, :] - flux)
            lap_u = lap_u + (lap - gu[below, :])
            lap_v = lap_v + lap2

            higher = pl.ds(above + r, strip)
            rise = 0.125 * ((kd[higher, :] + k0) * (t[higher, :] - t0))
            rise = jnp.where(d > kf + 1.0, rise, 0.0)
            change = change + (rise - up[plane, :])
            up[plane, :] = rise

            t_next = jnp.where(wet, t0 + change, 0.0)
            t_out[here, :] = t_next
            p[padded, :] = p[padded, :] + t_next
            c, f = coriolis[plane, :], drag[plane, :]
            u_out[here, :] = u0 + (c * v0 + f * lap_u)
            v_out[here, :] = v0 + (f * lap_v - c * u0)
        middle = pl.ds(PAD, rows)
        back[middle, :] = 0.0125 * p[middle, :] - dragn[...] * gv[...]
        slope = jnp.dot(halves(p[middle, :]), slope_of, preferred_element_type=F32)
        for r in starts:
            plane, here = pl.ds(r, strip), pl.ds(base + r, strip)
            wet = depth[plane, :] > kf
            u_next = u_out[here, :] - 0.0125 * slope[r : r + strip]
            v_next = v_out[here, :] + back[pl.ds(PAD + r - 1, strip), :] - 0.0125 * p[pl.ds(PAD + r + 1, strip), :]
            u_out[here, :] = jnp.where(wet, u_next, 0.0)
            v_out[here, :] = jnp.where(wet, v_next, 0.0)


def border_kernel(
    levels, t_in, u_in, v_in,
    send_a, send_b, recv_a, recv_b, lat_a, lat_b, rim_a, rim_b, drag, drag_ends,
    t_out, u_out, v_out, tb, ub, vb, tr, ur, vr0, vr1, sem,
):
    rows, cols = drag.shape
    lon_even, lat_even = parity("lon"), parity("lat")
    is_top = lax.axis_index("lat") == lax.axis_size("lat") - 1

    def sides(even, a, b):
        a, b = a[...], b[...]
        return jnp.where(even, b, a), jnp.where(even, a, b)

    own_w, own_e = sides(lon_even, send_a, send_b)
    west, east = sides(lon_even, recv_a, recv_b)
    own_s, own_n = sides(lat_even, lat_a, lat_b)
    south, north = sides(lat_even, rim_a, rim_b)

    shape = (RIM, 2 * cols)
    unit = jnp.where((iota(shape, 1) & (cols - 1)) == iota(shape, 0), 1.0, 0.0).astype(BF16)
    tails = jnp.concatenate([south[TAIL:], north[TAIL:]], 0)
    ends = across(unit, halves(tails))
    sw, se = ends[:, 2:3], ends[:, 3:4]
    low, high = RIM - TAIL + 2, RIM - TAIL + 3
    nw, ne = ends[:, low : low + 1], ends[:, high : high + 1]
    line = iota((RIM, 1), 0)
    turn = jnp.where((line >= 4 * levels) & (line < 7 * levels), -1.0, 1.0)
    nw, ne = jnp.where(is_top, turn * ne, nw), jnp.where(is_top, turn * nw, ne)
    mirrored = turn * jnp.take_along_axis(north, cols - 1 - iota((RIM, cols), 1), axis=1)
    north = jnp.where(is_top, mirrored, north)

    four, half = (4 * levels, cols), 2 * levels

    def stack(q, blocks):
        return jnp.concatenate([x[q * levels : (q + 1) * levels] for x in blocks], 0)

    def lines(rows_of_one):
        return jnp.concatenate([jnp.broadcast_to(x, (levels, cols)) for x in rows_of_one], 0)

    outside, inside = (west, east, south, north), (own_w, own_e, own_s, own_n)
    t1, t2, k1, k2, n1, n2, s1 = (stack(q, outside) for q in range(7))
    t0, k0, n0, s0 = (stack(q, inside) for q in (0, 2, 4, 6))
    d1, d2 = (lines([x[TAIL + n : TAIL + n + 1] for x in outside]) for n in (0, 1))
    d0, d0b = (lines([x[TAIL + n : TAIL + n + 1] for x in inside]) for n in (0, 1))
    f0 = lines([drag_ends[2:3, :], drag_ends[1:2, :], drag[0:1, :], drag[rows - 1 : rows, :]])
    sub, lane = iota(four, 0), iota(four, 1)
    level_i = sub & (levels - 1)
    level = level_i.astype(F32)
    side = jnp.where((sub & levels) == 0, 1.0, -1.0)
    wet0, wet1 = level < d0, level < d1
    wet01, wet12 = level < jnp.minimum(d0, d1), level < jnp.minimum(d1, d2)

    def face(side, ua, ub, ta, tb, ka, kb):
        return side * (0.0625 * ((ua + ub) * (ta + tb))) - 0.125 * ((ka + kb) * (tb - ta))

    inward = jnp.where(wet01, face(side, n1, n0, t1, t0, k1, k0), 0.0)
    outer = jnp.where(wet12, face(side, n2, n1, t2, t1, k2, k1), 0.0)

    before, after = (sw, se, sw, nw), (nw, ne, se, ne)

    def beyond(x, at):
        lo, hi = (
            jnp.concatenate(
                [jnp.broadcast_to(c[n : n + m], (levels, 1)) for c, (n, m) in zip(cells, at)], 0
            )
            for cells in (before, after)
        )
        lo, hi = jnp.broadcast_to(lo, four), jnp.broadcast_to(hi, four)
        return jnp.where(lane == 0, lo, lanes(x, 1)), jnp.where(lane == cols - 1, hi, lanes(x, -1))

    t_w, t_e = beyond(t1, ((0, levels),) * 4)
    k_w, k_e = beyond(k1, ((2 * levels, levels),) * 4)
    s_w, s_e = beyond(s1, ((6 * levels, levels),) * 2 + ((4 * levels, levels),) * 2)
    d_w, d_e = beyond(d1, ((TAIL, 1),) * 4)
    flux_w = jnp.where(level < jnp.minimum(d_w, d1), face(1.0, s_w, s1, t_w, t1, k_w, k1), 0.0)
    flux_e = jnp.where(level < jnp.minimum(d1, d_e), face(1.0, s1, s_e, t1, t_e, k1, k_e), 0.0)
    rise = 0.125 * ((sublanes(k1, -1) + k1) * (sublanes(t1, -1) - t1))
    rise = jnp.where((level + 1.0 < d1) & (level_i < levels - 1), rise, 0.0)
    change = outer - inward + flux_w - flux_e + rise - sublanes(rise, 1)
    p1, dp0 = jnp.where(wet1, t1 + change, 0.0), inward
    step = 1
    while step < levels:
        p1 = p1 + jnp.where(level_i >= step, sublanes(p1, step), 0.0)
        dp0 = dp0 + jnp.where(level_i >= step, sublanes(dp0, step), 0.0)
        step *= 2
    dn = 0.0125 * (side * p1) + f0 * jnp.where(wet01, n1 - n0, 0.0)
    dn = jnp.where(wet0, dn, 0.0)
    dn2 = jnp.where(level < d0b, 0.0125 * (side * dp0), 0.0)
    slope = jnp.where(lane < cols - 1, lanes(dp0, -1), 0.0) - jnp.where(lane > 0, lanes(dp0, 1), 0.0)
    ds = f0 * jnp.where(wet01, s1 - s0, 0.0) - 0.0125 * slope
    ds = jnp.where(wet0, ds, 0.0)
    tr[...] = inward[half:]
    ur[...] = ds[half:]
    vr0[...] = dn[half:]
    vr1[...] = dn2[half:]

    columns = jnp.concatenate(
        [dn2[levels:half], dn[levels:half], dn[:levels], dn2[:levels],
         inward[levels:half], inward[:levels], ds[levels:half], ds[:levels]], 0,
    ).T
    shape = (2 * cols, 3 * cols)
    group, target = (iota(shape, 0) & (cols - 1)) >> 4, iota(shape, 1)
    want = jnp.full(shape, -1, jnp.int32)
    for g, at in enumerate(
        (2 * cols - 2, 2 * cols - 1, cols, cols + 1, cols - 1, 0, 3 * cols - 1, 2 * cols)
    ):
        want = jnp.where(group == g, at, want)
    place = jnp.where(target == want, 1.0, 0.0).astype(BF16)
    lane = iota((rows, cols), 1) & (levels - 1)

    tail = (8, cols)
    sub = iota(tail, 0)
    fields = ((t_in, t_out, tb), (u_in, u_out, ub), (v_in, v_out, vb))

    def copy_out(n, k):
        at = pl.ds(pl.multiple_of(k * rows, rows), rows)
        return pltpu.make_async_copy(fields[n][2].at[at], fields[n][1].at[at], sem.at[n, k])

    @pl.loop(0, levels)
    def one_level(k):
        base = pl.multiple_of(k * rows, rows)
        moved = jnp.dot(halves(jnp.where(lane == k, columns, 0.0)), place, preferred_element_type=F32)
        for n, (part, _, buf) in enumerate(fields):
            at = pl.ds(base, rows)
            buf[at, :] = part[at, :] + moved[:, n * cols : (n + 1) * cols]

            def row_of(ref, s):
                return jnp.broadcast_to(ref[pl.ds(s * levels + k, 1), :], tail)

            for s, (near, far, begin) in enumerate(((0, 1, 0), (7, 6, rows - 8))):
                add = jnp.where(sub == near, row_of((tr, ur, vr0)[n], s), 0.0)
                if n == 2:
                    add = jnp.where(sub == far, row_of(vr1, s), add)
                at = pl.ds(base + begin, 8)
                buf[at, :] = buf[at, :] + add
            copy_out(n, k).start()

    @pl.loop(0, levels)
    def finish(k):
        for n in range(3):
            copy_out(n, k).wait()


def on_device(t, u, v, kd, friction, water, strata):
    levels, rows, cols = t.shape
    lon_n, lat_n = lax.axis_size("lon"), lax.axis_size("lat")
    vmem = pl.BlockSpec(memory_space=pltpu.VMEM)
    hbm = pl.BlockSpec(memory_space=pltpu.HBM)
    params = pltpu.CompilerParams(vmem_limit_bytes=12 * 1024 * 1024)
    tall = levels * rows
    plane, message, stack = (rows, cols), (RIM, cols), (tall, cols)

    def in_hbm(*arrays):
        return [pltpu.with_memory_space_constraint(x, pltpu.HBM) for x in arrays]

    send_a, send_b, depth, drag, drag_ends, *fields = pl.pallas_call(
        functools.partial(pack_kernel, levels),
        out_shape=[pltpu.VMEM(s, F32) for s in (message, message, plane, plane, (8, cols)) + (stack,) * 4],
        in_specs=[hbm] * 7,
        out_specs=[vmem] * 9,
        scratch_shapes=[pltpu.VMEM(plane, jnp.int32)] * 2
        + [pltpu.VMEM((8 * 4 * levels, cols), F32)]
        + [pltpu.SemaphoreType.DMA((4, levels // CHUNK)), pltpu.SemaphoreType.DMA((3,))],
        compiler_params=params,
        name="pack",
    )(*in_hbm(*[x.reshape(stack) for x in (t, u, v, kd)], water, strata, friction))

    lon_pairs = [(i, i ^ 1) for i in range(lon_n)]
    lon_cross = [(i, (i + 1) % lon_n if i % 2 else (i - 1) % lon_n) for i in range(lon_n)]
    recv_a = lax.ppermute(send_a, "lon", lon_pairs)
    recv_b = lax.ppermute(send_b, "lon", lon_cross)

    *moved, lat_a, lat_b, te, ke, ue, uw, ve, vw, coriolis = pl.pallas_call(
        functools.partial(shift_kernel, levels),
        out_shape=[pltpu.VMEM((levels, rows, 1, cols), F32)] * 4 + [pltpu.VMEM((RIM, 1, cols), F32)] * 2
        + [pltpu.VMEM(stack, F32)] * 6 + [pltpu.VMEM(plane, F32)],
        in_specs=[hbm] * 4 + [vmem] * 5,
        out_specs=[vmem] * 13,
        scratch_shapes=[pltpu.SemaphoreType.DMA(x) for x in ((4,), (2, 7), (2, 2))],
        compiler_params=params,
        name="shift",
    )(*in_hbm(*[x.reshape(levels, rows, 1, cols) for x in (t, u, v, kd)]), depth.reshape(rows, 1, cols), *fields)
    moved = [x.reshape(stack) for x in moved]
    lat_a, lat_b = lat_a.reshape(message), lat_b.reshape(message)

    next_a, next_b = pl.pallas_call(
        corner_kernel,
        out_shape=[pltpu.VMEM(message, F32)] * 2,
        in_specs=[vmem] * 4,
        out_specs=[vmem] * 2,
        compiler_params=params,
        name="corners",
    )(lat_a, lat_b, recv_a, recv_b)
    lat_pairs = [(i, i ^ 1) for i in range(lat_n)]
    cross = []
    for m in range(lon_n):
        for i in range(1, lat_n - 1, 2):
            here, north = m * lat_n + i, m * lat_n + i + 1
            cross += [(here, north), (north, here)]
        cross.append((m * lat_n + lat_n - 1, (lon_n - 1 - m) * lat_n + lat_n - 1))
    rim_a = lax.ppermute(next_a, "lat", lat_pairs)
    rim_b = lax.ppermute(next_b, ("lon", "lat"), cross)

    padded = pltpu.VMEM((rows + 2 * PAD, cols), F32)
    flat = pltpu.VMEM(plane, F32)
    inner = pl.pallas_call(
        functools.partial(inner_kernel, levels, 32),
        out_shape=[pltpu.VMEM(stack, F32)] * 3,
        in_specs=[vmem] * 17,
        out_specs=[vmem] * 3,
        scratch_shapes=[padded, padded, flat, padded, flat, flat, flat, flat, padded, flat],
        compiler_params=params,
        cost_estimate=pl.CostEstimate(flops=100 * tall * cols, bytes_accessed=1 << 20, transcendentals=0),
        name="inner",
    )(*fields, *moved, te, ke, ue, uw, ve, vw, depth, drag, coriolis)

    rim_pair = pltpu.VMEM((2 * levels, cols), F32)
    outs = pl.pallas_call(
        functools.partial(border_kernel, levels),
        out_shape=[jax.ShapeDtypeStruct(stack, F32)] * 3,
        in_specs=[vmem] * 13,
        out_specs=[hbm] * 3,
        scratch_shapes=[pltpu.VMEM(stack, F32)] * 3
        + [rim_pair] * 4
        + [pltpu.SemaphoreType.DMA((3, levels))],
        compiler_params=params,
        name="border",
    )(*inner, send_a, send_b, recv_a, recv_b, lat_a, lat_b, rim_a, rim_b, drag, drag_ends)
    return tuple(x.reshape(levels, rows, cols) for x in outs)


def solution(mesh):
    stack, plane = P(None, "lat", "lon"), P("lat", "lon")
    return jax.shard_map(
        on_device,
        mesh=mesh,
        in_specs=(stack,) * 4 + (plane,) * 3,
        out_specs=(stack,) * 3,
        check_vma=False,
    )
```

```python
import functools

import jax
import jax.numpy as jnp
from jax import lax
from jax.experimental import pallas as pl
from jax.experimental.pallas import tpu as pltpu
from jax.sharding import PartitionSpec as P

DT = 0.25
GRAV = 0.1
F32, BF16 = jnp.float32, jnp.bfloat16
PAD = 8
RIM = 128
TAIL = 112
CHUNK = 4
STRIP = 32


def lanes(x, by):
    by %= x.shape[1]
    return x if by == 0 else pltpu.roll(x, by, 1)


def sublanes(x, by):
    by %= x.shape[0]
    return x if by == 0 else pltpu.roll(x, by, 0)


def iota(shape, dim):
    return lax.broadcasted_iota(jnp.int32, shape, dim)


def halves(x):
    high = x.astype(BF16)
    return jnp.concatenate([high, (x - high.astype(F32)).astype(BF16)], 1)


def across(a, b):
    return lax.dot_general(a, b, (((1,), (1,)), ((), ())), preferred_element_type=F32)


def parity(axis):
    return lax.axis_index(axis) % 2 == 0


def pack_kernel(
    levels, t, u, v, kd, water_hbm, strata_hbm, friction_hbm,
    send_a, send_b, depth, drag, drag_ends, tv, uv, vv, kv,
    water, strata, gathered, ends, sem, plane_sem,
):
    rows, cols = depth.shape
    pieces, size = levels // CHUNK, CHUNK * rows
    planes = []
    for n, (src, dst) in enumerate(((water_hbm, water), (strata_hbm, strata), (friction_hbm, drag))):
        planes.append(pltpu.make_async_copy(src, dst, plane_sem.at[n]))
        planes[n].start()
    fields = ((t, tv), (kd, kv), (u, uv), (v, vv))
    for part in range(pieces):
        for f, (src, dst) in enumerate(fields):
            at = pl.ds(part * size, size)
            pltpu.make_async_copy(src.at[at], dst.at[at], sem.at[f, part]).start()

    lane = iota((STRIP, cols), 1)
    edge = (lane < 2) | (lane >= cols - 2)
    strips = [pl.ds(r, STRIP) for r in range(0, rows, STRIP)]
    for copy in planes:
        copy.wait()
    for at in strips:
        d = (water[at, :] * strata[at, :]).astype(F32)
        depth[at, :] = d
        drag[at, :] = DT * drag[at, :]
        gathered[2, at, :] = lanes(d, 2)
        gathered[3, at, :] = lanes(drag[at, :], 2)
        gathered[0, at, :] = jnp.zeros((STRIP, cols), F32)
        gathered[1, at, :] = jnp.zeros((STRIP, cols), F32)

    @pl.loop(0, pieces)
    def one_piece(part):
        begin = pl.multiple_of(part * size, size)
        for f, (src, full) in enumerate(fields):
            pltpu.make_async_copy(src.at[pl.ds(begin, size)], full.at[pl.ds(begin, size)], sem.at[f, part]).wait()
            for r in range(0, rows, STRIP):
                acc = gathered[f // 2, pl.ds(r, STRIP), :]
                for n in range(CHUNK):
                    x = jnp.where(edge, full[pl.ds(begin + n * rows + r, STRIP), :], 0.0)
                    to = 8 * (part * CHUNK + n) + 4 * (f % 2) + 2
                    acc = acc + pltpu.roll(x, to & (cols - 1), 1)
                gathered[f // 2, pl.ds(r, STRIP), :] = acc

    for n in range(2):
        ends[pl.ds(n * rows, rows), :] = gathered[n, :, :].T
    d = gathered[2, :, :].T
    drag_ends[...] = gathered[3, :, :].T[0:8]

    lon_even = parity("lon")
    for q, (f, near) in enumerate(
        ((0, True), (0, False), (1, True), (1, False), (2, True), (2, False), (3, True))
    ):
        first = (f // 2) * rows + 4 * (f % 2)
        east = ends[pl.ds(first + (1 if near else 0), levels, stride=8), :]
        west = ends[pl.ds(first + (2 if near else 3), levels, stride=8), :]
        at = pl.ds(q * levels, levels)
        send_a[at, :] = jnp.where(lon_even, east, west)
        send_b[at, :] = jnp.where(lon_even, west, east)
    tail = (RIM - TAIL, cols)
    sub = iota(tail, 0)

    def tail_of(near, far):
        near, far = (jnp.broadcast_to(d[r : r + 1], tail) for r in (near, far))
        return jnp.where(sub == 0, near, jnp.where(sub == 1, far, 0.0))

    east, west = tail_of(1, 0), tail_of(2, 3)
    send_a[pl.ds(TAIL, RIM - TAIL), :] = jnp.where(lon_even, east, west)
    send_b[pl.ds(TAIL, RIM - TAIL), :] = jnp.where(lon_even, west, east)


def shift_kernel(
    levels, t, u, v, kd, depth, tv, uv, vv, kv,
    tn, un, vn, kn, lat_a, lat_b, te, ke, ue, uw, ve, vw, coriolis, sem, row_sem, depth_sem,
):
    rows, cols = coriolis.shape
    copies = []
    lat_even = parity("lat")
    for side, message in enumerate((lat_a, lat_b)):
        north = lat_even if side == 0 else jnp.logical_not(lat_even)
        near = jnp.where(north, rows - 1, 0)
        far = jnp.where(north, rows - 2, 1)
        for q, (src, row) in enumerate(
            ((t, near), (t, far), (kd, near), (kd, far), (v, near), (v, far), (u, near))
        ):
            at = message.at[pl.ds(q * levels, levels)]
            copies.append(pltpu.make_async_copy(src.at[:, row], at, row_sem.at[side, q]))
        for n, row in enumerate((near, far)):
            at = message.at[pl.ds(TAIL + n, 1)]
            copies.append(pltpu.make_async_copy(depth.at[pl.ds(row, 1)], at, depth_sem.at[side, n]))
    for n, (src, dst) in enumerate(((t, tn), (v, vn), (kd, kn), (u, un))):
        here, north = pl.ds(0, rows - 1), pl.ds(1, rows - 1)
        copies.append(pltpu.make_async_copy(src.at[:, north], dst.at[:, here], sem.at[n]))
    for copy in copies:
        copy.start()

    row = iota((rows, cols), 0) + lax.axis_index("lat") * rows
    total = rows * lax.axis_size("lat")
    coriolis[...] = DT * jnp.sin(jnp.pi * ((row.astype(F32) + 0.5) / total - 0.5))

    @pl.loop(0, levels)
    def one_level(k):
        for r in range(0, rows, STRIP):
            at = pl.ds(pl.multiple_of(k * rows, rows) + r, STRIP)
            for src, east in ((tv, te), (kv, ke), (uv, ue), (vv, ve)):
                east[at, :] = lanes(src[at, :], -1)
            for src, west in ((uv, uw), (vv, vw)):
                west[at, :] = lanes(src[at, :], 1)

    for copy in copies:
        copy.wait()


def corner_kernel(lat_a, lat_b, recv_a, recv_b, out_a, out_b):
    cols = recv_a.shape[1]
    lon_even, lat_even = parity("lon"), parity("lat")
    a, b = recv_a[...], recv_b[...]
    west, east = jnp.where(lon_even, b, a), jnp.where(lon_even, a, b)
    shape = (8, 2 * cols)
    lane, sub = iota(shape, 1) & (cols - 1), iota(shape, 0)
    chosen = ((sub == 0) & (lane == 0)) | ((sub == 1) & (lane == cols - 1))
    take = jnp.where(chosen, 1.0, 0.0).astype(BF16)
    west, east = across(take, halves(west)), across(take, halves(east))
    tail = (RIM - TAIL, cols)
    sub = iota(tail, 0)
    for n, (main, out) in enumerate(((lat_a, out_a), (lat_b, out_b))):
        north = lat_even if n == 0 else jnp.logical_not(lat_even)
        w = jnp.broadcast_to(jnp.where(north, west[1:2], west[0:1]), tail)
        e = jnp.broadcast_to(jnp.where(north, east[1:2], east[0:1]), tail)
        out[pl.ds(0, TAIL), :] = main[pl.ds(0, TAIL), :]
        end = jnp.where(sub == 2, w, jnp.where(sub == 3, e, 0.0))
        out[pl.ds(TAIL, RIM - TAIL), :] = jnp.where(sub < 2, main[pl.ds(TAIL, RIM - TAIL), :], end)


def inner_kernel(
    levels, strip, t, u, v, kd, tn, un, vn, kn, te, ke, ue, uw, ve, vw, depth, drag, coriolis,
    t_out, u_out, v_out,
    fn, gu, gv, back, de, dw, dn, dragn, p, up,
):
    rows, cols = depth.shape
    zero = jnp.zeros((PAD, cols), F32)
    for ref in (fn, gu, back):
        ref[pl.ds(0, PAD), :] = zero

    shape = (strip, cols)
    lane = iota(shape, 1)
    row = iota(shape, 0)
    starts = range(0, rows, strip)
    for r in starts:
        here = pl.ds(r, strip)
        d, f = depth[here, :], drag[here, :]
        de[here, :] = jnp.where(lane < cols - 1, jnp.minimum(d, lanes(d, -1)), 0.0)
        dw[here, :] = jnp.where(lane > 0, jnp.minimum(d, lanes(d, 1)), 0.0)
        if r + strip < rows:
            north = pl.ds(r + 1, strip)
            dn[here, :] = jnp.minimum(d, depth[north, :])
            dragn[here, :] = drag[north, :]
        else:
            dn[here, :] = jnp.where(row < strip - 1, jnp.minimum(d, sublanes(d, -1)), 0.0)
            dragn[here, :] = sublanes(f, -1)

    up[...] = jnp.zeros(up.shape, F32)
    p[...] = jnp.zeros(p.shape, F32)

    @pl.loop(0, levels)
    def one_level(k):
        kf = k.astype(F32)
        base = pl.multiple_of(k * rows, rows)
        above = pl.multiple_of(jnp.minimum(k + 1, levels - 1) * rows, rows)
        for r in starts:
            here = pl.ds(base + r, strip)
            plane, padded, below = pl.ds(r, strip), pl.ds(PAD + r, strip), pl.ds(PAD + r - 1, strip)
            d = depth[plane, :]
            t0, u0, v0, k0 = t[here, :], u[here, :], v[here, :], kd[here, :]
            wet, wet_e, wet_n = d > kf, de[plane, :] > kf, dn[plane, :] > kf

            t1, u1, k1 = te[here, :], ue[here, :], ke[here, :]
            flux = 0.0625 * ((u0 + u1) * (t0 + t1)) - 0.125 * ((k0 + k1) * (t1 - t0))
            flux = jnp.where(wet_e, flux, 0.0)
            change = lanes(flux, 1) - flux
            wet_w = dw[plane, :] > kf
            lap_u = jnp.where(wet_e, u1 - u0, 0.0) + jnp.where(wet_w, uw[here, :] - u0, 0.0)
            lap_v = jnp.where(wet_e, ve[here, :] - v0, 0.0) + jnp.where(wet_w, vw[here, :] - v0, 0.0)

            t1, v1, k1 = tn[here, :], vn[here, :], kn[here, :]
            flux = 0.0625 * ((v0 + v1) * (t0 + t1)) - 0.125 * ((k0 + k1) * (t1 - t0))
            flux = jnp.where(wet_n, flux, 0.0)
            lap = jnp.where(wet_n, un[here, :] - u0, 0.0)
            lap2 = jnp.where(wet_n, v1 - v0, 0.0)
            fn[padded, :] = flux
            gu[padded, :] = lap
            gv[plane, :] = lap2
            change = change + (fn[below, :] - flux)
            lap_u = lap_u + (lap - gu[below, :])
            lap_v = lap_v + lap2

            higher = pl.ds(above + r, strip)
            rise = 0.125 * ((kd[higher, :] + k0) * (t[higher, :] - t0))
            rise = jnp.where(d > kf + 1.0, rise, 0.0)
            change = change + (rise - up[plane, :])
            up[plane, :] = rise

            t_next = jnp.where(wet, t0 + change, 0.0)
            t_out[here, :] = t_next
            p[padded, :] = p[padded, :] + t_next
            c, f = coriolis[plane, :], drag[plane, :]
            u_out[here, :] = u0 + (c * v0 + f * lap_u)
            v_out[here, :] = v0 + (f * lap_v - c * u0)
        middle = pl.ds(PAD, rows)
        back[middle, :] = 0.0125 * p[middle, :] - dragn[...] * gv[...]
        for r in starts:
            plane, here = pl.ds(r, strip), pl.ds(base + r, strip)
            wet = depth[plane, :] > kf
            mid = p[pl.ds(PAD + r, strip), :]
            slope = jnp.where(lane < cols - 1, lanes(mid, -1), 0.0) - jnp.where(lane > 0, lanes(mid, 1), 0.0)
            u_next = u_out[here, :] - 0.0125 * slope
            v_next = v_out[here, :] + back[pl.ds(PAD + r - 1, strip), :] - 0.0125 * p[pl.ds(PAD + r + 1, strip), :]
            u_out[here, :] = jnp.where(wet, u_next, 0.0)
            v_out[here, :] = jnp.where(wet, v_next, 0.0)


def border_kernel(
    levels, t_in, u_in, v_in,
    send_a, send_b, recv_a, recv_b, lat_a, lat_b, rim_a, gathered, drag, drag_ends,
    t_out, u_out, v_out, tb, ub, vb, tr, ur, vr0, vr1, turned, rim_b, sem, rim_sem,
):
    rows, cols = drag.shape
    lon_even, lat_even = parity("lon"), parity("lat")
    lat = lax.axis_index("lat")
    is_top, is_bottom = lat == lax.axis_size("lat") - 1, lat == 0

    def sides(even, a, b):
        a, b = a[...], b[...]
        return jnp.where(even, b, a), jnp.where(even, a, b)

    west_half = lax.axis_index("lon") < lax.axis_size("lon") // 2
    first_of_pair = jnp.where(is_top | is_bottom, west_half, jnp.logical_not(lat_even))
    fetch = pltpu.make_async_copy(gathered.at[jnp.where(first_of_pair, 1, 0)], rim_b, rim_sem)
    fetch.start()
    fetch.wait()

    own_w, own_e = sides(lon_even, send_a, send_b)
    west, east = sides(lon_even, recv_a, recv_b)
    own_s, own_n = sides(lat_even, lat_a, lat_b)
    south, north = sides(lat_even, rim_a, rim_b)
    south = jnp.where(is_bottom, 0.0, south)

    shape = (RIM, 2 * cols)
    unit = jnp.where((iota(shape, 1) & (cols - 1)) == iota(shape, 0), 1.0, 0.0).astype(BF16)
    tails = jnp.concatenate([south[TAIL:], north[TAIL:]], 0)
    ends = across(unit, halves(tails))
    sw, se = ends[:, 2:3], ends[:, 3:4]
    low, high = RIM - TAIL + 2, RIM - TAIL + 3
    nw, ne = ends[:, low : low + 1], ends[:, high : high + 1]
    line = iota((RIM, 1), 0)
    turn = jnp.where((line >= 4 * levels) & (line < 7 * levels), -1.0, 1.0)
    nw, ne = jnp.where(is_top, turn * ne, nw), jnp.where(is_top, turn * nw, ne)
    mirrored = turn * jnp.take_along_axis(north, cols - 1 - iota((RIM, cols), 1), axis=1)
    north = jnp.where(is_top, mirrored, north)

    four, half = (4 * levels, cols), 2 * levels

    def stack(q, blocks):
        return jnp.concatenate([x[q * levels : (q + 1) * levels] for x in blocks], 0)

    def lines(rows_of_one):
        return jnp.concatenate([jnp.broadcast_to(x, (levels, cols)) for x in rows_of_one], 0)

    outside, inside = (west, east, south, north), (own_w, own_e, own_s, own_n)
    t1, t2, k1, k2, n1, n2, s1 = (stack(q, outside) for q in range(7))
    t0, k0, n0, s0 = (stack(q, inside) for q in (0, 2, 4, 6))
    d1, d2 = (lines([x[TAIL + n : TAIL + n + 1] for x in outside]) for n in (0, 1))
    d0, d0b = (lines([x[TAIL + n : TAIL + n + 1] for x in inside]) for n in (0, 1))
    f0 = lines([drag_ends[2:3, :], drag_ends[1:2, :], drag[0:1, :], drag[rows - 1 : rows, :]])
    sub, lane = iota(four, 0), iota(four, 1)
    level_i = sub & (levels - 1)
    level = level_i.astype(F32)
    side = jnp.where((sub & levels) == 0, 1.0, -1.0)
    wet0, wet1 = level < d0, level < d1
    wet01, wet12 = level < jnp.minimum(d0, d1), level < jnp.minimum(d1, d2)

    def face(side, ua, ub, ta, tb, ka, kb):
        return side * (0.0625 * ((ua + ub) * (ta + tb))) - 0.125 * ((ka + kb) * (tb - ta))

    inward = jnp.where(wet01, face(side, n1, n0, t1, t0, k1, k0), 0.0)
    outer = jnp.where(wet12, face(side, n2, n1, t2, t1, k2, k1), 0.0)

    before, after = (sw, se, sw, nw), (nw, ne, se, ne)

    def beyond(x, at):
        lo, hi = (
            jnp.concatenate(
                [jnp.broadcast_to(c[n : n + m], (levels, 1)) for c, (n, m) in zip(cells, at)], 0
            )
            for cells in (before, after)
        )
        lo, hi = jnp.broadcast_to(lo, four), jnp.broadcast_to(hi, four)
        return jnp.where(lane == 0, lo, lanes(x, 1)), jnp.where(lane == cols - 1, hi, lanes(x, -1))

    t_w, t_e = beyond(t1, ((0, levels),) * 4)
    k_w, k_e = beyond(k1, ((2 * levels, levels),) * 4)
    s_w, s_e = beyond(s1, ((6 * levels, levels),) * 2 + ((4 * levels, levels),) * 2)
    d_w, d_e = beyond(d1, ((TAIL, 1),) * 4)
    flux_w = jnp.where(level < jnp.minimum(d_w, d1), face(1.0, s_w, s1, t_w, t1, k_w, k1), 0.0)
    flux_e = jnp.where(level < jnp.minimum(d1, d_e), face(1.0, s1, s_e, t1, t_e, k1, k_e), 0.0)
    rise = 0.125 * ((sublanes(k1, -1) + k1) * (sublanes(t1, -1) - t1))
    rise = jnp.where((level + 1.0 < d1) & (level_i < levels - 1), rise, 0.0)
    change = outer - inward + flux_w - flux_e + rise - sublanes(rise, 1)
    p1, dp0 = jnp.where(wet1, t1 + change, 0.0), inward
    step = 1
    while step < levels:
        p1 = p1 + jnp.where(level_i >= step, sublanes(p1, step), 0.0)
        dp0 = dp0 + jnp.where(level_i >= step, sublanes(dp0, step), 0.0)
        step *= 2
    dn = 0.0125 * (side * p1) + f0 * jnp.where(wet01, n1 - n0, 0.0)
    dn = jnp.where(wet0, dn, 0.0)
    dn2 = jnp.where(level < d0b, 0.0125 * (side * dp0), 0.0)
    slope = jnp.where(lane < cols - 1, lanes(dp0, -1), 0.0) - jnp.where(lane > 0, lanes(dp0, 1), 0.0)
    ds = f0 * jnp.where(wet01, s1 - s0, 0.0) - 0.0125 * slope
    ds = jnp.where(wet0, ds, 0.0)
    tr[...] = inward[half:]
    ur[...] = ds[half:]
    vr0[...] = dn[half:]
    vr1[...] = dn2[half:]

    for g, x in enumerate(
        (dn2[levels:half], dn[levels:half], dn[:levels], dn2[:levels],
         inward[levels:half], inward[:levels], ds[levels:half], ds[:levels])
    ):
        turned[pl.ds(g, levels, stride=8), :] = x
    turned[...] = turned[...].T
    lane = iota((STRIP, cols), 1)
    one, wide = (lane < 1) | (lane >= cols - 1), (lane < 2) | (lane >= cols - 2)
    spots = ((one, cols - 1 - 4), (wide, cols - 2), (one, cols - 1 - 6))

    tail = (8, cols)
    sub = iota(tail, 0)
    fields = ((t_in, t_out, tb), (u_in, u_out, ub), (v_in, v_out, vb))

    def copy_out(n, k):
        at = pl.ds(pl.multiple_of(k * rows, rows), rows)
        return pltpu.make_async_copy(fields[n][2].at[at], fields[n][1].at[at], sem.at[n, k])

    @pl.loop(0, levels)
    def one_level(k):
        base = pl.multiple_of(k * rows, rows)
        for n, (part, _, buf) in enumerate(fields):
            mask, to = spots[n]
            by = (to - 8 * k) & (cols - 1)
            for r in range(0, rows, STRIP):
                at = pl.ds(base + r, STRIP)
                moved = pltpu.roll(turned[pl.ds(r, STRIP), :], by, 1)
                buf[at, :] = part[at, :] + jnp.where(mask, moved, 0.0)

            def row_of(ref, s):
                return jnp.broadcast_to(ref[pl.ds(s * levels + k, 1), :], tail)

            for s, (near, far, begin) in enumerate(((0, 1, 0), (7, 6, rows - 8))):
                add = jnp.where(sub == near, row_of((tr, ur, vr0)[n], s), 0.0)
                if n == 2:
                    add = jnp.where(sub == far, row_of(vr1, s), add)
                at = pl.ds(base + begin, 8)
                buf[at, :] = buf[at, :] + add
            copy_out(n, k).start()

    @pl.loop(0, levels)
    def finish(k):
        for n in range(3):
            copy_out(n, k).wait()


def on_device(t, u, v, kd, friction, water, strata):
    levels, rows, cols = t.shape
    lon_n, lat_n = lax.axis_size("lon"), lax.axis_size("lat")
    vmem = pl.BlockSpec(memory_space=pltpu.VMEM)
    hbm = pl.BlockSpec(memory_space=pltpu.HBM)
    params = pltpu.CompilerParams(vmem_limit_bytes=12 * 1024 * 1024)
    tall = levels * rows
    plane, message, stack = (rows, cols), (RIM, cols), (tall, cols)

    def in_hbm(*arrays):
        return [pltpu.with_memory_space_constraint(x, pltpu.HBM) for x in arrays]

    send_a, send_b, depth, drag, drag_ends, *fields = pl.pallas_call(
        functools.partial(pack_kernel, levels),
        out_shape=[pltpu.VMEM(s, F32) for s in (message, message, plane, plane, (8, cols)) + (stack,) * 4],
        in_specs=[hbm] * 7,
        out_specs=[vmem] * 9,
        scratch_shapes=[pltpu.VMEM(plane, jnp.int32)] * 2
        + [pltpu.VMEM((4, rows, cols), F32), pltpu.VMEM((2 * rows, cols), F32)]
        + [pltpu.SemaphoreType.DMA((4, levels // CHUNK)), pltpu.SemaphoreType.DMA((3,))],
        compiler_params=params,
        name="pack",
    )(*in_hbm(*[x.reshape(stack) for x in (t, u, v, kd)], water, strata, friction))

    lon_pairs = [(i, i ^ 1) for i in range(lon_n)]
    lon_cross = [(i, (i + 1) % lon_n if i % 2 else (i - 1) % lon_n) for i in range(lon_n)]
    recv_a = lax.ppermute(send_a, "lon", lon_pairs)
    recv_b = lax.ppermute(send_b, "lon", lon_cross)

    *moved, lat_a, lat_b, te, ke, ue, uw, ve, vw, coriolis = pl.pallas_call(
        functools.partial(shift_kernel, levels),
        out_shape=[pltpu.VMEM((levels, rows, 1, cols), F32)] * 4 + [pltpu.VMEM((RIM, 1, cols), F32)] * 2
        + [pltpu.VMEM(stack, F32)] * 6 + [pltpu.VMEM(plane, F32)],
        in_specs=[hbm] * 4 + [vmem] * 5,
        out_specs=[vmem] * 13,
        scratch_shapes=[pltpu.SemaphoreType.DMA(x) for x in ((4,), (2, 7), (2, 2))],
        compiler_params=params,
        name="shift",
    )(*in_hbm(*[x.reshape(levels, rows, 1, cols) for x in (t, u, v, kd)]), depth.reshape(rows, 1, cols), *fields)
    moved = [x.reshape(stack) for x in moved]
    lat_a, lat_b = lat_a.reshape(message), lat_b.reshape(message)

    next_a, next_b = pl.pallas_call(
        corner_kernel,
        out_shape=[pltpu.VMEM(message, F32)] * 2,
        in_specs=[vmem] * 4,
        out_specs=[vmem] * 2,
        compiler_params=params,
        name="corners",
    )(lat_a, lat_b, recv_a, recv_b)
    lat_pairs = [(i, i ^ 1) for i in range(lat_n)]
    cross = [[m * lat_n + i, m * lat_n + i + 1] for m in range(lon_n) for i in range(1, lat_n - 1, 2)]
    for i in (0, lat_n - 1):
        cross += [[m * lat_n + i, (lon_n - 1 - m) * lat_n + i] for m in range(lon_n // 2)]
    rim_b = lax.all_gather(next_b, ("lon", "lat"), axis_index_groups=cross)
    rim_a = lax.ppermute(next_a, "lat", lat_pairs)

    padded = pltpu.VMEM((rows + 2 * PAD, cols), F32)
    flat = pltpu.VMEM(plane, F32)
    inner = pl.pallas_call(
        functools.partial(inner_kernel, levels, 32),
        out_shape=[pltpu.VMEM(stack, F32)] * 3,
        in_specs=[vmem] * 17,
        out_specs=[vmem] * 3,
        scratch_shapes=[padded, padded, flat, padded, flat, flat, flat, flat, padded, flat],
        compiler_params=params,
        cost_estimate=pl.CostEstimate(flops=100 * tall * cols, bytes_accessed=1 << 20, transcendentals=0),
        name="inner",
    )(*fields, *moved, te, ke, ue, uw, ve, vw, depth, drag, coriolis)

    rim_pair = pltpu.VMEM((2 * levels, cols), F32)
    outs = pl.pallas_call(
        functools.partial(border_kernel, levels),
        out_shape=[jax.ShapeDtypeStruct(stack, F32)] * 3,
        in_specs=[vmem] * 10 + [hbm] + [vmem] * 2,
        out_specs=[hbm] * 3,
        scratch_shapes=[pltpu.VMEM(stack, F32)] * 3
        + [rim_pair] * 4
        + [pltpu.VMEM(plane, F32), pltpu.VMEM(message, F32)]
        + [pltpu.SemaphoreType.DMA((3, levels)), pltpu.SemaphoreType.DMA],
        compiler_params=params,
        name="border",
    )(*inner, send_a, send_b, recv_a, recv_b, lat_a, lat_b, rim_a, *in_hbm(rim_b), drag, drag_ends)
    return tuple(x.reshape(levels, rows, cols) for x in outs)


def solution(mesh):
    stack, plane = P(None, "lat", "lon"), P("lat", "lon")
    return jax.shard_map(
        on_device,
        mesh=mesh,
        in_specs=(stack,) * 4 + (plane,) * 3,
        out_specs=(stack,) * 3,
        check_vma=False,
    )
```

```python
import functools

import jax
import jax.numpy as jnp
from jax import lax
from jax.experimental import pallas as pl
from jax.experimental.pallas import tpu as pltpu
from jax.sharding import PartitionSpec as P

DT = 0.25
GRAV = 0.1
F32 = jnp.float32
PAD = 8
RIM = 128
TAIL = 112
CHUNK = 4
STRIP = 32


def lanes(x, by):
    by %= x.shape[1]
    return x if by == 0 else pltpu.roll(x, by, 1)


def sublanes(x, by):
    by %= x.shape[0]
    return x if by == 0 else pltpu.roll(x, by, 0)


def iota(shape, dim):
    return lax.broadcasted_iota(jnp.int32, shape, dim)


def parity(axis):
    return lax.axis_index(axis) % 2 == 0


def rows_kernel(
    levels, t, u, v, kd, water, strata, friction, lat_a, lat_b, coriolis, drag,
    water_rows, strata_rows, sem, plane_sem, drag_sem,
):
    rows, cols = coriolis.shape
    copies, planes = [], []
    lat_even = parity("lat")
    for side, message in enumerate((lat_a, lat_b)):
        north = lat_even if side == 0 else jnp.logical_not(lat_even)
        near = jnp.where(north, rows - 1, 0)
        far = jnp.where(north, rows - 2, 1)
        for n, row in enumerate((near, far)):
            for m, (src, dst) in enumerate(((water, water_rows), (strata, strata_rows))):
                at = dst.at[pl.ds(2 * side + n, 1)]
                planes.append(pltpu.make_async_copy(src.at[pl.ds(row, 1)], at, plane_sem.at[m, side, n]))
        for q, (src, row) in enumerate(
            ((t, near), (t, far), (kd, near), (kd, far), (v, near), (v, far), (u, near))
        ):
            at = message.at[pl.ds(q * levels, levels)]
            copies.append(pltpu.make_async_copy(src.at[:, row], at, sem.at[side, q]))
    whole = pltpu.make_async_copy(friction, drag, drag_sem)
    for copy in planes + copies + [whole]:
        copy.start()
    row = iota((rows, cols), 0) + lax.axis_index("lat") * rows
    total = rows * lax.axis_size("lat")
    coriolis[...] = DT * jnp.sin(jnp.pi * ((row.astype(F32) + 0.5) / total - 0.5))
    for copy in planes:
        copy.wait()
    for side, message in enumerate((lat_a, lat_b)):
        message[pl.ds(TAIL + 2, RIM - TAIL - 2)] = jnp.zeros((RIM - TAIL - 2, 1, cols), F32)
        for n in range(2):
            at = pl.ds(2 * side + n, 1)
            message[pl.ds(TAIL + n, 1)] = (water_rows[at] * strata_rows[at]).astype(F32)
    whole.wait()
    drag[...] = DT * drag[...]
    for copy in copies:
        copy.wait()


def pack_kernel(
    levels, t, u, v, kd, water, strata, drag,
    send_a, send_b, depth, drag_ends, gathered, ends,
):
    rows, cols = depth.shape
    lane = iota((STRIP, cols), 1)
    edge = (lane < 2) | (lane >= cols - 2)
    for r in range(0, rows, STRIP):
        at = pl.ds(r, STRIP)
        d = (water[at, :] * strata[at, :]).astype(F32)
        depth[at, :] = d
        gathered[2, at, :] = lanes(d, 2)
        gathered[3, at, :] = lanes(drag[at, :], 2)
        gathered[0, at, :] = jnp.zeros((STRIP, cols), F32)
        gathered[1, at, :] = jnp.zeros((STRIP, cols), F32)

    @pl.loop(0, levels // CHUNK)
    def one_piece(part):
        begin = pl.multiple_of(part * CHUNK * rows, rows)
        for f, full in enumerate((t, kd, u, v)):
            for r in range(0, rows, STRIP):
                acc = gathered[f // 2, pl.ds(r, STRIP), :]
                for n in range(CHUNK):
                    x = jnp.where(edge, full[pl.ds(begin + n * rows + r, STRIP), :], 0.0)
                    to = 8 * (part * CHUNK + n) + 4 * (f % 2) + 2
                    acc = acc + pltpu.roll(x, to & (cols - 1), 1)
                gathered[f // 2, pl.ds(r, STRIP), :] = acc

    for n in range(2):
        ends[pl.ds(n * rows, rows), :] = gathered[n, :, :].T
    d = gathered[2, :, :].T
    drag_ends[...] = gathered[3, :, :].T[0:8]

    lon_even, lat_even = parity("lon"), parity("lat")
    for q, (f, near) in enumerate(
        ((0, True), (0, False), (1, True), (1, False), (2, True), (2, False), (3, True))
    ):
        first = (f // 2) * rows + 4 * (f % 2)
        east = ends[pl.ds(first + (1 if near else 0), levels, stride=8), :]
        west = ends[pl.ds(first + (2 if near else 3), levels, stride=8), :]
        at = pl.ds(q * levels, levels)
        send_a[at, :] = jnp.where(lon_even, east, west)
        send_b[at, :] = jnp.where(lon_even, west, east)

    tail = (RIM - TAIL, cols)
    sub = iota(tail, 0)

    def tail_of(near, far):
        near, far = (jnp.broadcast_to(d[r : r + 1], tail) for r in (near, far))
        return jnp.where(sub == 0, near, jnp.where(sub == 1, far, 0.0))

    east, west = tail_of(1, 0), tail_of(2, 3)
    send_a[pl.ds(TAIL, RIM - TAIL), :] = jnp.where(lon_even, east, west)
    send_b[pl.ds(TAIL, RIM - TAIL), :] = jnp.where(lon_even, west, east)


def corner_kernel(levels, send_a, send_b, rim_a, rim_b, out_a, out_b):
    cols = send_a.shape[1]
    lon_even, lat_even = parity("lon"), parity("lat")
    a, b = rim_a[...], rim_b[...]
    south, north = jnp.where(lat_even, b, a).T, jnp.where(lat_even, a, b).T
    is_top = lax.axis_index("lat") == lax.axis_size("lat") - 1
    line = iota((1, cols), 1)
    turn = jnp.where((line >= 4 * levels) & (line < 7 * levels), -1.0, 1.0)
    first, last = north[0:1], north[cols - 1 : cols]
    first, last = jnp.where(is_top, turn * last, first), jnp.where(is_top, turn * first, last)
    tail = (RIM - TAIL, cols)
    sub = iota(tail, 0)
    for n, (main, out) in enumerate(((send_a, out_a), (send_b, out_b))):
        east = lon_even if n == 0 else jnp.logical_not(lon_even)
        s = jnp.broadcast_to(jnp.where(east, south[cols - 1 : cols], south[0:1]), tail)
        q = jnp.broadcast_to(jnp.where(east, last, first), tail)
        out[pl.ds(0, TAIL), :] = main[pl.ds(0, TAIL), :]
        depths = main[pl.ds(TAIL, RIM - TAIL), :]
        out[pl.ds(TAIL, RIM - TAIL), :] = jnp.where(sub == 2, s, jnp.where(sub == 3, q, depths))


def inner_kernel(
    levels, strip, t, u, v, kd, depth, drag, coriolis,
    t_out, u_out, v_out,
    fn, gu, gv, back, de, dw, dn, dragn, p, up,
):
    rows, cols = depth.shape
    zero = jnp.zeros((PAD, cols), F32)
    for ref in (fn, gu, back):
        ref[pl.ds(0, PAD), :] = zero

    shape = (strip, cols)
    lane = iota(shape, 1)
    row = iota(shape, 0)
    starts = range(0, rows, strip)
    for r in starts:
        here = pl.ds(r, strip)
        d, f = depth[here, :], drag[here, :]
        de[here, :] = jnp.where(lane < cols - 1, jnp.minimum(d, lanes(d, -1)), 0.0)
        dw[here, :] = jnp.where(lane > 0, jnp.minimum(d, lanes(d, 1)), 0.0)
        if r + strip < rows:
            north = pl.ds(r + 1, strip)
            dn[here, :] = jnp.minimum(d, depth[north, :])
            dragn[here, :] = drag[north, :]
        else:
            dn[here, :] = jnp.where(row < strip - 1, jnp.minimum(d, sublanes(d, -1)), 0.0)
            dragn[here, :] = sublanes(f, -1)

    up[...] = jnp.zeros(up.shape, F32)
    p[...] = jnp.zeros(p.shape, F32)

    @pl.loop(0, levels)
    def one_level(k):
        kf = k.astype(F32)
        base = pl.multiple_of(k * rows, rows)
        above = pl.multiple_of(jnp.minimum(k + 1, levels - 1) * rows, rows)
        for r in starts:
            here = pl.ds(base + r, strip)
            plane, padded, below = pl.ds(r, strip), pl.ds(PAD + r, strip), pl.ds(PAD + r - 1, strip)

            def north_of(ref, mid):
                return ref[pl.ds(base + r + 1, strip), :] if r + strip < rows else sublanes(mid, -1)

            d = depth[plane, :]
            t0, u0, v0, k0 = t[here, :], u[here, :], v[here, :], kd[here, :]
            wet, wet_e, wet_n = d > kf, de[plane, :] > kf, dn[plane, :] > kf

            t1, u1, k1 = lanes(t0, -1), lanes(u0, -1), lanes(k0, -1)
            flux = 0.0625 * ((u0 + u1) * (t0 + t1)) - 0.125 * ((k0 + k1) * (t1 - t0))
            flux = jnp.where(wet_e, flux, 0.0)
            change = lanes(flux, 1) - flux
            wet_w = dw[plane, :] > kf
            lap_u = jnp.where(wet_e, u1 - u0, 0.0) + jnp.where(wet_w, lanes(u0, 1) - u0, 0.0)
            lap_v = jnp.where(wet_e, lanes(v0, -1) - v0, 0.0) + jnp.where(wet_w, lanes(v0, 1) - v0, 0.0)

            t1, v1, k1 = north_of(t, t0), north_of(v, v0), north_of(kd, k0)
            flux = 0.0625 * ((v0 + v1) * (t0 + t1)) - 0.125 * ((k0 + k1) * (t1 - t0))
            flux = jnp.where(wet_n, flux, 0.0)
            lap = jnp.where(wet_n, north_of(u, u0) - u0, 0.0)
            lap2 = jnp.where(wet_n, v1 - v0, 0.0)
            fn[padded, :] = flux
            gu[padded, :] = lap
            gv[plane, :] = lap2
            change = change + (fn[below, :] - flux)
            lap_u = lap_u + (lap - gu[below, :])
            lap_v = lap_v + lap2

            higher = pl.ds(above + r, strip)
            rise = 0.125 * ((kd[higher, :] + k0) * (t[higher, :] - t0))
            rise = jnp.where(d > kf + 1.0, rise, 0.0)
            change = change + (rise - up[plane, :])
            up[plane, :] = rise

            t_next = jnp.where(wet, t0 + change, 0.0)
            t_out[here, :] = t_next
            p[padded, :] = p[padded, :] + t_next
            c, f = coriolis[plane, :], drag[plane, :]
            u_out[here, :] = u0 + (c * v0 + f * lap_u)
            v_out[here, :] = v0 + (f * lap_v - c * u0)
        middle = pl.ds(PAD, rows)
        back[middle, :] = 0.0125 * p[middle, :] - dragn[...] * gv[...]
        for r in starts:
            plane, here = pl.ds(r, strip), pl.ds(base + r, strip)
            wet = depth[plane, :] > kf
            mid = p[pl.ds(PAD + r, strip), :]
            slope = jnp.where(lane < cols - 1, lanes(mid, -1), 0.0) - jnp.where(lane > 0, lanes(mid, 1), 0.0)
            u_next = u_out[here, :] - 0.0125 * slope
            v_next = v_out[here, :] + back[pl.ds(PAD + r - 1, strip), :] - 0.0125 * p[pl.ds(PAD + r + 1, strip), :]
            u_out[here, :] = jnp.where(wet, u_next, 0.0)
            v_out[here, :] = jnp.where(wet, v_next, 0.0)


def border_kernel(
    levels, t_in, u_in, v_in,
    send_a, send_b, recv_a, recv_b, lat_a, lat_b, rim_a, rim_b, drag, drag_ends,
    t_out, u_out, v_out, tb, ub, vb, tr, ur, vr0, vr1, turned, sem,
):
    rows, cols = drag.shape
    lon_even, lat_even = parity("lon"), parity("lat")
    is_top = lax.axis_index("lat") == lax.axis_size("lat") - 1

    def sides(even, a, b):
        a, b = a[...], b[...]
        return jnp.where(even, b, a), jnp.where(even, a, b)

    own_w, own_e = sides(lon_even, send_a, send_b)
    west, east = sides(lon_even, recv_a, recv_b)
    own_s, own_n = sides(lat_even, lat_a, lat_b)
    south, north = sides(lat_even, rim_a, rim_b)

    low, high = TAIL + 2, TAIL + 3
    sw, nw = (west.T[:, n : n + 1] for n in (low, high))
    se, ne = (east.T[:, n : n + 1] for n in (low, high))
    line = iota((RIM, 1), 0)
    turn = jnp.where((line >= 4 * levels) & (line < 7 * levels), -1.0, 1.0)
    mirrored = turn * jnp.take_along_axis(north, cols - 1 - iota((RIM, cols), 1), axis=1)
    north = jnp.where(is_top, mirrored, north)

    four, half = (4 * levels, cols), 2 * levels

    def stack(q, blocks):
        return jnp.concatenate([x[q * levels : (q + 1) * levels] for x in blocks], 0)

    def lines(rows_of_one):
        return jnp.concatenate([jnp.broadcast_to(x, (levels, cols)) for x in rows_of_one], 0)

    outside, inside = (west, east, south, north), (own_w, own_e, own_s, own_n)
    t1, t2, k1, k2, n1, n2, s1 = (stack(q, outside) for q in range(7))
    t0, k0, n0, s0 = (stack(q, inside) for q in (0, 2, 4, 6))
    d1, d2 = (lines([x[TAIL + n : TAIL + n + 1] for x in outside]) for n in (0, 1))
    d0, d0b = (lines([x[TAIL + n : TAIL + n + 1] for x in inside]) for n in (0, 1))
    f0 = lines([drag_ends[2:3, :], drag_ends[1:2, :], drag[0:1, :], drag[rows - 1 : rows, :]])
    sub, lane = iota(four, 0), iota(four, 1)
    level_i = sub & (levels - 1)
    level = level_i.astype(F32)
    side = jnp.where((sub & levels) == 0, 1.0, -1.0)
    wet0, wet1 = level < d0, level < d1
    wet01, wet12 = level < jnp.minimum(d0, d1), level < jnp.minimum(d1, d2)

    def face(side, ua, ub, ta, tb, ka, kb):
        return side * (0.0625 * ((ua + ub) * (ta + tb))) - 0.125 * ((ka + kb) * (tb - ta))

    inward = jnp.where(wet01, face(side, n1, n0, t1, t0, k1, k0), 0.0)
    outer = jnp.where(wet12, face(side, n2, n1, t2, t1, k2, k1), 0.0)

    before, after = (sw, se, sw, nw), (nw, ne, se, ne)

    def beyond(x, at):
        lo, hi = (
            jnp.concatenate(
                [jnp.broadcast_to(c[n : n + m], (levels, 1)) for c, (n, m) in zip(cells, at)], 0
            )
            for cells in (before, after)
        )
        lo, hi = jnp.broadcast_to(lo, four), jnp.broadcast_to(hi, four)
        return jnp.where(lane == 0, lo, lanes(x, 1)), jnp.where(lane == cols - 1, hi, lanes(x, -1))

    t_w, t_e = beyond(t1, ((0, levels),) * 4)
    k_w, k_e = beyond(k1, ((2 * levels, levels),) * 4)
    s_w, s_e = beyond(s1, ((4 * levels, levels),) * 2 + ((6 * levels, levels),) * 2)
    d_w, d_e = beyond(d1, ((TAIL, 1),) * 4)
    flux_w = jnp.where(level < jnp.minimum(d_w, d1), face(1.0, s_w, s1, t_w, t1, k_w, k1), 0.0)
    flux_e = jnp.where(level < jnp.minimum(d1, d_e), face(1.0, s1, s_e, t1, t_e, k1, k_e), 0.0)
    rise = 0.125 * ((sublanes(k1, -1) + k1) * (sublanes(t1, -1) - t1))
    rise = jnp.where((level + 1.0 < d1) & (level_i < levels - 1), rise, 0.0)
    change = outer - inward + flux_w - flux_e + rise - sublanes(rise, 1)
    p1, dp0 = jnp.where(wet1, t1 + change, 0.0), inward
    step = 1
    while step < levels:
        p1 = p1 + jnp.where(level_i >= step, sublanes(p1, step), 0.0)
        dp0 = dp0 + jnp.where(level_i >= step, sublanes(dp0, step), 0.0)
        step *= 2
    dn = 0.0125 * (side * p1) + f0 * jnp.where(wet01, n1 - n0, 0.0)
    dn = jnp.where(wet0, dn, 0.0)
    dn2 = jnp.where(level < d0b, 0.0125 * (side * dp0), 0.0)
    slope = jnp.where(lane < cols - 1, lanes(dp0, -1), 0.0) - jnp.where(lane > 0, lanes(dp0, 1), 0.0)
    ds = f0 * jnp.where(wet01, s1 - s0, 0.0) - 0.0125 * slope
    ds = jnp.where(wet0, ds, 0.0)
    tr[...] = inward[half:]
    ur[...] = ds[half:]
    vr0[...] = dn[half:]
    vr1[...] = dn2[half:]

    for g, x in enumerate(
        (dn2[levels:half], dn[levels:half], dn[:levels], dn2[:levels],
         inward[levels:half], inward[:levels], ds[levels:half], ds[:levels])
    ):
        turned[pl.ds(g, levels, stride=8), :] = x
    turned[...] = turned[...].T
    lane = iota((STRIP, cols), 1)
    one, wide = (lane < 1) | (lane >= cols - 1), (lane < 2) | (lane >= cols - 2)
    spots = ((one, cols - 1 - 4), (wide, cols - 2), (one, cols - 1 - 6))

    tail = (8, cols)
    sub = iota(tail, 0)
    fields = ((t_in, t_out, tb), (u_in, u_out, ub), (v_in, v_out, vb))

    def copy_out(n, k):
        at = pl.ds(pl.multiple_of(k * rows, rows), rows)
        return pltpu.make_async_copy(fields[n][2].at[at], fields[n][1].at[at], sem.at[n, k])

    @pl.loop(0, levels)
    def one_level(k):
        base = pl.multiple_of(k * rows, rows)
        for n, (part, _, buf) in enumerate(fields):
            mask, to = spots[n]
            by = (to - 8 * k) & (cols - 1)
            for r in range(0, rows, STRIP):
                at = pl.ds(base + r, STRIP)
                moved = pltpu.roll(turned[pl.ds(r, STRIP), :], by, 1)
                buf[at, :] = part[at, :] + jnp.where(mask, moved, 0.0)

            def row_of(ref, s):
                return jnp.broadcast_to(ref[pl.ds(s * levels + k, 1), :], tail)

            for s, (near, far, begin) in enumerate(((0, 1, 0), (7, 6, rows - 8))):
                add = jnp.where(sub == near, row_of((tr, ur, vr0)[n], s), 0.0)
                if n == 2:
                    add = jnp.where(sub == far, row_of(vr1, s), add)
                at = pl.ds(base + begin, 8)
                buf[at, :] = buf[at, :] + add
            copy_out(n, k).start()

    @pl.loop(0, levels)
    def finish(k):
        for n in range(3):
            copy_out(n, k).wait()


def on_device(t, u, v, kd, friction, water, strata):
    levels, rows, cols = t.shape
    lon_n, lat_n = lax.axis_size("lon"), lax.axis_size("lat")
    vmem = pl.BlockSpec(memory_space=pltpu.VMEM)
    hbm = pl.BlockSpec(memory_space=pltpu.HBM)
    params = pltpu.CompilerParams(vmem_limit_bytes=12 * 1024 * 1024)
    tall = levels * rows
    plane, message, stack = (rows, cols), (RIM, cols), (tall, cols)

    def in_hbm(*arrays):
        return [pltpu.with_memory_space_constraint(x, pltpu.HBM) for x in arrays]

    lat_a, lat_b, coriolis, drag = pl.pallas_call(
        functools.partial(rows_kernel, levels),
        out_shape=[pltpu.VMEM((RIM, 1, cols), F32)] * 2 + [pltpu.VMEM(plane, F32)] * 2,
        in_specs=[hbm] * 7,
        out_specs=[vmem] * 4,
        scratch_shapes=[pltpu.VMEM((4, 1, cols), jnp.int32)] * 2
        + [pltpu.SemaphoreType.DMA((2, 7)), pltpu.SemaphoreType.DMA((2, 2, 2)), pltpu.SemaphoreType.DMA],
        compiler_params=params,
        name="rows",
    )(
        *in_hbm(*[x.reshape(levels, rows, 1, cols) for x in (t, u, v, kd)]),
        *in_hbm(*[x.reshape(rows, 1, cols) for x in (water, strata)], friction),
    )
    lat_a, lat_b = lat_a.reshape(message), lat_b.reshape(message)
    lat_pairs = [(i, i ^ 1) for i in range(lat_n)]
    cross = []
    for m in range(lon_n):
        for i in range(1, lat_n - 1, 2):
            here, north = m * lat_n + i, m * lat_n + i + 1
            cross += [(here, north), (north, here)]
        cross.append((m * lat_n + lat_n - 1, (lon_n - 1 - m) * lat_n + lat_n - 1))
    rim_b = lax.ppermute(lat_b, ("lon", "lat"), cross)
    rim_a = lax.ppermute(lat_a, "lat", lat_pairs)

    fields = [x.reshape(stack) for x in (t, u, v, kd)]
    send_a, send_b, depth, drag_ends = pl.pallas_call(
        functools.partial(pack_kernel, levels),
        out_shape=[pltpu.VMEM(s, F32) for s in (message, message, plane, (8, cols))],
        in_specs=[vmem] * 7,
        out_specs=[vmem] * 4,
        scratch_shapes=[pltpu.VMEM((4, rows, cols), F32), pltpu.VMEM((2 * rows, cols), F32)],
        compiler_params=params,
        name="pack",
    )(*fields, water, strata, drag)
    send_a, send_b = pl.pallas_call(
        functools.partial(corner_kernel, levels),
        out_shape=[pltpu.VMEM(message, F32)] * 2,
        in_specs=[vmem] * 4,
        out_specs=[vmem] * 2,
        compiler_params=params,
        name="corners",
    )(send_a, send_b, rim_a, rim_b)
    lon_pairs = [(i, i ^ 1) for i in range(lon_n)]
    lon_cross = [(i, (i + 1) % lon_n if i % 2 else (i - 1) % lon_n) for i in range(lon_n)]
    recv_b = lax.ppermute(send_b, "lon", lon_cross)
    recv_a = lax.ppermute(send_a, "lon", lon_pairs)

    padded = pltpu.VMEM((rows + 2 * PAD, cols), F32)
    flat = pltpu.VMEM(plane, F32)
    inner = pl.pallas_call(
        functools.partial(inner_kernel, levels, 32),
        out_shape=[pltpu.VMEM(stack, F32)] * 3,
        in_specs=[vmem] * 7,
        out_specs=[vmem] * 3,
        scratch_shapes=[padded, padded, flat, padded, flat, flat, flat, flat, padded, flat],
        compiler_params=params,
        cost_estimate=pl.CostEstimate(flops=100 * tall * cols, bytes_accessed=1 << 20, transcendentals=0),
        name="inner",
    )(*fields, depth, drag, coriolis)

    rim_pair = pltpu.VMEM((2 * levels, cols), F32)
    outs = pl.pallas_call(
        functools.partial(border_kernel, levels),
        out_shape=[jax.ShapeDtypeStruct(stack, F32)] * 3,
        in_specs=[vmem] * 13,
        out_specs=[hbm] * 3,
        scratch_shapes=[pltpu.VMEM(stack, F32)] * 3
        + [rim_pair] * 4
        + [pltpu.VMEM(plane, F32)]
        + [pltpu.SemaphoreType.DMA((3, levels))],
        compiler_params=params,
        name="border",
    )(*inner, send_a, send_b, recv_a, recv_b, lat_a, lat_b, rim_a, rim_b, drag, drag_ends)
    return tuple(x.reshape(levels, rows, cols) for x in outs)


def solution(mesh):
    stack, plane = P(None, "lat", "lon"), P("lat", "lon")
    return jax.shard_map(
        on_device,
        mesh=mesh,
        in_specs=(stack,) * 4 + (plane,) * 3,
        out_specs=(stack,) * 3,
        check_vma=False,
    )
```

```python
import functools

import jax
import jax.numpy as jnp
from jax import lax
from jax.experimental import pallas as pl
from jax.experimental.pallas import tpu as pltpu
from jax.sharding import PartitionSpec as P

DT = 0.25
GRAV = 0.1
F32 = jnp.float32
PAD = 8
RIM = 128
TAIL = 112
CHUNK = 4
STRIP = 32


def lanes(x, by):
    by %= x.shape[1]
    return x if by == 0 else pltpu.roll(x, by, 1)


def sublanes(x, by):
    by %= x.shape[0]
    return x if by == 0 else pltpu.roll(x, by, 0)


def iota(shape, dim):
    return lax.broadcasted_iota(jnp.int32, shape, dim)


def parity(axis):
    return lax.axis_index(axis) % 2 == 0


def rows_kernel(
    levels, t, u, v, kd, water, strata, friction, lat_a, lat_b, coriolis, drag,
    water_rows, strata_rows, sem, plane_sem, drag_sem,
):
    rows, cols = coriolis.shape
    copies, planes = [], []
    lat_even = parity("lat")
    for side, message in enumerate((lat_a, lat_b)):
        north = lat_even if side == 0 else jnp.logical_not(lat_even)
        near = jnp.where(north, rows - 1, 0)
        far = jnp.where(north, rows - 2, 1)
        for n, row in enumerate((near, far)):
            for m, (src, dst) in enumerate(((water, water_rows), (strata, strata_rows))):
                at = dst.at[pl.ds(2 * side + n, 1)]
                planes.append(pltpu.make_async_copy(src.at[pl.ds(row, 1)], at, plane_sem.at[m, side, n]))
        for q, (src, row) in enumerate(
            ((t, near), (t, far), (kd, near), (kd, far), (v, near), (v, far), (u, near))
        ):
            at = message.at[pl.ds(q * levels, levels)]
            copies.append(pltpu.make_async_copy(src.at[:, row], at, sem.at[side, q]))
    whole = pltpu.make_async_copy(friction, drag, drag_sem)
    for copy in planes + copies + [whole]:
        copy.start()
    row = iota((rows, cols), 0) + lax.axis_index("lat") * rows
    total = rows * lax.axis_size("lat")
    coriolis[...] = DT * jnp.sin(jnp.pi * ((row.astype(F32) + 0.5) / total - 0.5))
    for copy in planes:
        copy.wait()
    for side, message in enumerate((lat_a, lat_b)):
        message[pl.ds(TAIL + 2, RIM - TAIL - 2)] = jnp.zeros((RIM - TAIL - 2, 1, cols), F32)
        for n in range(2):
            at = pl.ds(2 * side + n, 1)
            message[pl.ds(TAIL + n, 1)] = (water_rows[at] * strata_rows[at]).astype(F32)
    whole.wait()
    drag[...] = DT * drag[...]
    for copy in copies:
        copy.wait()


def pack_kernel(
    levels, t, u, v, kd, water, strata, drag,
    send_a, send_b, depth, drag_ends, gathered, ends,
):
    rows, cols = depth.shape
    lane = iota((STRIP, cols), 1)
    edge = (lane < 2) | (lane >= cols - 2)
    for r in range(0, rows, STRIP):
        at = pl.ds(r, STRIP)
        d = (water[at, :] * strata[at, :]).astype(F32)
        depth[at, :] = d
        gathered[2, at, :] = lanes(d, 2)
        gathered[3, at, :] = lanes(drag[at, :], 2)
        gathered[0, at, :] = jnp.zeros((STRIP, cols), F32)
        gathered[1, at, :] = jnp.zeros((STRIP, cols), F32)

    @pl.loop(0, levels // CHUNK)
    def one_piece(part):
        begin = pl.multiple_of(part * CHUNK * rows, rows)
        for f, full in enumerate((t, kd, u, v)):
            for r in range(0, rows, STRIP):
                acc = gathered[f // 2, pl.ds(r, STRIP), :]
                for n in range(CHUNK):
                    x = jnp.where(edge, full[pl.ds(begin + n * rows + r, STRIP), :], 0.0)
                    to = 8 * (part * CHUNK + n) + 4 * (f % 2) + 2
                    acc = acc + pltpu.roll(x, to & (cols - 1), 1)
                gathered[f // 2, pl.ds(r, STRIP), :] = acc

    for n in range(2):
        ends[pl.ds(n * rows, rows), :] = gathered[n, :, :].T
    d = gathered[2, :, :].T
    drag_ends[...] = gathered[3, :, :].T[0:8]

    lon_even, lat_even = parity("lon"), parity("lat")
    for q, (f, near) in enumerate(
        ((0, True), (0, False), (1, True), (1, False), (2, True), (2, False), (3, True))
    ):
        first = (f // 2) * rows + 4 * (f % 2)
        east = ends[pl.ds(first + (1 if near else 0), levels, stride=8), :]
        west = ends[pl.ds(first + (2 if near else 3), levels, stride=8), :]
        at = pl.ds(q * levels, levels)
        send_a[at, :] = jnp.where(lon_even, east, west)
        send_b[at, :] = jnp.where(lon_even, west, east)

    tail = (RIM - TAIL, cols)
    sub = iota(tail, 0)

    def tail_of(near, far):
        near, far = (jnp.broadcast_to(d[r : r + 1], tail) for r in (near, far))
        return jnp.where(sub == 0, near, jnp.where(sub == 1, far, 0.0))

    east, west = tail_of(1, 0), tail_of(2, 3)
    send_a[pl.ds(TAIL, RIM - TAIL), :] = jnp.where(lon_even, east, west)
    send_b[pl.ds(TAIL, RIM - TAIL), :] = jnp.where(lon_even, west, east)


def corner_kernel(levels, send_a, send_b, rim_b, rim_a, when, out_a, out_b):
    cols = send_a.shape[1]
    lon_even, lat_even = parity("lon"), parity("lat")
    a, b = rim_a[...], rim_b[...]
    b = jnp.where(lax.axis_index("lat") == 0, 0.0, b)
    south, north = jnp.where(lat_even, b, a).T, jnp.where(lat_even, a, b).T
    is_top = lax.axis_index("lat") == lax.axis_size("lat") - 1
    line = iota((1, cols), 1)
    turn = jnp.where((line >= 4 * levels) & (line < 7 * levels), -1.0, 1.0)
    first, last = north[0:1], north[cols - 1 : cols]
    first, last = jnp.where(is_top, turn * last, first), jnp.where(is_top, turn * first, last)
    tail = (RIM - TAIL, cols)
    sub = iota(tail, 0)
    for n, (main, out) in enumerate(((send_a, out_a), (send_b, out_b))):
        east = lon_even if n == 0 else jnp.logical_not(lon_even)
        s = jnp.broadcast_to(jnp.where(east, south[cols - 1 : cols], south[0:1]), tail)
        q = jnp.broadcast_to(jnp.where(east, last, first), tail)
        out[pl.ds(0, TAIL), :] = main[pl.ds(0, TAIL), :]
        depths = main[pl.ds(TAIL, RIM - TAIL), :]
        out[pl.ds(TAIL, RIM - TAIL), :] = jnp.where(sub == 2, s, jnp.where(sub == 3, q, depths))


def inner_kernel(
    levels, first, last, strip, t, u, v, kd, depth, drag, coriolis, p_in, up_in,
    t_out, u_out, v_out, p, up,
    fn, gu, gv, back, fn2, gu2, gv2, back2, p2, de, dw, dn, dragn,
):
    rows, cols = depth.shape
    zero = jnp.zeros((PAD, cols), F32)
    for ref in (fn, gu, back, fn2, gu2, back2, p2):
        ref[pl.ds(0, PAD), :] = zero
    p2[pl.ds(PAD + rows, PAD), :] = zero

    shape = (strip, cols)
    lane = iota(shape, 1)
    row = iota(shape, 0)
    starts = range(0, rows, strip)
    for r in starts:
        here = pl.ds(r, strip)
        d, f = depth[here, :], drag[here, :]
        de[here, :] = jnp.where(lane < cols - 1, jnp.minimum(d, lanes(d, -1)), 0.0)
        dw[here, :] = jnp.where(lane > 0, jnp.minimum(d, lanes(d, 1)), 0.0)
        if r + strip < rows:
            north = pl.ds(r + 1, strip)
            dn[here, :] = jnp.minimum(d, depth[north, :])
            dragn[here, :] = drag[north, :]
        else:
            dn[here, :] = jnp.where(row < strip - 1, jnp.minimum(d, sublanes(d, -1)), 0.0)
            dragn[here, :] = sublanes(f, -1)

    up[...] = jnp.zeros(up.shape, F32) if p_in is None else up_in[...]
    p[...] = jnp.zeros(p.shape, F32) if p_in is None else p_in[...]

    def one_level(k, before, p, fn, gu, gv, back):
        kf = k.astype(F32)
        base = pl.multiple_of(k * rows, rows)
        above = pl.multiple_of(jnp.minimum(k + 1, levels - 1) * rows, rows)
        begin = pl.multiple_of((k - first) * rows, rows)
        for r in starts:
            here, out = pl.ds(base + r, strip), pl.ds(begin + r, strip)
            plane, padded, below = pl.ds(r, strip), pl.ds(PAD + r, strip), pl.ds(PAD + r - 1, strip)

            def north_of(ref, mid):
                return ref[pl.ds(base + r + 1, strip), :] if r + strip < rows else sublanes(mid, -1)

            d = depth[plane, :]
            t0, u0, v0, k0 = t[here, :], u[here, :], v[here, :], kd[here, :]
            wet, wet_e, wet_n = d > kf, de[plane, :] > kf, dn[plane, :] > kf

            t1, u1, k1 = lanes(t0, -1), lanes(u0, -1), lanes(k0, -1)
            flux = 0.0625 * ((u0 + u1) * (t0 + t1)) - 0.125 * ((k0 + k1) * (t1 - t0))
            flux = jnp.where(wet_e, flux, 0.0)
            change = lanes(flux, 1) - flux
            wet_w = dw[plane, :] > kf
            lap_u = jnp.where(wet_e, u1 - u0, 0.0) + jnp.where(wet_w, lanes(u0, 1) - u0, 0.0)
            lap_v = jnp.where(wet_e, lanes(v0, -1) - v0, 0.0) + jnp.where(wet_w, lanes(v0, 1) - v0, 0.0)

            t1, v1, k1 = north_of(t, t0), north_of(v, v0), north_of(kd, k0)
            flux = 0.0625 * ((v0 + v1) * (t0 + t1)) - 0.125 * ((k0 + k1) * (t1 - t0))
            flux = jnp.where(wet_n, flux, 0.0)
            lap = jnp.where(wet_n, north_of(u, u0) - u0, 0.0)
            lap2 = jnp.where(wet_n, v1 - v0, 0.0)
            fn[padded, :] = flux
            gu[padded, :] = lap
            gv[plane, :] = lap2
            change = change + (fn[below, :] - flux)
            lap_u = lap_u + (lap - gu[below, :])
            lap_v = lap_v + lap2

            higher = pl.ds(above + r, strip)
            rise = 0.125 * ((kd[higher, :] + k0) * (t[higher, :] - t0))
            rise = jnp.where(d > kf + 1.0, rise, 0.0)
            change = change + (rise - up[plane, :])
            up[plane, :] = rise

            t_next = jnp.where(wet, t0 + change, 0.0)
            t_out[out, :] = t_next
            p[padded, :] = before[padded, :] + t_next
            c, f = coriolis[plane, :], drag[plane, :]
            u_out[out, :] = u0 + (c * v0 + f * lap_u)
            v_out[out, :] = v0 + (f * lap_v - c * u0)

        def finish():
            middle = pl.ds(PAD, rows)
            back[middle, :] = 0.0125 * p[middle, :] - dragn[...] * gv[...]
            for r in starts:
                plane, out = pl.ds(r, strip), pl.ds(begin + r, strip)
                wet = depth[plane, :] > kf
                mid = p[pl.ds(PAD + r, strip), :]
                slope = jnp.where(lane < cols - 1, lanes(mid, -1), 0.0) - jnp.where(lane > 0, lanes(mid, 1), 0.0)
                u_next = u_out[out, :] - 0.0125 * slope
                v_next = v_out[out, :] + back[pl.ds(PAD + r - 1, strip), :] - 0.0125 * p[pl.ds(PAD + r + 1, strip), :]
                u_out[out, :] = jnp.where(wet, u_next, 0.0)
                v_out[out, :] = jnp.where(wet, v_next, 0.0)

        return finish

    @pl.loop(first, last, step=2)
    def two_levels(k):
        finish = one_level(k, p, p2, fn, gu, gv, back)
        finish2 = one_level(k + 1, p2, p, fn2, gu2, gv2, back2)
        finish()
        finish2()


def low_kernel(levels, half, strip, *refs):
    inner_kernel(levels, 0, half, strip, *refs[:7], None, None, *refs[7:])


def high_kernel(levels, half, strip, *refs):
    inner_kernel(levels, half, levels, strip, *refs[:9], *refs[10:])


def border_kernel(
    levels, t_low, u_low, v_low, t_high, u_high, v_high,
    send_a, send_b, recv_a, recv_b, lat_a, lat_b, rim_a, rim_b, drag, drag_ends,
    t_out, u_out, v_out, tb, ub, vb, tr, ur, vr0, vr1, turned, turned_t, sem,
):
    rows, cols = drag.shape
    lon_even, lat_even = parity("lon"), parity("lat")
    is_top = lax.axis_index("lat") == lax.axis_size("lat") - 1

    def sides(even, a, b):
        a, b = a[...], b[...]
        return jnp.where(even, b, a), jnp.where(even, a, b)

    own_w, own_e = sides(lon_even, send_a, send_b)
    west, east = sides(lon_even, recv_a, recv_b)
    own_s, own_n = sides(lat_even, lat_a, lat_b)
    south, north = sides(lat_even, rim_a, rim_b)
    south = jnp.where(lax.axis_index("lat") == 0, 0.0, south)

    low, high = TAIL + 2, TAIL + 3
    sw, nw = (west.T[:, n : n + 1] for n in (low, high))
    se, ne = (east.T[:, n : n + 1] for n in (low, high))
    line = iota((RIM, 1), 0)
    turn = jnp.where((line >= 4 * levels) & (line < 7 * levels), -1.0, 1.0)
    mirrored = turn * jnp.take_along_axis(north, cols - 1 - iota((RIM, cols), 1), axis=1)
    north = jnp.where(is_top, mirrored, north)

    four, half = (4 * levels, cols), 2 * levels

    def stack(q, blocks):
        return jnp.concatenate([x[q * levels : (q + 1) * levels] for x in blocks], 0)

    def lines(rows_of_one):
        return jnp.concatenate([jnp.broadcast_to(x, (levels, cols)) for x in rows_of_one], 0)

    outside, inside = (west, east, south, north), (own_w, own_e, own_s, own_n)
    t1, t2, k1, k2, n1, n2, s1 = (stack(q, outside) for q in range(7))
    t0, k0, n0, s0 = (stack(q, inside) for q in (0, 2, 4, 6))
    d1, d2 = (lines([x[TAIL + n : TAIL + n + 1] for x in outside]) for n in (0, 1))
    d0, d0b = (lines([x[TAIL + n : TAIL + n + 1] for x in inside]) for n in (0, 1))
    f0 = lines([drag_ends[2:3, :], drag_ends[1:2, :], drag[0:1, :], drag[rows - 1 : rows, :]])
    sub, lane = iota(four, 0), iota(four, 1)
    level_i = sub & (levels - 1)
    level = level_i.astype(F32)
    side = jnp.where((sub & levels) == 0, 1.0, -1.0)
    wet0, wet1 = level < d0, level < d1
    wet01, wet12 = level < jnp.minimum(d0, d1), level < jnp.minimum(d1, d2)

    def face(side, ua, ub, ta, tb, ka, kb):
        return side * (0.0625 * ((ua + ub) * (ta + tb))) - 0.125 * ((ka + kb) * (tb - ta))

    inward = jnp.where(wet01, face(side, n1, n0, t1, t0, k1, k0), 0.0)
    outer = jnp.where(wet12, face(side, n2, n1, t2, t1, k2, k1), 0.0)

    def turn_columns(ref, lines_of):
        for g, x in enumerate(lines_of):
            ref[pl.ds(g, levels, stride=8), :] = x
        ref[...] = ref[...].T

    tail = (8, cols)
    sub8, lane8 = iota(tail, 0), iota((STRIP, cols), 1)
    one, wide = (lane8 < 1) | (lane8 >= cols - 1), (lane8 < 2) | (lane8 >= cols - 2)
    spots = ((one, cols - 1), (wide, cols - 2), (one, cols - 1 - 4))
    bufs, outs = (tb, ub, vb), (t_out, u_out, v_out)

    def copy_out(n, k):
        at = pl.ds(pl.multiple_of(k * rows, rows), rows)
        return pltpu.make_async_copy(bufs[n].at[at], outs[n].at[at], sem.at[n, k])

    def one_level(k, n, part, inside):
        base, buf = pl.multiple_of(k * rows, rows), bufs[n]
        mask, to = spots[n]
        by = (to - 8 * k) & (cols - 1)
        for r in range(0, rows, STRIP):
            moved = pltpu.roll((turned_t if n == 0 else turned)[pl.ds(r, STRIP), :], by, 1)
            old = part[pl.ds(pl.multiple_of(inside * rows, rows) + r, STRIP), :]
            buf[pl.ds(base + r, STRIP), :] = old + jnp.where(mask, moved, 0.0)

        def row_of(ref, s):
            return jnp.broadcast_to(ref[pl.ds(s * levels + k, 1), :], tail)

        for s, (near, far, begin) in enumerate(((0, 1, 0), (7, 6, rows - 8))):
            add = jnp.where(sub8 == near, row_of((tr, ur, vr0)[n], s), 0.0)
            if n == 2:
                add = jnp.where(sub8 == far, row_of(vr1, s), add)
            at = pl.ds(base + begin, 8)
            buf[at, :] = buf[at, :] + add
        copy_out(n, k).start()

    def all_levels(*which):
        for begin, parts in ((0, (t_low, u_low, v_low)), (levels // 2, (t_high, u_high, v_high))):

            @pl.loop(0, levels // 2, step=CHUNK)
            def some_of_them(k):
                for i in range(CHUNK):
                    for n in which:
                        one_level(begin + k + i, n, parts[n], k + i)

    tr[...] = inward[half:]
    turn_columns(turned_t, (inward[levels:half], inward[:levels]))
    all_levels(0)

    before, after = (sw, se, sw, nw), (nw, ne, se, ne)

    def beyond(x, at):
        lo, hi = (
            jnp.concatenate(
                [jnp.broadcast_to(c[n : n + m], (levels, 1)) for c, (n, m) in zip(cells, at)], 0
            )
            for cells in (before, after)
        )
        lo, hi = jnp.broadcast_to(lo, four), jnp.broadcast_to(hi, four)
        return jnp.where(lane == 0, lo, lanes(x, 1)), jnp.where(lane == cols - 1, hi, lanes(x, -1))

    t_w, t_e = beyond(t1, ((0, levels),) * 4)
    k_w, k_e = beyond(k1, ((2 * levels, levels),) * 4)
    s_w, s_e = beyond(s1, ((4 * levels, levels),) * 2 + ((6 * levels, levels),) * 2)
    d_w, d_e = beyond(d1, ((TAIL, 1),) * 4)
    flux_w = jnp.where(level < jnp.minimum(d_w, d1), face(1.0, s_w, s1, t_w, t1, k_w, k1), 0.0)
    flux_e = jnp.where(level < jnp.minimum(d1, d_e), face(1.0, s1, s_e, t1, t_e, k1, k_e), 0.0)
    rise = 0.125 * ((sublanes(k1, -1) + k1) * (sublanes(t1, -1) - t1))
    rise = jnp.where((level + 1.0 < d1) & (level_i < levels - 1), rise, 0.0)
    change = outer - inward + flux_w - flux_e + rise - sublanes(rise, 1)
    p1, dp0 = jnp.where(wet1, t1 + change, 0.0), inward
    step = 1
    while step < levels:
        p1 = p1 + jnp.where(level_i >= step, sublanes(p1, step), 0.0)
        dp0 = dp0 + jnp.where(level_i >= step, sublanes(dp0, step), 0.0)
        step *= 2
    dn = 0.0125 * (side * p1) + f0 * jnp.where(wet01, n1 - n0, 0.0)
    dn = jnp.where(wet0, dn, 0.0)
    dn2 = jnp.where(level < d0b, 0.0125 * (side * dp0), 0.0)
    slope = jnp.where(lane < cols - 1, lanes(dp0, -1), 0.0) - jnp.where(lane > 0, lanes(dp0, 1), 0.0)
    ds = f0 * jnp.where(wet01, s1 - s0, 0.0) - 0.0125 * slope
    ds = jnp.where(wet0, ds, 0.0)
    ur[...] = ds[half:]
    vr0[...] = dn[half:]
    vr1[...] = dn2[half:]

    turn_columns(
        turned, (dn2[levels:half], dn[levels:half], dn[:levels], dn2[:levels], ds[levels:half], ds[:levels])
    )
    all_levels(1, 2)

    @pl.loop(0, levels)
    def finish(k):
        for n in range(3):
            copy_out(n, k).wait()


def on_device(t, u, v, kd, friction, water, strata):
    levels, rows, cols = t.shape
    lon_n, lat_n = lax.axis_size("lon"), lax.axis_size("lat")
    vmem = pl.BlockSpec(memory_space=pltpu.VMEM)
    hbm = pl.BlockSpec(memory_space=pltpu.HBM)
    params = pltpu.CompilerParams(vmem_limit_bytes=12 * 1024 * 1024)
    tall = levels * rows
    plane, message, stack = (rows, cols), (RIM, cols), (tall, cols)

    def in_hbm(*arrays):
        return [pltpu.with_memory_space_constraint(x, pltpu.HBM) for x in arrays]

    lat_a, lat_b, coriolis, drag = pl.pallas_call(
        functools.partial(rows_kernel, levels),
        out_shape=[pltpu.VMEM((RIM, 1, cols), F32)] * 2 + [pltpu.VMEM(plane, F32)] * 2,
        in_specs=[hbm] * 7,
        out_specs=[vmem] * 4,
        scratch_shapes=[pltpu.VMEM((4, 1, cols), jnp.int32)] * 2
        + [pltpu.SemaphoreType.DMA((2, 7)), pltpu.SemaphoreType.DMA((2, 2, 2)), pltpu.SemaphoreType.DMA],
        compiler_params=params,
        name="rows",
    )(
        *in_hbm(*[x.reshape(levels, rows, 1, cols) for x in (t, u, v, kd)]),
        *in_hbm(*[x.reshape(rows, 1, cols) for x in (water, strata)], friction),
    )
    lat_a, lat_b = lat_a.reshape(message), lat_b.reshape(message)
    lat_pairs = [(i, i ^ 1) for i in range(lat_n)]
    cross = []
    for m in range(lon_n):
        for i in range(1, lat_n - 1, 2):
            here, north = m * lat_n + i, m * lat_n + i + 1
            cross += [(here, north), (north, here)]
        cross.append((m * lat_n + lat_n - 1, (lon_n - 1 - m) * lat_n + lat_n - 1))
        cross.append((m * lat_n, m * lat_n))
    rim_a = lax.ppermute(lat_a, "lat", lat_pairs)
    rim_b = lax.ppermute(lat_b, ("lon", "lat"), cross)

    fields = [x.reshape(stack) for x in (t, u, v, kd)]
    send_a, send_b, depth, drag_ends = pl.pallas_call(
        functools.partial(pack_kernel, levels),
        out_shape=[pltpu.VMEM(s, F32) for s in (message, message, plane, (8, cols))],
        in_specs=[vmem] * 7,
        out_specs=[vmem] * 4,
        scratch_shapes=[pltpu.VMEM((4, rows, cols), F32), pltpu.VMEM((2 * rows, cols), F32)],
        compiler_params=params,
        name="pack",
    )(*fields, water, strata, drag)
    half = levels // 2
    padded, flat = pltpu.VMEM((rows + 2 * PAD, cols), F32), pltpu.VMEM(plane, F32)
    part = pltpu.VMEM((half * rows, cols), F32)
    work = [padded, padded, flat, padded] * 2 + [padded] + [flat] * 4
    cost = pl.CostEstimate(flops=50 * tall * cols, bytes_accessed=1 << 20, transcendentals=0)
    *first, p_mid, up_mid = pl.pallas_call(
        functools.partial(low_kernel, levels, half, STRIP),
        out_shape=[part] * 3 + [padded, flat],
        in_specs=[vmem] * 7,
        out_specs=[vmem] * 5,
        scratch_shapes=work,
        compiler_params=params,
        cost_estimate=cost,
        name="inner_low",
    )(*fields, depth, drag, coriolis)
    send_a, send_b = pl.pallas_call(
        functools.partial(corner_kernel, levels),
        out_shape=[pltpu.VMEM(message, F32)] * 2,
        in_specs=[vmem] * 5,
        out_specs=[vmem] * 2,
        compiler_params=params,
        name="corners",
    )(send_a, send_b, rim_b, rim_a, up_mid)
    lon_pairs = [(i, i ^ 1) for i in range(lon_n)]
    lon_cross = [(i, (i + 1) % lon_n if i % 2 else (i - 1) % lon_n) for i in range(lon_n)]
    recv_b = lax.ppermute(send_b, "lon", lon_cross)
    recv_a = lax.ppermute(send_a, "lon", lon_pairs)

    second = pl.pallas_call(
        functools.partial(high_kernel, levels, half, STRIP),
        out_shape=[part] * 3,
        in_specs=[vmem] * 10,
        out_specs=[vmem] * 3,
        scratch_shapes=[padded, flat] + work,
        compiler_params=params,
        cost_estimate=cost,
        name="inner_high",
    )(*fields, depth, drag, coriolis, p_mid, up_mid, send_a)

    rim_pair = pltpu.VMEM((2 * levels, cols), F32)
    outs = pl.pallas_call(
        functools.partial(border_kernel, levels),
        out_shape=[jax.ShapeDtypeStruct(stack, F32)] * 3,
        in_specs=[vmem] * 16,
        out_specs=[hbm] * 3,
        scratch_shapes=[pltpu.VMEM(stack, F32)] * 3
        + [rim_pair] * 4
        + [pltpu.VMEM(plane, F32)] * 2
        + [pltpu.SemaphoreType.DMA((3, levels))],
        compiler_params=params,
        name="border",
    )(*first, *second, send_a, send_b, recv_a, recv_b, lat_a, lat_b, rim_a, rim_b, drag, drag_ends)
    return tuple(x.reshape(levels, rows, cols) for x in outs)


def solution(mesh):
    stack, plane = P(None, "lat", "lon"), P("lat", "lon")
    return jax.shard_map(
        on_device,
        mesh=mesh,
        in_specs=(stack,) * 4 + (plane,) * 3,
        out_specs=(stack,) * 3,
        check_vma=False,
    )
```

```python
import functools

import jax
import jax.numpy as jnp
from jax import lax
from jax.experimental import pallas as pl
from jax.experimental.pallas import tpu as pltpu
from jax.sharding import PartitionSpec as P

DT = 0.25
GRAV = 0.1
F32 = jnp.float32
PAD = 8
RIM = 128
TAIL = 112
CHUNK = 4
STRIP = 32


def lanes(x, by):
    by %= x.shape[1]
    return x if by == 0 else pltpu.roll(x, by, 1)


def sublanes(x, by):
    by %= x.shape[0]
    return x if by == 0 else pltpu.roll(x, by, 0)


def iota(shape, dim):
    return lax.broadcasted_iota(jnp.int32, shape, dim)


def parity(axis):
    return lax.axis_index(axis) % 2 == 0


def rows_kernel(
    levels, t, u, v, kd, water, strata, friction, lat_a, lat_b, coriolis, drag,
    water_rows, strata_rows, sem, plane_sem, drag_sem,
):
    rows, cols = coriolis.shape
    copies, planes = [], []
    lat_even = parity("lat")
    for side, message in enumerate((lat_a, lat_b)):
        north = lat_even if side == 0 else jnp.logical_not(lat_even)
        near = jnp.where(north, rows - 1, 0)
        far = jnp.where(north, rows - 2, 1)
        for n, row in enumerate((near, far)):
            for m, (src, dst) in enumerate(((water, water_rows), (strata, strata_rows))):
                at = dst.at[pl.ds(2 * side + n, 1)]
                planes.append(pltpu.make_async_copy(src.at[pl.ds(row, 1)], at, plane_sem.at[m, side, n]))
        for q, (src, row) in enumerate(
            ((t, near), (t, far), (kd, near), (kd, far), (v, near), (v, far), (u, near))
        ):
            at = message.at[pl.ds(q * levels, levels)]
            copies.append(pltpu.make_async_copy(src.at[:, row], at, sem.at[side, q]))
    whole = pltpu.make_async_copy(friction, drag, drag_sem)
    for copy in planes + copies + [whole]:
        copy.start()
    row = iota((rows, cols), 0) + lax.axis_index("lat") * rows
    total = rows * lax.axis_size("lat")
    coriolis[...] = DT * jnp.sin(jnp.pi * ((row.astype(F32) + 0.5) / total - 0.5))
    for copy in planes:
        copy.wait()
    for side, message in enumerate((lat_a, lat_b)):
        message[pl.ds(TAIL + 2, RIM - TAIL - 2)] = jnp.zeros((RIM - TAIL - 2, 1, cols), F32)
        for n in range(2):
            at = pl.ds(2 * side + n, 1)
            message[pl.ds(TAIL + n, 1)] = (water_rows[at] * strata_rows[at]).astype(F32)
    whole.wait()
    drag[...] = DT * drag[...]
    for copy in copies:
        copy.wait()


def pack_kernel(
    levels, t, u, v, kd, water, strata, drag,
    send_a, send_b, depth, drag_ends, gathered, ends,
):
    rows, cols = depth.shape
    lane = iota((STRIP, cols), 1)
    edge = (lane < 2) | (lane >= cols - 2)
    for r in range(0, rows, STRIP):
        at = pl.ds(r, STRIP)
        d = (water[at, :] * strata[at, :]).astype(F32)
        depth[at, :] = d
        gathered[2, at, :] = lanes(d, 2)
        gathered[3, at, :] = lanes(drag[at, :], 2)
        gathered[0, at, :] = jnp.zeros((STRIP, cols), F32)
        gathered[1, at, :] = jnp.zeros((STRIP, cols), F32)

    @pl.loop(0, levels // CHUNK)
    def one_piece(part):
        begin = pl.multiple_of(part * CHUNK * rows, rows)
        for f, full in enumerate((t, kd, u, v)):
            for r in range(0, rows, STRIP):
                acc = gathered[f // 2, pl.ds(r, STRIP), :]
                for n in range(CHUNK):
                    x = jnp.where(edge, full[pl.ds(begin + n * rows + r, STRIP), :], 0.0)
                    to = 8 * (part * CHUNK + n) + 4 * (f % 2) + 2
                    acc = acc + pltpu.roll(x, to & (cols - 1), 1)
                gathered[f // 2, pl.ds(r, STRIP), :] = acc

    for n in range(2):
        ends[pl.ds(n * rows, rows), :] = gathered[n, :, :].T
    d = gathered[2, :, :].T
    drag_ends[...] = gathered[3, :, :].T[0:8]

    lon_even, lat_even = parity("lon"), parity("lat")
    for q, (f, near) in enumerate(
        ((0, True), (0, False), (1, True), (1, False), (2, True), (2, False), (3, True))
    ):
        first = (f // 2) * rows + 4 * (f % 2)
        east = ends[pl.ds(first + (1 if near else 0), levels, stride=8), :]
        west = ends[pl.ds(first + (2 if near else 3), levels, stride=8), :]
        at = pl.ds(q * levels, levels)
        send_a[at, :] = jnp.where(lon_even, east, west)
        send_b[at, :] = jnp.where(lon_even, west, east)

    tail = (RIM - TAIL, cols)
    sub = iota(tail, 0)

    def tail_of(near, far):
        near, far = (jnp.broadcast_to(d[r : r + 1], tail) for r in (near, far))
        return jnp.where(sub == 0, near, jnp.where(sub == 1, far, 0.0))

    east, west = tail_of(1, 0), tail_of(2, 3)
    send_a[pl.ds(TAIL, RIM - TAIL), :] = jnp.where(lon_even, east, west)
    send_b[pl.ds(TAIL, RIM - TAIL), :] = jnp.where(lon_even, west, east)


def corner_kernel(levels, send_a, send_b, rim_b, rim_a, when, out_a, out_b):
    cols = send_a.shape[1]
    lon_even, lat_even = parity("lon"), parity("lat")
    a, b = rim_a[...], rim_b[...]
    b = jnp.where(lax.axis_index("lat") == 0, 0.0, b)
    south, north = jnp.where(lat_even, b, a).T, jnp.where(lat_even, a, b).T
    is_top = lax.axis_index("lat") == lax.axis_size("lat") - 1
    line = iota((1, cols), 1)
    turn = jnp.where((line >= 4 * levels) & (line < 7 * levels), -1.0, 1.0)
    first, last = north[0:1], north[cols - 1 : cols]
    first, last = jnp.where(is_top, turn * last, first), jnp.where(is_top, turn * first, last)
    tail = (RIM - TAIL, cols)
    sub = iota(tail, 0)
    for n, (main, out) in enumerate(((send_a, out_a), (send_b, out_b))):
        east = lon_even if n == 0 else jnp.logical_not(lon_even)
        s = jnp.broadcast_to(jnp.where(east, south[cols - 1 : cols], south[0:1]), tail)
        q = jnp.broadcast_to(jnp.where(east, last, first), tail)
        out[pl.ds(0, TAIL), :] = main[pl.ds(0, TAIL), :]
        depths = main[pl.ds(TAIL, RIM - TAIL), :]
        out[pl.ds(TAIL, RIM - TAIL), :] = jnp.where(sub == 2, s, jnp.where(sub == 3, q, depths))


def inner_kernel(
    levels, first, last, strip, t, u, v, kd, depth, drag, coriolis, p_in, up_in,
    t_out, u_out, v_out, p, up,
    fn, gu, gv, back, de, dw, dn, dragn,
):
    rows, cols = depth.shape
    zero = jnp.zeros((PAD, cols), F32)
    for ref in (fn, gu, back):
        ref[pl.ds(0, PAD), :] = zero

    shape = (strip, cols)
    lane = iota(shape, 1)
    row = iota(shape, 0)
    starts = range(0, rows, strip)
    for r in starts:
        here = pl.ds(r, strip)
        d, f = depth[here, :], drag[here, :]
        de[here, :] = jnp.where(lane < cols - 1, jnp.minimum(d, lanes(d, -1)), 0.0)
        dw[here, :] = jnp.where(lane > 0, jnp.minimum(d, lanes(d, 1)), 0.0)
        if r + strip < rows:
            north = pl.ds(r + 1, strip)
            dn[here, :] = jnp.minimum(d, depth[north, :])
            dragn[here, :] = drag[north, :]
        else:
            dn[here, :] = jnp.where(row < strip - 1, jnp.minimum(d, sublanes(d, -1)), 0.0)
            dragn[here, :] = sublanes(f, -1)

    up[...] = jnp.zeros(up.shape, F32) if p_in is None else up_in[...]
    p[...] = jnp.zeros(p.shape, F32) if p_in is None else p_in[...]

    def one_level(k):
        kf = k.astype(F32)
        base = pl.multiple_of(k * rows, rows)
        above = pl.multiple_of(jnp.minimum(k + 1, levels - 1) * rows, rows)
        begin = pl.multiple_of((k - first) * rows, rows)
        for r in starts:
            here, out = pl.ds(base + r, strip), pl.ds(begin + r, strip)
            plane, padded, below = pl.ds(r, strip), pl.ds(PAD + r, strip), pl.ds(PAD + r - 1, strip)

            def north_of(ref, mid):
                return ref[pl.ds(base + r + 1, strip), :] if r + strip < rows else sublanes(mid, -1)

            d = depth[plane, :]
            t0, u0, v0, k0 = t[here, :], u[here, :], v[here, :], kd[here, :]
            wet, wet_e, wet_n = d > kf, de[plane, :] > kf, dn[plane, :] > kf

            t1, u1, k1 = lanes(t0, -1), lanes(u0, -1), lanes(k0, -1)
            flux = 0.0625 * ((u0 + u1) * (t0 + t1)) - 0.125 * ((k0 + k1) * (t1 - t0))
            flux = jnp.where(wet_e, flux, 0.0)
            change = lanes(flux, 1) - flux
            wet_w = dw[plane, :] > kf
            lap_u = jnp.where(wet_e, u1 - u0, 0.0) + jnp.where(wet_w, lanes(u0, 1) - u0, 0.0)
            lap_v = jnp.where(wet_e, lanes(v0, -1) - v0, 0.0) + jnp.where(wet_w, lanes(v0, 1) - v0, 0.0)

            t1, v1, k1 = north_of(t, t0), north_of(v, v0), north_of(kd, k0)
            flux = 0.0625 * ((v0 + v1) * (t0 + t1)) - 0.125 * ((k0 + k1) * (t1 - t0))
            flux = jnp.where(wet_n, flux, 0.0)
            lap = jnp.where(wet_n, north_of(u, u0) - u0, 0.0)
            lap2 = jnp.where(wet_n, v1 - v0, 0.0)
            fn[padded, :] = flux
            gu[padded, :] = lap
            gv[plane, :] = lap2
            change = change + (fn[below, :] - flux)
            lap_u = lap_u + (lap - gu[below, :])
            lap_v = lap_v + lap2

            higher = pl.ds(above + r, strip)
            rise = 0.125 * ((kd[higher, :] + k0) * (t[higher, :] - t0))
            rise = jnp.where(d > kf + 1.0, rise, 0.0)
            change = change + (rise - up[plane, :])
            up[plane, :] = rise

            t_next = jnp.where(wet, t0 + change, 0.0)
            t_out[out, :] = t_next
            p[padded, :] = p[padded, :] + t_next
            c, f = coriolis[plane, :], drag[plane, :]
            u_out[out, :] = u0 + (c * v0 + f * lap_u)
            v_out[out, :] = v0 + (f * lap_v - c * u0)

        middle = pl.ds(PAD, rows)
        back[middle, :] = 0.0125 * p[middle, :] - dragn[...] * gv[...]
        for r in starts:
            plane, out = pl.ds(r, strip), pl.ds(begin + r, strip)
            wet = depth[plane, :] > kf
            mid = p[pl.ds(PAD + r, strip), :]
            slope = jnp.where(lane < cols - 1, lanes(mid, -1), 0.0) - jnp.where(lane > 0, lanes(mid, 1), 0.0)
            u_next = u_out[out, :] - 0.0125 * slope
            v_next = v_out[out, :] + back[pl.ds(PAD + r - 1, strip), :] - 0.0125 * p[pl.ds(PAD + r + 1, strip), :]
            u_out[out, :] = jnp.where(wet, u_next, 0.0)
            v_out[out, :] = jnp.where(wet, v_next, 0.0)

    @pl.loop(first, last)
    def each_level(k):
        one_level(k)


def low_kernel(levels, half, strip, *refs):
    inner_kernel(levels, 0, half, strip, *refs[:7], None, None, *refs[7:])


def high_kernel(levels, half, strip, *refs):
    inner_kernel(levels, half, levels, strip, *refs[:9], *refs[10:])


def border_kernel(
    levels, t_low, u_low, v_low, t_high, u_high, v_high,
    send_a, send_b, recv_a, recv_b, lat_a, lat_b, rim_a, rim_b, drag, drag_ends,
    t_out, u_out, v_out, tb, ub, vb, tr, ur, vr0, vr1, turned, turned_t, sem,
):
    rows, cols = drag.shape
    lon_even, lat_even = parity("lon"), parity("lat")
    is_top = lax.axis_index("lat") == lax.axis_size("lat") - 1

    def sides(even, a, b):
        a, b = a[...], b[...]
        return jnp.where(even, b, a), jnp.where(even, a, b)

    own_w, own_e = sides(lon_even, send_a, send_b)
    west, east = sides(lon_even, recv_a, recv_b)
    own_s, own_n = sides(lat_even, lat_a, lat_b)
    south, north = sides(lat_even, rim_a, rim_b)
    south = jnp.where(lax.axis_index("lat") == 0, 0.0, south)

    low, high = TAIL + 2, TAIL + 3
    sw, nw = (west.T[:, n : n + 1] for n in (low, high))
    se, ne = (east.T[:, n : n + 1] for n in (low, high))
    line = iota((RIM, 1), 0)
    turn = jnp.where((line >= 4 * levels) & (line < 7 * levels), -1.0, 1.0)
    mirrored = turn * jnp.take_along_axis(north, cols - 1 - iota((RIM, cols), 1), axis=1)
    north = jnp.where(is_top, mirrored, north)

    four, half = (4 * levels, cols), 2 * levels

    def stack(q, blocks):
        return jnp.concatenate([x[q * levels : (q + 1) * levels] for x in blocks], 0)

    def lines(rows_of_one):
        return jnp.concatenate([jnp.broadcast_to(x, (levels, cols)) for x in rows_of_one], 0)

    outside, inside = (west, east, south, north), (own_w, own_e, own_s, own_n)
    t1, t2, k1, k2, n1, n2, s1 = (stack(q, outside) for q in range(7))
    t0, k0, n0, s0 = (stack(q, inside) for q in (0, 2, 4, 6))
    d1, d2 = (lines([x[TAIL + n : TAIL + n + 1] for x in outside]) for n in (0, 1))
    d0, d0b = (lines([x[TAIL + n : TAIL + n + 1] for x in inside]) for n in (0, 1))
    f0 = lines([drag_ends[2:3, :], drag_ends[1:2, :], drag[0:1, :], drag[rows - 1 : rows, :]])
    sub, lane = iota(four, 0), iota(four, 1)
    level_i = sub & (levels - 1)
    level = level_i.astype(F32)
    side = jnp.where((sub & levels) == 0, 1.0, -1.0)
    wet0, wet1 = level < d0, level < d1
    wet01, wet12 = level < jnp.minimum(d0, d1), level < jnp.minimum(d1, d2)

    def face(side, ua, ub, ta, tb, ka, kb):
        return side * (0.0625 * ((ua + ub) * (ta + tb))) - 0.125 * ((ka + kb) * (tb - ta))

    inward = jnp.where(wet01, face(side, n1, n0, t1, t0, k1, k0), 0.0)
    outer = jnp.where(wet12, face(side, n2, n1, t2, t1, k2, k1), 0.0)

    def turn_columns(ref, lines_of):
        for g, x in enumerate(lines_of):
            ref[pl.ds(g, levels, stride=8), :] = x
        ref[...] = ref[...].T

    tail = (8, cols)
    sub8, lane8 = iota(tail, 0), iota((STRIP, cols), 1)
    one, wide = (lane8 < 1) | (lane8 >= cols - 1), (lane8 < 2) | (lane8 >= cols - 2)
    spots = ((one, cols - 1), (wide, cols - 2), (one, cols - 1 - 4))
    bufs, outs = (tb, ub, vb), (t_out, u_out, v_out)

    def copy_out(n, k):
        at = pl.ds(pl.multiple_of(k * rows, rows), rows)
        return pltpu.make_async_copy(bufs[n].at[at], outs[n].at[at], sem.at[n, k])

    def one_level(k, n, part, inside):
        base, buf = pl.multiple_of(k * rows, rows), bufs[n]
        mask, to = spots[n]
        by = (to - 8 * k) & (cols - 1)
        for r in range(0, rows, STRIP):
            moved = pltpu.roll((turned_t if n == 0 else turned)[pl.ds(r, STRIP), :], by, 1)
            old = part[pl.ds(pl.multiple_of(inside * rows, rows) + r, STRIP), :]
            buf[pl.ds(base + r, STRIP), :] = old + jnp.where(mask, moved, 0.0)

        def row_of(ref, s):
            return jnp.broadcast_to(ref[pl.ds(s * levels + k, 1), :], tail)

        for s, (near, far, begin) in enumerate(((0, 1, 0), (7, 6, rows - 8))):
            add = jnp.where(sub8 == near, row_of((tr, ur, vr0)[n], s), 0.0)
            if n == 2:
                add = jnp.where(sub8 == far, row_of(vr1, s), add)
            at = pl.ds(base + begin, 8)
            buf[at, :] = buf[at, :] + add
        copy_out(n, k).start()

    def all_levels(*which):
        for begin, parts in ((0, (t_low, u_low, v_low)), (levels // 2, (t_high, u_high, v_high))):

            @pl.loop(0, levels // 2, step=CHUNK)
            def some_of_them(k):
                for i in range(CHUNK):
                    for n in which:
                        one_level(begin + k + i, n, parts[n], k + i)

    tr[...] = inward[half:]
    turn_columns(turned_t, (inward[levels:half], inward[:levels]))
    all_levels(0)

    before, after = (sw, se, sw, nw), (nw, ne, se, ne)

    def beyond(x, at):
        lo, hi = (
            jnp.concatenate(
                [jnp.broadcast_to(c[n : n + m], (levels, 1)) for c, (n, m) in zip(cells, at)], 0
            )
            for cells in (before, after)
        )
        lo, hi = jnp.broadcast_to(lo, four), jnp.broadcast_to(hi, four)
        return jnp.where(lane == 0, lo, lanes(x, 1)), jnp.where(lane == cols - 1, hi, lanes(x, -1))

    t_w, t_e = beyond(t1, ((0, levels),) * 4)
    k_w, k_e = beyond(k1, ((2 * levels, levels),) * 4)
    s_w, s_e = beyond(s1, ((4 * levels, levels),) * 2 + ((6 * levels, levels),) * 2)
    d_w, d_e = beyond(d1, ((TAIL, 1),) * 4)
    flux_w = jnp.where(level < jnp.minimum(d_w, d1), face(1.0, s_w, s1, t_w, t1, k_w, k1), 0.0)
    flux_e = jnp.where(level < jnp.minimum(d1, d_e), face(1.0, s1, s_e, t1, t_e, k1, k_e), 0.0)
    rise = 0.125 * ((sublanes(k1, -1) + k1) * (sublanes(t1, -1) - t1))
    rise = jnp.where((level + 1.0 < d1) & (level_i < levels - 1), rise, 0.0)
    change = outer - inward + flux_w - flux_e + rise - sublanes(rise, 1)
    p1, dp0 = jnp.where(wet1, t1 + change, 0.0), inward
    step = 1
    while step < levels:
        p1 = p1 + jnp.where(level_i >= step, sublanes(p1, step), 0.0)
        dp0 = dp0 + jnp.where(level_i >= step, sublanes(dp0, step), 0.0)
        step *= 2
    dn = 0.0125 * (side * p1) + f0 * jnp.where(wet01, n1 - n0, 0.0)
    dn = jnp.where(wet0, dn, 0.0)
    dn2 = jnp.where(level < d0b, 0.0125 * (side * dp0), 0.0)
    slope = jnp.where(lane < cols - 1, lanes(dp0, -1), 0.0) - jnp.where(lane > 0, lanes(dp0, 1), 0.0)
    ds = f0 * jnp.where(wet01, s1 - s0, 0.0) - 0.0125 * slope
    ds = jnp.where(wet0, ds, 0.0)
    ur[...] = ds[half:]
    vr0[...] = dn[half:]
    vr1[...] = dn2[half:]

    turn_columns(
        turned, (dn2[levels:half], dn[levels:half], dn[:levels], dn2[:levels], ds[levels:half], ds[:levels])
    )
    all_levels(1, 2)

    @pl.loop(0, levels)
    def finish(k):
        for n in range(3):
            copy_out(n, k).wait()


def on_device(t, u, v, kd, friction, water, strata):
    levels, rows, cols = t.shape
    lon_n, lat_n = lax.axis_size("lon"), lax.axis_size("lat")
    vmem = pl.BlockSpec(memory_space=pltpu.VMEM)
    hbm = pl.BlockSpec(memory_space=pltpu.HBM)
    params = pltpu.CompilerParams(vmem_limit_bytes=12 * 1024 * 1024)
    tall = levels * rows
    plane, message, stack = (rows, cols), (RIM, cols), (tall, cols)

    def in_hbm(*arrays):
        return [pltpu.with_memory_space_constraint(x, pltpu.HBM) for x in arrays]

    lat_a, lat_b, coriolis, drag = pl.pallas_call(
        functools.partial(rows_kernel, levels),
        out_shape=[pltpu.VMEM((RIM, 1, cols), F32)] * 2 + [pltpu.VMEM(plane, F32)] * 2,
        in_specs=[hbm] * 7,
        out_specs=[vmem] * 4,
        scratch_shapes=[pltpu.VMEM((4, 1, cols), jnp.int32)] * 2
        + [pltpu.SemaphoreType.DMA((2, 7)), pltpu.SemaphoreType.DMA((2, 2, 2)), pltpu.SemaphoreType.DMA],
        compiler_params=params,
        name="rows",
    )(
        *in_hbm(*[x.reshape(levels, rows, 1, cols) for x in (t, u, v, kd)]),
        *in_hbm(*[x.reshape(rows, 1, cols) for x in (water, strata)], friction),
    )
    lat_a, lat_b = lat_a.reshape(message), lat_b.reshape(message)
    lat_pairs = [(i, i ^ 1) for i in range(lat_n)]
    cross = []
    for m in range(lon_n):
        for i in range(1, lat_n - 1, 2):
            here, north = m * lat_n + i, m * lat_n + i + 1
            cross += [(here, north), (north, here)]
        cross.append((m * lat_n + lat_n - 1, (lon_n - 1 - m) * lat_n + lat_n - 1))
        cross.append((m * lat_n, (m ^ 1) * lat_n))
    rim_a = lax.ppermute(lat_a, "lat", lat_pairs)
    rim_b = lax.ppermute(lat_b, ("lon", "lat"), cross)

    fields = [x.reshape(stack) for x in (t, u, v, kd)]
    send_a, send_b, depth, drag_ends = pl.pallas_call(
        functools.partial(pack_kernel, levels),
        out_shape=[pltpu.VMEM(s, F32) for s in (message, message, plane, (8, cols))],
        in_specs=[vmem] * 7,
        out_specs=[vmem] * 4,
        scratch_shapes=[pltpu.VMEM((4, rows, cols), F32), pltpu.VMEM((2 * rows, cols), F32)],
        compiler_params=params,
        name="pack",
    )(*fields, water, strata, drag)
    half = levels // 2
    padded, flat = pltpu.VMEM((rows + 2 * PAD, cols), F32), pltpu.VMEM(plane, F32)
    part = pltpu.VMEM((half * rows, cols), F32)
    work = [padded, padded, flat, padded] + [flat] * 4
    cost = pl.CostEstimate(flops=50 * tall * cols, bytes_accessed=1 << 20, transcendentals=0)
    *first, p_mid, up_mid = pl.pallas_call(
        functools.partial(low_kernel, levels, half, STRIP),
        out_shape=[part] * 3 + [padded, flat],
        in_specs=[vmem] * 7,
        out_specs=[vmem] * 5,
        scratch_shapes=work,
        compiler_params=params,
        cost_estimate=cost,
        name="inner_low",
    )(*fields, depth, drag, coriolis)
    send_a, send_b = pl.pallas_call(
        functools.partial(corner_kernel, levels),
        out_shape=[pltpu.VMEM(message, F32)] * 2,
        in_specs=[vmem] * 5,
        out_specs=[vmem] * 2,
        compiler_params=params,
        name="corners",
    )(send_a, send_b, rim_b, rim_a, up_mid)
    lon_pairs = [(i, i ^ 1) for i in range(lon_n)]
    lon_cross = [(i, (i + 1) % lon_n if i % 2 else (i - 1) % lon_n) for i in range(lon_n)]
    recv_b = lax.ppermute(send_b, "lon", lon_cross)
    recv_a = lax.ppermute(send_a, "lon", lon_pairs)

    second = pl.pallas_call(
        functools.partial(high_kernel, levels, half, STRIP),
        out_shape=[part] * 3,
        in_specs=[vmem] * 10,
        out_specs=[vmem] * 3,
        scratch_shapes=[padded, flat] + work,
        compiler_params=params,
        cost_estimate=cost,
        name="inner_high",
    )(*fields, depth, drag, coriolis, p_mid, up_mid, send_a)

    rim_pair = pltpu.VMEM((2 * levels, cols), F32)
    outs = pl.pallas_call(
        functools.partial(border_kernel, levels),
        out_shape=[jax.ShapeDtypeStruct(stack, F32)] * 3,
        in_specs=[vmem] * 16,
        out_specs=[hbm] * 3,
        scratch_shapes=[pltpu.VMEM(stack, F32)] * 3
        + [rim_pair] * 4
        + [pltpu.VMEM(plane, F32)] * 2
        + [pltpu.SemaphoreType.DMA((3, levels))],
        compiler_params=params,
        name="border",
    )(*first, *second, send_a, send_b, recv_a, recv_b, lat_a, lat_b, rim_a, rim_b, drag, drag_ends)
    return tuple(x.reshape(levels, rows, cols) for x in outs)


def solution(mesh):
    stack, plane = P(None, "lat", "lon"), P("lat", "lon")
    return jax.shard_map(
        on_device,
        mesh=mesh,
        in_specs=(stack,) * 4 + (plane,) * 3,
        out_specs=(stack,) * 3,
        check_vma=False,
    )
```

```python
import functools

import jax
import jax.numpy as jnp
from jax import lax
from jax.experimental import pallas as pl
from jax.experimental.pallas import tpu as pltpu
from jax.sharding import PartitionSpec as P

DT = 0.25
GRAV = 0.1
F32 = jnp.float32
PAD = 8
RIM = 128
TAIL = 112
CHUNK = 4
STRIP = 32


def lanes(x, by):
    by %= x.shape[1]
    return x if by == 0 else pltpu.roll(x, by, 1)


def sublanes(x, by):
    by %= x.shape[0]
    return x if by == 0 else pltpu.roll(x, by, 0)


def iota(shape, dim):
    return lax.broadcasted_iota(jnp.int32, shape, dim)


def parity(axis):
    return lax.axis_index(axis) % 2 == 0


def rows_kernel(
    levels, t, u, v, kd, water, strata, friction, lat_a, lat_b, coriolis, drag,
    water_rows, strata_rows, sem, plane_sem, drag_sem,
):
    rows, cols = coriolis.shape
    copies, planes = [], []
    lat_even = parity("lat")
    for side, message in enumerate((lat_a, lat_b)):
        north = lat_even if side == 0 else jnp.logical_not(lat_even)
        near = jnp.where(north, rows - 1, 0)
        far = jnp.where(north, rows - 2, 1)
        for n, row in enumerate((near, far)):
            for m, (src, dst) in enumerate(((water, water_rows), (strata, strata_rows))):
                at = dst.at[pl.ds(2 * side + n, 1)]
                planes.append(pltpu.make_async_copy(src.at[pl.ds(row, 1)], at, plane_sem.at[m, side, n]))
        for q, (src, row) in enumerate(
            ((t, near), (t, far), (kd, near), (kd, far), (v, near), (v, far), (u, near))
        ):
            at = message.at[pl.ds(q * levels, levels)]
            copies.append(pltpu.make_async_copy(src.at[:, row], at, sem.at[side, q]))
    whole = pltpu.make_async_copy(friction, drag, drag_sem)
    for copy in planes + copies + [whole]:
        copy.start()
    row = iota((rows, cols), 0) + lax.axis_index("lat") * rows
    total = rows * lax.axis_size("lat")
    coriolis[...] = DT * jnp.sin(jnp.pi * ((row.astype(F32) + 0.5) / total - 0.5))
    for copy in planes:
        copy.wait()
    for side, message in enumerate((lat_a, lat_b)):
        message[pl.ds(TAIL + 2, RIM - TAIL - 2)] = jnp.zeros((RIM - TAIL - 2, 1, cols), F32)
        for n in range(2):
            at = pl.ds(2 * side + n, 1)
            message[pl.ds(TAIL + n, 1)] = (water_rows[at] * strata_rows[at]).astype(F32)
    whole.wait()
    drag[...] = DT * drag[...]
    for copy in copies:
        copy.wait()


def pack_kernel(
    levels, t, u, v, kd, water, strata, drag,
    send_a, send_b, depth, drag_ends, gathered, ends,
):
    rows, cols = depth.shape
    lane = iota((STRIP, cols), 1)
    edge = (lane < 2) | (lane >= cols - 2)
    for r in range(0, rows, STRIP):
        at = pl.ds(r, STRIP)
        d = (water[at, :] * strata[at, :]).astype(F32)
        depth[at, :] = d
        gathered[2, at, :] = lanes(d, 2)
        gathered[3, at, :] = lanes(drag[at, :], 2)
        gathered[0, at, :] = jnp.zeros((STRIP, cols), F32)
        gathered[1, at, :] = jnp.zeros((STRIP, cols), F32)

    @pl.loop(0, levels // CHUNK)
    def one_piece(part):
        begin = pl.multiple_of(part * CHUNK * rows, rows)
        for f, full in enumerate((t, kd, u, v)):
            for r in range(0, rows, STRIP):
                acc = gathered[f // 2, pl.ds(r, STRIP), :]
                for n in range(CHUNK):
                    x = jnp.where(edge, full[pl.ds(begin + n * rows + r, STRIP), :], 0.0)
                    to = 8 * (part * CHUNK + n) + 4 * (f % 2) + 2
                    acc = acc + pltpu.roll(x, to & (cols - 1), 1)
                gathered[f // 2, pl.ds(r, STRIP), :] = acc

    for n in range(2):
        ends[pl.ds(n * rows, rows), :] = gathered[n, :, :].T
    d = gathered[2, :, :].T
    drag_ends[...] = gathered[3, :, :].T[0:8]

    lon_even, lat_even = parity("lon"), parity("lat")
    for q, (f, near) in enumerate(
        ((0, True), (0, False), (1, True), (1, False), (2, True), (2, False), (3, True))
    ):
        first = (f // 2) * rows + 4 * (f % 2)
        east = ends[pl.ds(first + (1 if near else 0), levels, stride=8), :]
        west = ends[pl.ds(first + (2 if near else 3), levels, stride=8), :]
        at = pl.ds(q * levels, levels)
        send_a[at, :] = jnp.where(lon_even, east, west)
        send_b[at, :] = jnp.where(lon_even, west, east)

    tail = (RIM - TAIL, cols)
    sub = iota(tail, 0)

    def tail_of(near, far):
        near, far = (jnp.broadcast_to(d[r : r + 1], tail) for r in (near, far))
        return jnp.where(sub == 0, near, jnp.where(sub == 1, far, 0.0))

    east, west = tail_of(1, 0), tail_of(2, 3)
    send_a[pl.ds(TAIL, RIM - TAIL), :] = jnp.where(lon_even, east, west)
    send_b[pl.ds(TAIL, RIM - TAIL), :] = jnp.where(lon_even, west, east)


def corner_kernel(levels, send_a, send_b, rim_b, rim_a, when, out_a, out_b):
    cols = send_a.shape[1]
    lon_even, lat_even = parity("lon"), parity("lat")
    a, b = rim_a[...], rim_b[...]
    b = jnp.where(lax.axis_index("lat") == 0, 0.0, b)
    south, north = jnp.where(lat_even, b, a).T, jnp.where(lat_even, a, b).T
    is_top = lax.axis_index("lat") == lax.axis_size("lat") - 1
    line = iota((1, cols), 1)
    turn = jnp.where((line >= 4 * levels) & (line < 7 * levels), -1.0, 1.0)
    first, last = north[0:1], north[cols - 1 : cols]
    first, last = jnp.where(is_top, turn * last, first), jnp.where(is_top, turn * first, last)
    tail = (RIM - TAIL, cols)
    sub = iota(tail, 0)
    for n, (main, out) in enumerate(((send_a, out_a), (send_b, out_b))):
        east = lon_even if n == 0 else jnp.logical_not(lon_even)
        s = jnp.broadcast_to(jnp.where(east, south[cols - 1 : cols], south[0:1]), tail)
        q = jnp.broadcast_to(jnp.where(east, last, first), tail)
        out[pl.ds(0, TAIL), :] = main[pl.ds(0, TAIL), :]
        depths = main[pl.ds(TAIL, RIM - TAIL), :]
        out[pl.ds(TAIL, RIM - TAIL), :] = jnp.where(sub == 2, s, jnp.where(sub == 3, q, depths))


def inner_kernel(
    levels, first, last, strip, t, u, v, kd, depth, drag, coriolis, p_in, up_in,
    t_out, u_out, v_out, p, up,
    p2, de, dw, dn, dragn, *work,
):
    rows, cols = depth.shape
    zero = jnp.zeros((PAD, cols), F32)
    sets = work[:6], work[6:]
    for fn, gu, _, back, _, _ in sets:
        for ref in (fn, gu, back):
            ref[pl.ds(0, PAD), :] = zero
    p2[pl.ds(PAD + rows, PAD), :] = zero

    shape = (strip, cols)
    lane = iota(shape, 1)
    row = iota(shape, 0)
    starts = range(0, rows, strip)
    for r in starts:
        here = pl.ds(r, strip)
        d, f = depth[here, :], drag[here, :]
        de[here, :] = jnp.where(lane < cols - 1, jnp.minimum(d, lanes(d, -1)), 0.0)
        dw[here, :] = jnp.where(lane > 0, jnp.minimum(d, lanes(d, 1)), 0.0)
        if r + strip < rows:
            north = pl.ds(r + 1, strip)
            dn[here, :] = jnp.minimum(d, depth[north, :])
            dragn[here, :] = drag[north, :]
        else:
            dn[here, :] = jnp.where(row < strip - 1, jnp.minimum(d, sublanes(d, -1)), 0.0)
            dragn[here, :] = sublanes(f, -1)

    up[...] = jnp.zeros(up.shape, F32) if p_in is None else up_in[...]
    p[...] = jnp.zeros(p.shape, F32) if p_in is None else p_in[...]

    def one_level(k, before, p, fn, gu, gv, back, us, vs):
        kf = k.astype(F32)
        base = pl.multiple_of(k * rows, rows)
        above = pl.multiple_of(jnp.minimum(k + 1, levels - 1) * rows, rows)
        begin = pl.multiple_of((k - first) * rows, rows)
        for r in starts:
            here, out = pl.ds(base + r, strip), pl.ds(begin + r, strip)
            plane, padded, below = pl.ds(r, strip), pl.ds(PAD + r, strip), pl.ds(PAD + r - 1, strip)

            def north_of(ref, mid):
                if r + strip == rows:
                    return sublanes(mid, -1)
                return ref[pl.ds(base + r, strip + 8), :][1 : strip + 1]

            d = depth[plane, :]
            t0, u0, v0, k0 = t[here, :], u[here, :], v[here, :], kd[here, :]
            wet, wet_e, wet_n = d > kf, de[plane, :] > kf, dn[plane, :] > kf

            t1, u1, k1 = lanes(t0, -1), lanes(u0, -1), lanes(k0, -1)
            flux = 0.0625 * ((u0 + u1) * (t0 + t1)) - 0.125 * ((k0 + k1) * (t1 - t0))
            flux = jnp.where(wet_e, flux, 0.0)
            change = lanes(flux, 1) - flux
            wet_w = dw[plane, :] > kf
            lap_u = jnp.where(wet_e, u1 - u0, 0.0) + jnp.where(wet_w, lanes(u0, 1) - u0, 0.0)
            lap_v = jnp.where(wet_e, lanes(v0, -1) - v0, 0.0) + jnp.where(wet_w, lanes(v0, 1) - v0, 0.0)

            t1, v1, k1 = north_of(t, t0), north_of(v, v0), north_of(kd, k0)
            flux = 0.0625 * ((v0 + v1) * (t0 + t1)) - 0.125 * ((k0 + k1) * (t1 - t0))
            flux = jnp.where(wet_n, flux, 0.0)
            lap = jnp.where(wet_n, north_of(u, u0) - u0, 0.0)
            lap2 = jnp.where(wet_n, v1 - v0, 0.0)
            fn[padded, :] = flux
            gu[padded, :] = lap
            gv[plane, :] = lap2
            change = change + (fn[below, :] - flux)
            lap_u = lap_u + (lap - gu[below, :])
            lap_v = lap_v + lap2

            higher = pl.ds(above + r, strip)
            rise = 0.125 * ((kd[higher, :] + k0) * (t[higher, :] - t0))
            rise = jnp.where(d > kf + 1.0, rise, 0.0)
            change = change + (rise - up[plane, :])
            up[plane, :] = rise

            t_next = jnp.where(wet, t0 + change, 0.0)
            t_out[out, :] = t_next
            p[padded, :] = before[padded, :] + t_next
            c, f = coriolis[plane, :], drag[plane, :]
            us[plane, :] = u0 + (c * v0 + f * lap_u)
            vs[plane, :] = v0 + (f * lap_v - c * u0)

        def finish():
            middle = pl.ds(PAD, rows)
            back[middle, :] = 0.0125 * p[middle, :] - dragn[...] * gv[...]
            for r in starts:
                plane, out = pl.ds(r, strip), pl.ds(begin + r, strip)
                wet = depth[plane, :] > kf
                mid = p[pl.ds(PAD + r, strip), :]
                slope = jnp.where(lane < cols - 1, lanes(mid, -1), 0.0) - jnp.where(lane > 0, lanes(mid, 1), 0.0)
                u_next = us[plane, :] - 0.0125 * slope
                v_next = vs[plane, :] + back[pl.ds(PAD + r - 1, strip), :] - 0.0125 * p[pl.ds(PAD + r + 1, strip), :]
                u_out[out, :] = jnp.where(wet, u_next, 0.0)
                v_out[out, :] = jnp.where(wet, v_next, 0.0)

        return finish

    @pl.loop(first, last, step=2)
    def two_levels(k):
        finish = one_level(k, p, p2, *sets[0])
        finish2 = one_level(k + 1, p2, p, *sets[1])
        finish()
        finish2()


def low_kernel(levels, half, strip, *refs):
    inner_kernel(levels, 0, half, strip, *refs[:7], None, None, *refs[7:])


def high_kernel(levels, half, strip, *refs):
    inner_kernel(levels, half, levels, strip, *refs[:9], *refs[10:])


def border_kernel(
    levels, t_low, u_low, v_low, t_high, u_high, v_high,
    send_a, send_b, recv_a, recv_b, lat_a, lat_b, rim_a, rim_b, drag, drag_ends,
    t_out, u_out, v_out, tb, ub, vb, tr, ur, vr0, vr1, turned, turned_t, sem,
):
    rows, cols = drag.shape
    lon_even, lat_even = parity("lon"), parity("lat")
    is_top = lax.axis_index("lat") == lax.axis_size("lat") - 1

    def sides(even, a, b):
        a, b = a[...], b[...]
        return jnp.where(even, b, a), jnp.where(even, a, b)

    own_w, own_e = sides(lon_even, send_a, send_b)
    west, east = sides(lon_even, recv_a, recv_b)
    own_s, own_n = sides(lat_even, lat_a, lat_b)
    south, north = sides(lat_even, rim_a, rim_b)
    south = jnp.where(lax.axis_index("lat") == 0, 0.0, south)

    low, high = TAIL + 2, TAIL + 3
    sw, nw = (west.T[:, n : n + 1] for n in (low, high))
    se, ne = (east.T[:, n : n + 1] for n in (low, high))
    line = iota((RIM, 1), 0)
    turn = jnp.where((line >= 4 * levels) & (line < 7 * levels), -1.0, 1.0)
    mirrored = turn * jnp.take_along_axis(north, cols - 1 - iota((RIM, cols), 1), axis=1)
    north = jnp.where(is_top, mirrored, north)

    four, half = (4 * levels, cols), 2 * levels

    def stack(q, blocks):
        return jnp.concatenate([x[q * levels : (q + 1) * levels] for x in blocks], 0)

    def lines(rows_of_one):
        return jnp.concatenate([jnp.broadcast_to(x, (levels, cols)) for x in rows_of_one], 0)

    outside, inside = (west, east, south, north), (own_w, own_e, own_s, own_n)
    t1, t2, k1, k2, n1, n2, s1 = (stack(q, outside) for q in range(7))
    t0, k0, n0, s0 = (stack(q, inside) for q in (0, 2, 4, 6))
    d1, d2 = (lines([x[TAIL + n : TAIL + n + 1] for x in outside]) for n in (0, 1))
    d0, d0b = (lines([x[TAIL + n : TAIL + n + 1] for x in inside]) for n in (0, 1))
    f0 = lines([drag_ends[2:3, :], drag_ends[1:2, :], drag[0:1, :], drag[rows - 1 : rows, :]])
    sub, lane = iota(four, 0), iota(four, 1)
    level_i = sub & (levels - 1)
    level = level_i.astype(F32)
    side = jnp.where((sub & levels) == 0, 1.0, -1.0)
    wet0, wet1 = level < d0, level < d1
    wet01, wet12 = level < jnp.minimum(d0, d1), level < jnp.minimum(d1, d2)

    def face(side, ua, ub, ta, tb, ka, kb):
        return side * (0.0625 * ((ua + ub) * (ta + tb))) - 0.125 * ((ka + kb) * (tb - ta))

    inward = jnp.where(wet01, face(side, n1, n0, t1, t0, k1, k0), 0.0)
    outer = jnp.where(wet12, face(side, n2, n1, t2, t1, k2, k1), 0.0)

    def turn_columns(ref, lines_of):
        for g, x in enumerate(lines_of):
            ref[pl.ds(g, levels, stride=8), :] = x
        ref[...] = ref[...].T

    tail = (8, cols)
    sub8, lane8 = iota(tail, 0), iota((STRIP, cols), 1)
    one, wide = (lane8 < 1) | (lane8 >= cols - 1), (lane8 < 2) | (lane8 >= cols - 2)
    spots = ((one, cols - 1), (wide, cols - 2), (one, cols - 1 - 4))
    bufs, outs = (tb, ub, vb), (t_out, u_out, v_out)

    def copy_out(n, k):
        at = pl.ds(pl.multiple_of(k * rows, rows), rows)
        return pltpu.make_async_copy(bufs[n].at[at], outs[n].at[at], sem.at[n, k])

    def one_level(k, n, part, inside):
        base, buf = pl.multiple_of(k * rows, rows), bufs[n]
        mask, to = spots[n]
        by = (to - 8 * k) & (cols - 1)
        for r in range(0, rows, STRIP):
            moved = pltpu.roll((turned_t if n == 0 else turned)[pl.ds(r, STRIP), :], by, 1)
            old = part[pl.ds(pl.multiple_of(inside * rows, rows) + r, STRIP), :]
            buf[pl.ds(base + r, STRIP), :] = old + jnp.where(mask, moved, 0.0)

        def row_of(ref, s):
            return jnp.broadcast_to(ref[pl.ds(s * levels + k, 1), :], tail)

        for s, (near, far, begin) in enumerate(((0, 1, 0), (7, 6, rows - 8))):
            add = jnp.where(sub8 == near, row_of((tr, ur, vr0)[n], s), 0.0)
            if n == 2:
                add = jnp.where(sub8 == far, row_of(vr1, s), add)
            at = pl.ds(base + begin, 8)
            buf[at, :] = buf[at, :] + add
        copy_out(n, k).start()

    def all_levels(*which):
        for begin, parts in ((0, (t_low, u_low, v_low)), (levels // 2, (t_high, u_high, v_high))):

            @pl.loop(0, levels // 2, step=CHUNK)
            def some_of_them(k):
                for i in range(CHUNK):
                    for n in which:
                        one_level(begin + k + i, n, parts[n], k + i)

    tr[...] = inward[half:]
    turn_columns(turned_t, (inward[levels:half], inward[:levels]))
    all_levels(0)

    before, after = (sw, se, sw, nw), (nw, ne, se, ne)

    def beyond(x, at):
        lo, hi = (
            jnp.concatenate(
                [jnp.broadcast_to(c[n : n + m], (levels, 1)) for c, (n, m) in zip(cells, at)], 0
            )
            for cells in (before, after)
        )
        lo, hi = jnp.broadcast_to(lo, four), jnp.broadcast_to(hi, four)
        return jnp.where(lane == 0, lo, lanes(x, 1)), jnp.where(lane == cols - 1, hi, lanes(x, -1))

    t_w, t_e = beyond(t1, ((0, levels),) * 4)
    k_w, k_e = beyond(k1, ((2 * levels, levels),) * 4)
    s_w, s_e = beyond(s1, ((4 * levels, levels),) * 2 + ((6 * levels, levels),) * 2)
    d_w, d_e = beyond(d1, ((TAIL, 1),) * 4)
    flux_w = jnp.where(level < jnp.minimum(d_w, d1), face(1.0, s_w, s1, t_w, t1, k_w, k1), 0.0)
    flux_e = jnp.where(level < jnp.minimum(d1, d_e), face(1.0, s1, s_e, t1, t_e, k1, k_e), 0.0)
    rise = 0.125 * ((sublanes(k1, -1) + k1) * (sublanes(t1, -1) - t1))
    rise = jnp.where((level + 1.0 < d1) & (level_i < levels - 1), rise, 0.0)
    change = outer - inward + flux_w - flux_e + rise - sublanes(rise, 1)
    p1, dp0 = jnp.where(wet1, t1 + change, 0.0), inward
    step = 1
    while step < levels:
        p1 = p1 + jnp.where(level_i >= step, sublanes(p1, step), 0.0)
        dp0 = dp0 + jnp.where(level_i >= step, sublanes(dp0, step), 0.0)
        step *= 2
    dn = 0.0125 * (side * p1) + f0 * jnp.where(wet01, n1 - n0, 0.0)
    dn = jnp.where(wet0, dn, 0.0)
    dn2 = jnp.where(level < d0b, 0.0125 * (side * dp0), 0.0)
    slope = jnp.where(lane < cols - 1, lanes(dp0, -1), 0.0) - jnp.where(lane > 0, lanes(dp0, 1), 0.0)
    ds = f0 * jnp.where(wet01, s1 - s0, 0.0) - 0.0125 * slope
    ds = jnp.where(wet0, ds, 0.0)
    ur[...] = ds[half:]
    vr0[...] = dn[half:]
    vr1[...] = dn2[half:]

    turn_columns(
        turned, (dn2[levels:half], dn[levels:half], dn[:levels], dn2[:levels], ds[levels:half], ds[:levels])
    )
    all_levels(1, 2)

    @pl.loop(0, levels)
    def finish(k):
        for n in range(3):
            copy_out(n, k).wait()


def on_device(t, u, v, kd, friction, water, strata):
    levels, rows, cols = t.shape
    lon_n, lat_n = lax.axis_size("lon"), lax.axis_size("lat")
    vmem = pl.BlockSpec(memory_space=pltpu.VMEM)
    hbm = pl.BlockSpec(memory_space=pltpu.HBM)
    params = pltpu.CompilerParams(vmem_limit_bytes=12 * 1024 * 1024)
    tall = levels * rows
    plane, message, stack = (rows, cols), (RIM, cols), (tall, cols)

    def in_hbm(*arrays):
        return [pltpu.with_memory_space_constraint(x, pltpu.HBM) for x in arrays]

    lat_a, lat_b, coriolis, drag = pl.pallas_call(
        functools.partial(rows_kernel, levels),
        out_shape=[pltpu.VMEM((RIM, 1, cols), F32)] * 2 + [pltpu.VMEM(plane, F32)] * 2,
        in_specs=[hbm] * 7,
        out_specs=[vmem] * 4,
        scratch_shapes=[pltpu.VMEM((4, 1, cols), jnp.int32)] * 2
        + [pltpu.SemaphoreType.DMA((2, 7)), pltpu.SemaphoreType.DMA((2, 2, 2)), pltpu.SemaphoreType.DMA],
        compiler_params=params,
        name="rows",
    )(
        *in_hbm(*[x.reshape(levels, rows, 1, cols) for x in (t, u, v, kd)]),
        *in_hbm(*[x.reshape(rows, 1, cols) for x in (water, strata)], friction),
    )
    lat_a, lat_b = lat_a.reshape(message), lat_b.reshape(message)
    lat_pairs = [(i, i ^ 1) for i in range(lat_n)]
    cross = []
    for m in range(lon_n):
        for i in range(1, lat_n - 1, 2):
            here, north = m * lat_n + i, m * lat_n + i + 1
            cross += [(here, north), (north, here)]
        cross.append((m * lat_n + lat_n - 1, (lon_n - 1 - m) * lat_n + lat_n - 1))
        cross.append((m * lat_n, (m ^ 1) * lat_n))
    rim_a = lax.ppermute(lat_a, "lat", lat_pairs)
    rim_b = lax.ppermute(lat_b, ("lon", "lat"), cross)

    fields = [x.reshape(stack) for x in (t, u, v, kd)]
    send_a, send_b, depth, drag_ends = pl.pallas_call(
        functools.partial(pack_kernel, levels),
        out_shape=[pltpu.VMEM(s, F32) for s in (message, message, plane, (8, cols))],
        in_specs=[vmem] * 7,
        out_specs=[vmem] * 4,
        scratch_shapes=[pltpu.VMEM((4, rows, cols), F32), pltpu.VMEM((2 * rows, cols), F32)],
        compiler_params=params,
        name="pack",
    )(*fields, water, strata, drag)
    half = levels // 2
    padded, flat = pltpu.VMEM((rows + 2 * PAD, cols), F32), pltpu.VMEM(plane, F32)
    part = pltpu.VMEM((half * rows, cols), F32)
    work = [padded] + [flat] * 4 + [padded, padded, flat, padded, flat, flat] * 2
    cost = pl.CostEstimate(flops=50 * tall * cols, bytes_accessed=1 << 20, transcendentals=0)
    *first, p_mid, up_mid = pl.pallas_call(
        functools.partial(low_kernel, levels, half, STRIP),
        out_shape=[part] * 3 + [padded, flat],
        in_specs=[vmem] * 7,
        out_specs=[vmem] * 5,
        scratch_shapes=work,
        compiler_params=params,
        cost_estimate=cost,
        name="inner_low",
    )(*fields, depth, drag, coriolis)
    send_a, send_b = pl.pallas_call(
        functools.partial(corner_kernel, levels),
        out_shape=[pltpu.VMEM(message, F32)] * 2,
        in_specs=[vmem] * 5,
        out_specs=[vmem] * 2,
        compiler_params=params,
        name="corners",
    )(send_a, send_b, rim_b, rim_a, up_mid)
    lon_pairs = [(i, i ^ 1) for i in range(lon_n)]
    lon_cross = [(i, (i + 1) % lon_n if i % 2 else (i - 1) % lon_n) for i in range(lon_n)]
    recv_b = lax.ppermute(send_b, "lon", lon_cross)
    recv_a = lax.ppermute(send_a, "lon", lon_pairs)

    second = pl.pallas_call(
        functools.partial(high_kernel, levels, half, STRIP),
        out_shape=[part] * 3,
        in_specs=[vmem] * 10,
        out_specs=[vmem] * 3,
        scratch_shapes=[padded, flat] + work,
        compiler_params=params,
        cost_estimate=cost,
        name="inner_high",
    )(*fields, depth, drag, coriolis, p_mid, up_mid, send_a)

    rim_pair = pltpu.VMEM((2 * levels, cols), F32)
    outs = pl.pallas_call(
        functools.partial(border_kernel, levels),
        out_shape=[jax.ShapeDtypeStruct(stack, F32)] * 3,
        in_specs=[vmem] * 16,
        out_specs=[hbm] * 3,
        scratch_shapes=[pltpu.VMEM(stack, F32)] * 3
        + [rim_pair] * 4
        + [pltpu.VMEM(plane, F32)] * 2
        + [pltpu.SemaphoreType.DMA((3, levels))],
        compiler_params=params,
        name="border",
    )(*first, *second, send_a, send_b, recv_a, recv_b, lat_a, lat_b, rim_a, rim_b, drag, drag_ends)
    return tuple(x.reshape(levels, rows, cols) for x in outs)


def solution(mesh):
    stack, plane = P(None, "lat", "lon"), P("lat", "lon")
    return jax.shard_map(
        on_device,
        mesh=mesh,
        in_specs=(stack,) * 4 + (plane,) * 3,
        out_specs=(stack,) * 3,
        check_vma=False,
    )
```

```python
import functools

import jax
import jax.numpy as jnp
from jax import lax
from jax.experimental import pallas as pl
from jax.experimental.pallas import tpu as pltpu
from jax.sharding import PartitionSpec as P

DT = 0.25
GRAV = 0.1
F32 = jnp.float32
PAD = 8
RIM = 88
TAIL = 80
CHUNK = 8
STRIP = 32


def lanes(x, by):
    by %= x.shape[1]
    return x if by == 0 else pltpu.roll(x, by, 1)


def sublanes(x, by):
    by %= x.shape[0]
    return x if by == 0 else pltpu.roll(x, by, 0)


def iota(shape, dim):
    return lax.broadcasted_iota(jnp.int32, shape, dim)


def parity(axis):
    return lax.axis_index(axis) % 2 == 0


def face(side, ua, ub, ta, tb, ka, kb):
    return side * (0.0625 * ((ua + ub) * (ta + tb))) - 0.125 * ((ka + kb) * (tb - ta))


def square(x):
    rows, cols = x.shape
    return jnp.concatenate([x, jnp.zeros((cols - rows, cols), F32)], 0)


def rows_kernel(
    levels, t, u, v, kd, water, strata, friction, lat_a, lat_b, coriolis, drag,
    far_rows, water_rows, strata_rows, sem, plane_sem, drag_sem,
):
    rows, cols = coriolis.shape
    copies, planes = [], []
    lat_even = parity("lat")
    for side, message in enumerate((lat_a, lat_b)):
        north = lat_even if side == 0 else jnp.logical_not(lat_even)
        near = jnp.where(north, rows - 1, 0)
        far = jnp.where(north, rows - 2, 1)
        for n, row in enumerate((near, far)):
            for m, (src, dst) in enumerate(((water, water_rows), (strata, strata_rows))):
                at = dst.at[pl.ds(2 * side + n, 1)]
                planes.append(pltpu.make_async_copy(src.at[pl.ds(row, 1)], at, plane_sem.at[m, side, n]))
        for q, src in enumerate((t, kd, v, u)):
            at = message.at[pl.ds(q * levels, levels)]
            copies.append(pltpu.make_async_copy(src.at[:, near], at, sem.at[side, q]))
        for q, src in enumerate((t, kd, v)):
            copies.append(pltpu.make_async_copy(src.at[:, far], far_rows.at[side, q], sem.at[side, 4 + q]))
    whole = pltpu.make_async_copy(friction, drag, drag_sem)
    for copy in planes + copies + [whole]:
        copy.start()
    row = iota((8, rows), 1) + lax.axis_index("lat") * rows
    total = rows * lax.axis_size("lat")
    line = DT * jnp.sin(jnp.pi * ((row.astype(F32) + 0.5) / total - 0.5))
    coriolis[...] = jnp.broadcast_to(line[0:1], (cols, rows)).T
    for copy in planes:
        copy.wait()
    for side, message in enumerate((lat_a, lat_b)):
        message[pl.ds(TAIL + 2, RIM - TAIL - 2)] = jnp.zeros((RIM - TAIL - 2, 1, cols), F32)
        for n in range(2):
            at = pl.ds(2 * side + n, 1)
            message[pl.ds(TAIL + n, 1)] = (water_rows[at] * strata_rows[at]).astype(F32)
    whole.wait()
    drag[...] = DT * drag[...]
    for copy in copies:
        copy.wait()
    level = iota((levels, 1, cols), 0).astype(F32)
    for side, message in enumerate((lat_a, lat_b)):
        north = lat_even if side == 0 else jnp.logical_not(lat_even)
        t1, k1, v1 = (message[pl.ds(q * levels, levels)] for q in range(3))
        t2, k2, v2 = (far_rows[side, q] for q in range(3))
        wet = level < jnp.minimum(message[pl.ds(TAIL, 1)], message[pl.ds(TAIL + 1, 1)])
        flux = face(jnp.where(north, 1.0, -1.0), v2, v1, t2, t1, k2, k1)
        message[pl.ds(4 * levels, levels)] = jnp.where(wet, flux, 0.0)


def pack_kernel(
    levels, t, u, v, kd, water, strata, drag,
    send_a, send_b, depth, drag_ends, gathered, ends,
):
    rows, cols = depth.shape
    lane = iota((STRIP, cols), 1)
    edge = (lane < 2) | (lane >= cols - 2)
    for r in range(0, rows, STRIP):
        at = pl.ds(r, STRIP)
        d = (water[at, :] * strata[at, :]).astype(F32)
        depth[at, :] = d
        gathered[2, at, :] = lanes(d, 2)
        gathered[3, at, :] = lanes(drag[at, :], 2)
        gathered[0, at, :] = jnp.zeros((STRIP, cols), F32)
        gathered[1, at, :] = jnp.zeros((STRIP, cols), F32)

    @pl.loop(0, levels // CHUNK)
    def one_piece(part):
        begin = pl.multiple_of(part * CHUNK * rows, rows)
        for f, full in enumerate((t, kd, u, v)):
            for r in range(0, rows, STRIP):
                acc = gathered[f // 2, pl.ds(r, STRIP), :]
                for n in range(CHUNK):
                    x = jnp.where(edge, full[pl.ds(begin + n * rows + r, STRIP), :], 0.0)
                    to = 8 * (part * CHUNK + n) + 4 * (f % 2) + 2
                    acc = acc + pltpu.roll(x, to & (cols - 1), 1)
                gathered[f // 2, pl.ds(r, STRIP), :] = acc

    for n in range(2):
        ends[pl.ds(n * rows, rows), :] = gathered[n, :, :].T
    d = gathered[2, :, :].T
    drag_ends[...] = gathered[3, :, :].T[0:8]

    lon_even, lat_even = parity("lon"), parity("lat")

    def line_of(f, c):
        return ends[pl.ds((f // 2) * rows + 4 * (f % 2) + c, levels, stride=8), :]

    def side_of(side, near, far):
        t1, k1, u1, v1 = (line_of(f, near) for f in range(4))
        t2, k2, u2 = (line_of(f, far) for f in range(3))
        wet = iota((levels, cols), 0).astype(F32) < jnp.minimum(d[near : near + 1], d[far : far + 1])
        return t1, k1, u1, v1, jnp.where(wet, face(side, u2, u1, t2, t1, k2, k1), 0.0)

    for q, (east, west) in enumerate(zip(side_of(1.0, 1, 0), side_of(-1.0, 2, 3))):
        at = pl.ds(q * levels, levels)
        send_a[at, :] = jnp.where(lon_even, east, west)
        send_b[at, :] = jnp.where(lon_even, west, east)
    tail = (RIM - TAIL, cols)
    sub = iota(tail, 0)

    def tail_of(near, far):
        near, far = (jnp.broadcast_to(d[r : r + 1], tail) for r in (near, far))
        return jnp.where(sub == 0, near, jnp.where(sub == 1, far, 0.0))

    east, west = tail_of(1, 0), tail_of(2, 3)
    send_a[pl.ds(TAIL, RIM - TAIL), :] = jnp.where(lon_even, east, west)
    send_b[pl.ds(TAIL, RIM - TAIL), :] = jnp.where(lon_even, west, east)


def corner_kernel(levels, send_a, send_b, rim_b, rim_a, when, out_a, out_b):
    cols = send_a.shape[1]
    lon_even, lat_even = parity("lon"), parity("lat")
    a, b = rim_a[...], rim_b[...]
    b = jnp.where(lax.axis_index("lat") == 0, 0.0, b)
    south, north = square(jnp.where(lat_even, b, a)).T, square(jnp.where(lat_even, a, b)).T
    is_top = lax.axis_index("lat") == lax.axis_size("lat") - 1
    line = iota((1, cols), 1)
    turn = jnp.where((line >= 2 * levels) & (line < 4 * levels), -1.0, 1.0)
    first, last = north[0:1], north[cols - 1 : cols]
    first, last = jnp.where(is_top, turn * last, first), jnp.where(is_top, turn * first, last)
    tail = (RIM - TAIL, cols)
    sub = iota(tail, 0)
    for n, (main, out) in enumerate(((send_a, out_a), (send_b, out_b))):
        east = lon_even if n == 0 else jnp.logical_not(lon_even)
        s = jnp.broadcast_to(jnp.where(east, south[cols - 1 : cols], south[0:1]), tail)
        q = jnp.broadcast_to(jnp.where(east, last, first), tail)
        out[pl.ds(0, TAIL), :] = main[pl.ds(0, TAIL), :]
        depths = main[pl.ds(TAIL, RIM - TAIL), :]
        out[pl.ds(TAIL, RIM - TAIL), :] = jnp.where(sub == 2, s, jnp.where(sub == 3, q, depths))


def inner_kernel(
    levels, first, last, strip, t, u, v, kd, depth, drag, coriolis, p_in, up_in,
    t_out, u_out, v_out, p, up,
    fn, gu, gv, back, de, dw, dn, dragn,
):
    rows, cols = depth.shape
    zero = jnp.zeros((PAD, cols), F32)
    for ref in (fn, gu, back):
        ref[pl.ds(0, PAD), :] = zero

    shape = (strip, cols)
    lane = iota(shape, 1)
    row = iota(shape, 0)
    starts = range(0, rows, strip)
    for r in starts:
        here = pl.ds(r, strip)
        d, f = depth[here, :], drag[here, :]
        de[here, :] = jnp.where(lane < cols - 1, jnp.minimum(d, lanes(d, -1)), 0.0)
        dw[here, :] = jnp.where(lane > 0, jnp.minimum(d, lanes(d, 1)), 0.0)
        if r + strip < rows:
            north = pl.ds(r + 1, strip)
            dn[here, :] = jnp.minimum(d, depth[north, :])
            dragn[here, :] = drag[north, :]
        else:
            dn[here, :] = jnp.where(row < strip - 1, jnp.minimum(d, sublanes(d, -1)), 0.0)
            dragn[here, :] = sublanes(f, -1)

    up[...] = jnp.zeros(up.shape, F32) if p_in is None else up_in[...]
    p[...] = jnp.zeros(p.shape, F32) if p_in is None else p_in[...]

    def one_level(k):
        kf = k.astype(F32)
        base = pl.multiple_of(k * rows, rows)
        above = pl.multiple_of(jnp.minimum(k + 1, levels - 1) * rows, rows)
        begin = pl.multiple_of((k - first) * rows, rows)
        for r in starts:
            here, out = pl.ds(base + r, strip), pl.ds(begin + r, strip)
            plane, padded, below = pl.ds(r, strip), pl.ds(PAD + r, strip), pl.ds(PAD + r - 1, strip)

            def north_of(ref, mid):
                return ref[pl.ds(base + r + 1, strip), :] if r + strip < rows else sublanes(mid, -1)

            d = depth[plane, :]
            t0, u0, v0, k0 = t[here, :], u[here, :], v[here, :], kd[here, :]
            wet, wet_e, wet_n = d > kf, de[plane, :] > kf, dn[plane, :] > kf

            t1, u1, k1 = lanes(t0, -1), lanes(u0, -1), lanes(k0, -1)
            flux = 0.0625 * ((u0 + u1) * (t0 + t1)) - 0.125 * ((k0 + k1) * (t1 - t0))
            flux = jnp.where(wet_e, flux, 0.0)
            change = lanes(flux, 1) - flux
            wet_w = dw[plane, :] > kf
            lap_u = jnp.where(wet_e, u1 - u0, 0.0) + jnp.where(wet_w, lanes(u0, 1) - u0, 0.0)
            lap_v = jnp.where(wet_e, lanes(v0, -1) - v0, 0.0) + jnp.where(wet_w, lanes(v0, 1) - v0, 0.0)

            t1, v1, k1 = north_of(t, t0), north_of(v, v0), north_of(kd, k0)
            flux = 0.0625 * ((v0 + v1) * (t0 + t1)) - 0.125 * ((k0 + k1) * (t1 - t0))
            flux = jnp.where(wet_n, flux, 0.0)
            lap = jnp.where(wet_n, north_of(u, u0) - u0, 0.0)
            lap2 = jnp.where(wet_n, v1 - v0, 0.0)
            fn[padded, :] = flux
            gu[padded, :] = lap
            gv[plane, :] = lap2
            change = change + (fn[below, :] - flux)
            lap_u = lap_u + (lap - gu[below, :])
            lap_v = lap_v + lap2

            higher = pl.ds(above + r, strip)
            rise = 0.125 * ((kd[higher, :] + k0) * (t[higher, :] - t0))
            rise = jnp.where(d > kf + 1.0, rise, 0.0)
            change = change + (rise - up[plane, :])
            up[plane, :] = rise

            t_next = jnp.where(wet, t0 + change, 0.0)
            t_out[out, :] = t_next
            p[padded, :] = p[padded, :] + t_next
            c, f = coriolis[plane, :], drag[plane, :]
            u_out[out, :] = u0 + (c * v0 + f * lap_u)
            v_out[out, :] = v0 + (f * lap_v - c * u0)

        middle = pl.ds(PAD, rows)
        back[middle, :] = 0.0125 * p[middle, :] - dragn[...] * gv[...]
        for r in starts:
            plane, out = pl.ds(r, strip), pl.ds(begin + r, strip)
            wet = depth[plane, :] > kf
            mid = p[pl.ds(PAD + r, strip), :]
            slope = jnp.where(lane < cols - 1, lanes(mid, -1), 0.0) - jnp.where(lane > 0, lanes(mid, 1), 0.0)
            u_next = u_out[out, :] - 0.0125 * slope
            v_next = v_out[out, :] + back[pl.ds(PAD + r - 1, strip), :] - 0.0125 * p[pl.ds(PAD + r + 1, strip), :]
            u_out[out, :] = jnp.where(wet, u_next, 0.0)
            v_out[out, :] = jnp.where(wet, v_next, 0.0)

    @pl.loop(first, last)
    def each_level(k):
        one_level(k)


def low_kernel(levels, half, strip, *refs):
    inner_kernel(levels, 0, half, strip, *refs[:7], None, None, *refs[7:])


def high_kernel(levels, half, strip, *refs):
    inner_kernel(levels, half, levels, strip, *refs[:9], *refs[10:])


def border_kernel(
    levels, t_low, u_low, v_low, t_high, u_high, v_high,
    send_a, send_b, recv_a, recv_b, lat_a, lat_b, rim_a, rim_b, drag, drag_ends,
    t_out, u_out, v_out, tb, ub, vb, tr, ur, vr0, vr1, turned, turned_t, sem,
):
    rows, cols = drag.shape
    lon_even, lat_even = parity("lon"), parity("lat")
    is_top = lax.axis_index("lat") == lax.axis_size("lat") - 1

    def sides(even, a, b):
        a, b = a[...], b[...]
        return jnp.where(even, b, a), jnp.where(even, a, b)

    own_w, own_e = sides(lon_even, send_a, send_b)
    west, east = sides(lon_even, recv_a, recv_b)
    own_s, own_n = sides(lat_even, lat_a, lat_b)
    south, north = sides(lat_even, rim_a, rim_b)
    south = jnp.where(lax.axis_index("lat") == 0, 0.0, south)

    low, high = TAIL + 2, TAIL + 3
    ends_w, ends_e = square(west).T, square(east).T
    sw, nw = (ends_w[:, n : n + 1] for n in (low, high))
    se, ne = (ends_e[:, n : n + 1] for n in (low, high))
    line = iota((RIM, 1), 0)
    turn = jnp.where((line >= 2 * levels) & (line < 4 * levels), -1.0, 1.0)
    mirrored = turn * jnp.take_along_axis(north, cols - 1 - iota((RIM, cols), 1), axis=1)
    north = jnp.where(is_top, mirrored, north)

    four, half = (4 * levels, cols), 2 * levels

    def stack(q, blocks):
        return jnp.concatenate([x[q * levels : (q + 1) * levels] for x in blocks], 0)

    def lines(rows_of_one):
        return jnp.concatenate([jnp.broadcast_to(x, (levels, cols)) for x in rows_of_one], 0)

    outside, inside = (west, east, south, north), (own_w, own_e, own_s, own_n)
    t1, k1, n1, s1, outer = (stack(q, outside) for q in range(5))
    t0, k0, n0, s0 = (stack(q, inside) for q in range(4))
    d1 = lines([x[TAIL : TAIL + 1] for x in outside])
    d0, d0b = (lines([x[TAIL + n : TAIL + n + 1] for x in inside]) for n in (0, 1))
    f0 = lines([drag_ends[2:3, :], drag_ends[1:2, :], drag[0:1, :], drag[rows - 1 : rows, :]])
    sub, lane = iota(four, 0), iota(four, 1)
    level_i = sub & (levels - 1)
    level = level_i.astype(F32)
    side = jnp.where((sub & levels) == 0, 1.0, -1.0)
    wet0, wet1 = level < d0, level < d1
    wet01 = level < jnp.minimum(d0, d1)

    inward = jnp.where(wet01, face(side, n1, n0, t1, t0, k1, k0), 0.0)

    def turn_columns(ref, lines_of):
        for g, x in enumerate(lines_of):
            ref[pl.ds(g, levels, stride=8), :] = x
        ref[...] = ref[...].T

    tail = (8, cols)
    sub8, lane8 = iota(tail, 0), iota((STRIP, cols), 1)
    one, wide = (lane8 < 1) | (lane8 >= cols - 1), (lane8 < 2) | (lane8 >= cols - 2)
    spots = ((one, cols - 1), (wide, cols - 2), (one, cols - 1 - 4))
    bufs, outs = (tb, ub, vb), (t_out, u_out, v_out)

    def copy_out(n, k):
        at = pl.ds(pl.multiple_of(k * rows, rows), rows)
        return pltpu.make_async_copy(bufs[n].at[at], outs[n].at[at], sem.at[n, k])

    def one_level(k, n, part, inside):
        base, buf = pl.multiple_of(k * rows, rows), bufs[n]
        mask, to = spots[n]
        by = (to - 8 * k) & (cols - 1)
        for r in range(0, rows, STRIP):
            moved = pltpu.roll((turned_t if n == 0 else turned)[pl.ds(r, STRIP), :], by, 1)
            old = part[pl.ds(pl.multiple_of(inside * rows, rows) + r, STRIP), :]
            buf[pl.ds(base + r, STRIP), :] = old + jnp.where(mask, moved, 0.0)

        def row_of(ref, s):
            return jnp.broadcast_to(ref[pl.ds(s * levels + k, 1), :], tail)

        for s, (near, far, begin) in enumerate(((0, 1, 0), (7, 6, rows - 8))):
            add = jnp.where(sub8 == near, row_of((tr, ur, vr0)[n], s), 0.0)
            if n == 2:
                add = jnp.where(sub8 == far, row_of(vr1, s), add)
            at = pl.ds(base + begin, 8)
            buf[at, :] = buf[at, :] + add
        copy_out(n, k).start()

    def all_levels(*which):
        for begin, parts in ((0, (t_low, u_low, v_low)), (levels // 2, (t_high, u_high, v_high))):

            @pl.loop(0, levels // 2, step=CHUNK)
            def some_of_them(k):
                for i in range(CHUNK):
                    for n in which:
                        one_level(begin + k + i, n, parts[n], k + i)

    tr[...] = inward[half:]
    turn_columns(turned_t, (inward[levels:half], inward[:levels]))
    all_levels(0)

    before, after = (sw, se, sw, nw), (nw, ne, se, ne)

    def beyond(x, at):
        lo, hi = (
            jnp.concatenate(
                [jnp.broadcast_to(c[n : n + m], (levels, 1)) for c, (n, m) in zip(cells, at)], 0
            )
            for cells in (before, after)
        )
        lo, hi = jnp.broadcast_to(lo, four), jnp.broadcast_to(hi, four)
        return jnp.where(lane == 0, lo, lanes(x, 1)), jnp.where(lane == cols - 1, hi, lanes(x, -1))

    t_w, t_e = beyond(t1, ((0, levels),) * 4)
    k_w, k_e = beyond(k1, ((levels, levels),) * 4)
    s_w, s_e = beyond(s1, ((2 * levels, levels),) * 2 + ((3 * levels, levels),) * 2)
    d_w, d_e = beyond(d1, ((TAIL, 1),) * 4)
    flux_w = jnp.where(level < jnp.minimum(d_w, d1), face(1.0, s_w, s1, t_w, t1, k_w, k1), 0.0)
    flux_e = jnp.where(level < jnp.minimum(d1, d_e), face(1.0, s1, s_e, t1, t_e, k1, k_e), 0.0)
    rise = 0.125 * ((sublanes(k1, -1) + k1) * (sublanes(t1, -1) - t1))
    rise = jnp.where((level + 1.0 < d1) & (level_i < levels - 1), rise, 0.0)
    change = outer - inward + flux_w - flux_e + rise - sublanes(rise, 1)
    p1, dp0 = jnp.where(wet1, t1 + change, 0.0), inward
    step = 1
    while step < levels:
        p1 = p1 + jnp.where(level_i >= step, sublanes(p1, step), 0.0)
        dp0 = dp0 + jnp.where(level_i >= step, sublanes(dp0, step), 0.0)
        step *= 2
    dn = 0.0125 * (side * p1) + f0 * jnp.where(wet01, n1 - n0, 0.0)
    dn = jnp.where(wet0, dn, 0.0)
    dn2 = jnp.where(level < d0b, 0.0125 * (side * dp0), 0.0)
    slope = jnp.where(lane < cols - 1, lanes(dp0, -1), 0.0) - jnp.where(lane > 0, lanes(dp0, 1), 0.0)
    ds = f0 * jnp.where(wet01, s1 - s0, 0.0) - 0.0125 * slope
    ds = jnp.where(wet0, ds, 0.0)
    ur[...] = ds[half:]
    vr0[...] = dn[half:]
    vr1[...] = dn2[half:]

    turn_columns(
        turned, (dn2[levels:half], dn[levels:half], dn[:levels], dn2[:levels], ds[levels:half], ds[:levels])
    )
    all_levels(1, 2)

    @pl.loop(0, levels)
    def finish(k):
        for n in range(3):
            copy_out(n, k).wait()


def on_device(t, u, v, kd, friction, water, strata):
    levels, rows, cols = t.shape
    lon_n, lat_n = lax.axis_size("lon"), lax.axis_size("lat")
    vmem = pl.BlockSpec(memory_space=pltpu.VMEM)
    hbm = pl.BlockSpec(memory_space=pltpu.HBM)
    params = pltpu.CompilerParams(vmem_limit_bytes=12 * 1024 * 1024)
    tall = levels * rows
    plane, message, stack = (rows, cols), (RIM, cols), (tall, cols)

    def in_hbm(*arrays):
        return [pltpu.with_memory_space_constraint(x, pltpu.HBM) for x in arrays]

    lat_a, lat_b, coriolis, drag = pl.pallas_call(
        functools.partial(rows_kernel, levels),
        out_shape=[pltpu.VMEM((RIM, 1, cols), F32)] * 2 + [pltpu.VMEM(plane, F32)] * 2,
        in_specs=[hbm] * 7,
        out_specs=[vmem] * 4,
        scratch_shapes=[pltpu.VMEM((2, 3, levels, 1, cols), F32)]
        + [pltpu.VMEM((4, 1, cols), jnp.int32)] * 2
        + [pltpu.SemaphoreType.DMA((2, 7)), pltpu.SemaphoreType.DMA((2, 2, 2)), pltpu.SemaphoreType.DMA],
        compiler_params=params,
        name="rows",
    )(
        *in_hbm(*[x.reshape(levels, rows, 1, cols) for x in (t, u, v, kd)]),
        *in_hbm(*[x.reshape(rows, 1, cols) for x in (water, strata)], friction),
    )
    lat_a, lat_b = lat_a.reshape(message), lat_b.reshape(message)
    lat_pairs = [(i, i ^ 1) for i in range(lat_n)]
    cross = []
    for m in range(lon_n):
        for i in range(1, lat_n - 1, 2):
            here, north = m * lat_n + i, m * lat_n + i + 1
            cross += [(here, north), (north, here)]
        cross.append((m * lat_n + lat_n - 1, (lon_n - 1 - m) * lat_n + lat_n - 1))
        cross.append((m * lat_n, (m ^ 1) * lat_n))
    rim_a = lax.ppermute(lat_a, "lat", lat_pairs)
    rim_b = lax.ppermute(lat_b, ("lon", "lat"), cross)

    fields = [x.reshape(stack) for x in (t, u, v, kd)]
    send_a, send_b, depth, drag_ends = pl.pallas_call(
        functools.partial(pack_kernel, levels),
        out_shape=[pltpu.VMEM(s, F32) for s in (message, message, plane, (8, cols))],
        in_specs=[vmem] * 7,
        out_specs=[vmem] * 4,
        scratch_shapes=[pltpu.VMEM((4, rows, cols), F32), pltpu.VMEM((2 * rows, cols), F32)],
        compiler_params=params,
        name="pack",
    )(*fields, water, strata, drag)
    half = levels // 2
    padded, flat = pltpu.VMEM((rows + 2 * PAD, cols), F32), pltpu.VMEM(plane, F32)
    part = pltpu.VMEM((half * rows, cols), F32)
    work = [padded, padded, flat, padded] + [flat] * 4
    cost = pl.CostEstimate(flops=50 * tall * cols, bytes_accessed=1 << 20, transcendentals=0)
    *first, p_mid, up_mid = pl.pallas_call(
        functools.partial(low_kernel, levels, half, STRIP),
        out_shape=[part] * 3 + [padded, flat],
        in_specs=[vmem] * 7,
        out_specs=[vmem] * 5,
        scratch_shapes=work,
        compiler_params=params,
        cost_estimate=cost,
        name="inner_low",
    )(*fields, depth, drag, coriolis)
    send_a, send_b = pl.pallas_call(
        functools.partial(corner_kernel, levels),
        out_shape=[pltpu.VMEM(message, F32)] * 2,
        in_specs=[vmem] * 5,
        out_specs=[vmem] * 2,
        compiler_params=params,
        name="corners",
    )(send_a, send_b, rim_b, rim_a, up_mid)
    lon_pairs = [(i, i ^ 1) for i in range(lon_n)]
    lon_cross = [(i, (i + 1) % lon_n if i % 2 else (i - 1) % lon_n) for i in range(lon_n)]
    recv_b = lax.ppermute(send_b, "lon", lon_cross)
    recv_a = lax.ppermute(send_a, "lon", lon_pairs)

    second = pl.pallas_call(
        functools.partial(high_kernel, levels, half, STRIP),
        out_shape=[part] * 3,
        in_specs=[vmem] * 10,
        out_specs=[vmem] * 3,
        scratch_shapes=[padded, flat] + work,
        compiler_params=params,
        cost_estimate=cost,
        name="inner_high",
    )(*fields, depth, drag, coriolis, p_mid, up_mid, send_a)

    rim_pair = pltpu.VMEM((2 * levels, cols), F32)
    outs = pl.pallas_call(
        functools.partial(border_kernel, levels),
        out_shape=[jax.ShapeDtypeStruct(stack, F32)] * 3,
        in_specs=[vmem] * 16,
        out_specs=[hbm] * 3,
        scratch_shapes=[pltpu.VMEM(stack, F32)] * 3
        + [rim_pair] * 4
        + [pltpu.VMEM(plane, F32)] * 2
        + [pltpu.SemaphoreType.DMA((3, levels))],
        compiler_params=params,
        name="border",
    )(*first, *second, send_a, send_b, recv_a, recv_b, lat_a, lat_b, rim_a, rim_b, drag, drag_ends)
    return tuple(x.reshape(levels, rows, cols) for x in outs)


def solution(mesh):
    stack, plane = P(None, "lat", "lon"), P("lat", "lon")
    return jax.shard_map(
        on_device,
        mesh=mesh,
        in_specs=(stack,) * 4 + (plane,) * 3,
        out_specs=(stack,) * 3,
        check_vma=False,
    )
```

```python
import functools

import jax
import jax.numpy as jnp
from jax import lax
from jax.experimental import pallas as pl
from jax.experimental.pallas import tpu as pltpu
from jax.sharding import PartitionSpec as P

DT = 0.25
GRAV = 0.1
F32 = jnp.float32
PAD = 8
RIM = 88
TAIL = 80
CHUNK = 8
STRIP = 32


def lanes(x, by):
    by %= x.shape[1]
    return x if by == 0 else pltpu.roll(x, by, 1)


def sublanes(x, by):
    by %= x.shape[0]
    return x if by == 0 else pltpu.roll(x, by, 0)


def iota(shape, dim):
    return lax.broadcasted_iota(jnp.int32, shape, dim)


def parity(axis):
    return lax.axis_index(axis) % 2 == 0


def face(side, ua, ub, ta, tb, ka, kb):
    return side * (0.0625 * ((ua + ub) * (ta + tb))) - 0.125 * ((ka + kb) * (tb - ta))


def square(x):
    rows, cols = x.shape
    return jnp.concatenate([x, jnp.zeros((cols - rows, cols), F32)], 0)


def rows_kernel(
    levels, t, u, v, kd, water, strata, friction, lat_a, lat_b, coriolis, drag,
    far_rows, water_rows, strata_rows, sem, plane_sem, drag_sem,
):
    rows, cols = coriolis.shape
    copies, planes = [], []
    lat_even = parity("lat")
    for side, message in enumerate((lat_a, lat_b)):
        north = lat_even if side == 0 else jnp.logical_not(lat_even)
        near = jnp.where(north, rows - 1, 0)
        far = jnp.where(north, rows - 2, 1)
        for n, row in enumerate((near, far)):
            for m, (src, dst) in enumerate(((water, water_rows), (strata, strata_rows))):
                at = dst.at[pl.ds(2 * side + n, 1)]
                planes.append(pltpu.make_async_copy(src.at[pl.ds(row, 1)], at, plane_sem.at[m, side, n]))
        for q, src in enumerate((t, kd, v, u)):
            at = message.at[pl.ds(q * levels, levels)]
            copies.append(pltpu.make_async_copy(src.at[:, near], at, sem.at[side, q]))
        for q, src in enumerate((t, kd, v)):
            copies.append(pltpu.make_async_copy(src.at[:, far], far_rows.at[side, q], sem.at[side, 4 + q]))
    whole = pltpu.make_async_copy(friction, drag, drag_sem)
    for copy in planes + copies + [whole]:
        copy.start()
    row = iota((8, rows), 1) + lax.axis_index("lat") * rows
    total = rows * lax.axis_size("lat")
    line = DT * jnp.sin(jnp.pi * ((row.astype(F32) + 0.5) / total - 0.5))
    coriolis[...] = jnp.broadcast_to(line[0:1], (cols, rows)).T
    for copy in planes:
        copy.wait()
    for side, message in enumerate((lat_a, lat_b)):
        message[pl.ds(TAIL + 2, RIM - TAIL - 2)] = jnp.zeros((RIM - TAIL - 2, 1, cols), F32)
        for n in range(2):
            at = pl.ds(2 * side + n, 1)
            message[pl.ds(TAIL + n, 1)] = (water_rows[at] * strata_rows[at]).astype(F32)
    whole.wait()
    drag[...] = DT * drag[...]
    for copy in copies:
        copy.wait()
    level = iota((levels, 1, cols), 0).astype(F32)
    for side, message in enumerate((lat_a, lat_b)):
        north = lat_even if side == 0 else jnp.logical_not(lat_even)
        t1, k1, v1 = (message[pl.ds(q * levels, levels)] for q in range(3))
        t2, k2, v2 = (far_rows[side, q] for q in range(3))
        wet = level < jnp.minimum(message[pl.ds(TAIL, 1)], message[pl.ds(TAIL + 1, 1)])
        flux = face(jnp.where(north, 1.0, -1.0), v2, v1, t2, t1, k2, k1)
        message[pl.ds(4 * levels, levels)] = jnp.where(wet, flux, 0.0)


def pack_kernel(
    levels, t, u, v, kd, water, strata, drag,
    send_a, send_b, depth, drag_ends, gathered, ends,
):
    rows, cols = depth.shape
    lane = iota((STRIP, cols), 1)
    edge = (lane < 2) | (lane >= cols - 2)
    for r in range(0, rows, STRIP):
        at = pl.ds(r, STRIP)
        d = (water[at, :] * strata[at, :]).astype(F32)
        depth[at, :] = d
        gathered[2, at, :] = lanes(d, 2)
        gathered[3, at, :] = lanes(drag[at, :], 2)
        gathered[0, at, :] = jnp.zeros((STRIP, cols), F32)
        gathered[1, at, :] = jnp.zeros((STRIP, cols), F32)

    @pl.loop(0, levels // CHUNK)
    def one_piece(part):
        begin = pl.multiple_of(part * CHUNK * rows, rows)
        for f, full in enumerate((t, kd, u, v)):
            for r in range(0, rows, STRIP):
                acc = gathered[f // 2, pl.ds(r, STRIP), :]
                for n in range(CHUNK):
                    x = jnp.where(edge, full[pl.ds(begin + n * rows + r, STRIP), :], 0.0)
                    to = 8 * (part * CHUNK + n) + 4 * (f % 2) + 2
                    acc = acc + pltpu.roll(x, to & (cols - 1), 1)
                gathered[f // 2, pl.ds(r, STRIP), :] = acc

    for n in range(2):
        ends[pl.ds(n * rows, rows), :] = gathered[n, :, :].T
    d = gathered[2, :, :].T
    drag_ends[...] = gathered[3, :, :].T[0:8]

    lon_even, lat_even = parity("lon"), parity("lat")

    def line_of(f, c):
        return ends[pl.ds((f // 2) * rows + 4 * (f % 2) + c, levels, stride=8), :]

    def side_of(side, near, far):
        t1, k1, u1, v1 = (line_of(f, near) for f in range(4))
        t2, k2, u2 = (line_of(f, far) for f in range(3))
        wet = iota((levels, cols), 0).astype(F32) < jnp.minimum(d[near : near + 1], d[far : far + 1])
        return t1, k1, u1, v1, jnp.where(wet, face(side, u2, u1, t2, t1, k2, k1), 0.0)

    for q, (east, west) in enumerate(zip(side_of(1.0, 1, 0), side_of(-1.0, 2, 3))):
        at = pl.ds(q * levels, levels)
        send_a[at, :] = jnp.where(lon_even, east, west)
        send_b[at, :] = jnp.where(lon_even, west, east)
    tail = (RIM - TAIL, cols)
    sub = iota(tail, 0)

    def tail_of(near, far):
        near, far = (jnp.broadcast_to(d[r : r + 1], tail) for r in (near, far))
        return jnp.where(sub == 0, near, jnp.where(sub == 1, far, 0.0))

    east, west = tail_of(1, 0), tail_of(2, 3)
    send_a[pl.ds(TAIL, RIM - TAIL), :] = jnp.where(lon_even, east, west)
    send_b[pl.ds(TAIL, RIM - TAIL), :] = jnp.where(lon_even, west, east)


def corner_kernel(levels, send_a, send_b, rim_b, rim_a, when, out_a, out_b):
    cols = send_a.shape[1]
    lon_even, lat_even = parity("lon"), parity("lat")
    a, b = rim_a[...], rim_b[...]
    b = jnp.where(lax.axis_index("lat") == 0, 0.0, b)
    south, north = square(jnp.where(lat_even, b, a)).T, square(jnp.where(lat_even, a, b)).T
    is_top = lax.axis_index("lat") == lax.axis_size("lat") - 1
    line = iota((1, cols), 1)
    turn = jnp.where((line >= 2 * levels) & (line < 4 * levels), -1.0, 1.0)
    first, last = north[0:1], north[cols - 1 : cols]
    first, last = jnp.where(is_top, turn * last, first), jnp.where(is_top, turn * first, last)
    tail = (RIM - TAIL, cols)
    sub = iota(tail, 0)
    for n, (main, out) in enumerate(((send_a, out_a), (send_b, out_b))):
        east = lon_even if n == 0 else jnp.logical_not(lon_even)
        s = jnp.broadcast_to(jnp.where(east, south[cols - 1 : cols], south[0:1]), tail)
        q = jnp.broadcast_to(jnp.where(east, last, first), tail)
        out[pl.ds(0, TAIL), :] = main[pl.ds(0, TAIL), :]
        depths = main[pl.ds(TAIL, RIM - TAIL), :]
        out[pl.ds(TAIL, RIM - TAIL), :] = jnp.where(sub == 2, s, jnp.where(sub == 3, q, depths))


def inner_kernel(
    levels, first, last, strip, t, u, v, kd, depth, drag, coriolis, p_in, up_in,
    t_out, u_out, v_out, p, up,
    fn, gu, gv, back, de, dw, dn, dragn,
):
    rows, cols = depth.shape
    zero = jnp.zeros((PAD, cols), F32)
    for ref in (fn, gu, back):
        ref[pl.ds(0, PAD), :] = zero

    shape = (strip, cols)
    lane = iota(shape, 1)
    row = iota(shape, 0)
    starts = range(0, rows, strip)
    for r in starts:
        here = pl.ds(r, strip)
        d, f = depth[here, :], drag[here, :]
        de[here, :] = jnp.where(lane < cols - 1, jnp.minimum(d, lanes(d, -1)), 0.0)
        dw[here, :] = jnp.where(lane > 0, jnp.minimum(d, lanes(d, 1)), 0.0)
        if r + strip < rows:
            north = pl.ds(r + 1, strip)
            dn[here, :] = jnp.minimum(d, depth[north, :])
            dragn[here, :] = drag[north, :]
        else:
            dn[here, :] = jnp.where(row < strip - 1, jnp.minimum(d, sublanes(d, -1)), 0.0)
            dragn[here, :] = sublanes(f, -1)

    up[...] = jnp.zeros(up.shape, F32) if p_in is None else up_in[...]
    p[...] = jnp.zeros(p.shape, F32) if p_in is None else p_in[...]

    def one_level(k):
        kf = k.astype(F32)
        base = pl.multiple_of(k * rows, rows)
        above = pl.multiple_of(jnp.minimum(k + 1, levels - 1) * rows, rows)
        for r in starts:
            here = out = pl.ds(base + r, strip)
            plane, padded, below = pl.ds(r, strip), pl.ds(PAD + r, strip), pl.ds(PAD + r - 1, strip)

            def north_of(ref, mid):
                return ref[pl.ds(base + r + 1, strip), :] if r + strip < rows else sublanes(mid, -1)

            d = depth[plane, :]
            t0, u0, v0, k0 = t[here, :], u[here, :], v[here, :], kd[here, :]
            wet, wet_e, wet_n = d > kf, de[plane, :] > kf, dn[plane, :] > kf

            t1, u1, k1 = lanes(t0, -1), lanes(u0, -1), lanes(k0, -1)
            flux = 0.0625 * ((u0 + u1) * (t0 + t1)) - 0.125 * ((k0 + k1) * (t1 - t0))
            flux = jnp.where(wet_e, flux, 0.0)
            change = lanes(flux, 1) - flux
            wet_w = dw[plane, :] > kf
            lap_u = jnp.where(wet_e, u1 - u0, 0.0) + jnp.where(wet_w, lanes(u0, 1) - u0, 0.0)
            lap_v = jnp.where(wet_e, lanes(v0, -1) - v0, 0.0) + jnp.where(wet_w, lanes(v0, 1) - v0, 0.0)

            t1, v1, k1 = north_of(t, t0), north_of(v, v0), north_of(kd, k0)
            flux = 0.0625 * ((v0 + v1) * (t0 + t1)) - 0.125 * ((k0 + k1) * (t1 - t0))
            flux = jnp.where(wet_n, flux, 0.0)
            lap = jnp.where(wet_n, north_of(u, u0) - u0, 0.0)
            lap2 = jnp.where(wet_n, v1 - v0, 0.0)
            fn[padded, :] = flux
            gu[padded, :] = lap
            gv[plane, :] = lap2
            change = change + (fn[below, :] - flux)
            lap_u = lap_u + (lap - gu[below, :])
            lap_v = lap_v + lap2

            higher = pl.ds(above + r, strip)
            rise = 0.125 * ((kd[higher, :] + k0) * (t[higher, :] - t0))
            rise = jnp.where(d > kf + 1.0, rise, 0.0)
            change = change + (rise - up[plane, :])
            up[plane, :] = rise

            t_next = jnp.where(wet, t0 + change, 0.0)
            t_out[out, :] = t_next
            p[padded, :] = p[padded, :] + t_next
            c, f = coriolis[plane, :], drag[plane, :]
            u_out[out, :] = u0 + (c * v0 + f * lap_u)
            v_out[out, :] = v0 + (f * lap_v - c * u0)

        middle = pl.ds(PAD, rows)
        back[middle, :] = 0.0125 * p[middle, :] - dragn[...] * gv[...]
        for r in starts:
            plane, out = pl.ds(r, strip), pl.ds(base + r, strip)
            wet = depth[plane, :] > kf
            mid = p[pl.ds(PAD + r, strip), :]
            slope = jnp.where(lane < cols - 1, lanes(mid, -1), 0.0) - jnp.where(lane > 0, lanes(mid, 1), 0.0)
            u_next = u_out[out, :] - 0.0125 * slope
            v_next = v_out[out, :] + back[pl.ds(PAD + r - 1, strip), :] - 0.0125 * p[pl.ds(PAD + r + 1, strip), :]
            u_out[out, :] = jnp.where(wet, u_next, 0.0)
            v_out[out, :] = jnp.where(wet, v_next, 0.0)

    @pl.loop(first, last)
    def each_level(k):
        one_level(k)


def levels_before(levels):
    lon, lat = lax.axis_index("lon"), lax.axis_index("lat")
    is_top = lat == lax.axis_size("lat") - 1
    is_last = lon == lax.axis_size("lon") - 1
    some = jnp.where(jnp.logical_not(is_top) & is_last, 0, levels // 2)
    some = jnp.where(is_top & (lon == 0), 3 * levels // 8, some)
    return jnp.where(is_top & (lon == 1), 5 * levels // 8, some)


def low_kernel(levels, strip, *refs):
    inner_kernel(levels, 0, levels_before(levels), strip, *refs[:7], None, None, *refs[7:])


def high_kernel(levels, strip, *refs):
    inputs, (_, *low), outs, rest = refs[:9], refs[9:13], refs[13:16], refs[16:]
    rows = refs[4].shape[0]
    split = levels_before(levels)

    @pl.loop(0, split)
    def hand_on(k):
        for src, dst in zip(low, outs):
            for r in range(0, rows, strip):
                at = pl.ds(pl.multiple_of(k * rows, rows) + r, strip)
                dst[at, :] = src[at, :]

    inner_kernel(levels, split, levels, strip, *inputs, *outs, *rest)


def border_kernel(
    levels, t_in, u_in, v_in,
    send_a, send_b, recv_a, recv_b, lat_a, lat_b, rim_a, rim_b, drag, drag_ends,
    t_out, u_out, v_out, tb, ub, vb, tr, ur, turned, turned_t, sem, end_sem,
):
    rows, cols = drag.shape
    lon_even, lat_even = parity("lon"), parity("lat")
    is_top = lax.axis_index("lat") == lax.axis_size("lat") - 1

    def sides(even, a, b):
        a, b = a[...], b[...]
        return jnp.where(even, b, a), jnp.where(even, a, b)

    own_w, own_e = sides(lon_even, send_a, send_b)
    west, east = sides(lon_even, recv_a, recv_b)
    own_s, own_n = sides(lat_even, lat_a, lat_b)
    south, north = sides(lat_even, rim_a, rim_b)
    south = jnp.where(lax.axis_index("lat") == 0, 0.0, south)

    low, high = TAIL + 2, TAIL + 3
    ends_w, ends_e = square(west).T, square(east).T
    sw, nw = (ends_w[:, n : n + 1] for n in (low, high))
    se, ne = (ends_e[:, n : n + 1] for n in (low, high))
    line = iota((RIM, 1), 0)
    turn = jnp.where((line >= 2 * levels) & (line < 4 * levels), -1.0, 1.0)
    mirrored = turn * jnp.take_along_axis(north, cols - 1 - iota((RIM, cols), 1), axis=1)
    north = jnp.where(is_top, mirrored, north)

    four, half = (4 * levels, cols), 2 * levels

    def stack(q, blocks):
        return jnp.concatenate([x[q * levels : (q + 1) * levels] for x in blocks], 0)

    def lines(rows_of_one):
        return jnp.concatenate([jnp.broadcast_to(x, (levels, cols)) for x in rows_of_one], 0)

    outside, inside = (west, east, south, north), (own_w, own_e, own_s, own_n)
    t1, k1, n1, s1, outer = (stack(q, outside) for q in range(5))
    t0, k0, n0, s0 = (stack(q, inside) for q in range(4))
    d1 = lines([x[TAIL : TAIL + 1] for x in outside])
    d0, d0b = (lines([x[TAIL + n : TAIL + n + 1] for x in inside]) for n in (0, 1))
    f0 = lines([drag_ends[2:3, :], drag_ends[1:2, :], drag[0:1, :], drag[rows - 1 : rows, :]])
    sub, lane = iota(four, 0), iota(four, 1)
    level_i = sub & (levels - 1)
    level = level_i.astype(F32)
    side = jnp.where((sub & levels) == 0, 1.0, -1.0)
    wet0, wet1 = level < d0, level < d1
    wet01 = level < jnp.minimum(d0, d1)

    inward = jnp.where(wet01, face(side, n1, n0, t1, t0, k1, k0), 0.0)

    def turn_columns(ref, lines_of):
        for g, x in enumerate(lines_of):
            ref[pl.ds(g, levels, stride=8), :] = x
        ref[...] = ref[...].T

    tail = (8, cols)
    sub8, lane8 = iota(tail, 0), iota((STRIP, cols), 1)
    one, wide = (lane8 < 1) | (lane8 >= cols - 1), (lane8 < 2) | (lane8 >= cols - 2)
    middle = pl.ds(8, rows - 16)

    def add_columns(k, part, buf, ref, mask, to):
        base = pl.multiple_of(k * rows, rows)
        by = (to - 8 * k) & (cols - 1)
        for r in range(0, rows, STRIP):
            moved = jnp.where(mask, pltpu.roll(ref[pl.ds(r, STRIP), :], by, 1), 0.0)
            buf[k, pl.ds(r, STRIP), :] = part[pl.ds(base + r, STRIP), :] + moved

    def add_rows(k, buf, ref):
        for s, near, begin in ((0, 0, 0), (1, 7, rows - 8)):
            line = jnp.broadcast_to(ref[pl.ds(s * levels + k, 1), :], tail)
            at = pl.ds(begin, 8)
            buf[k, at, :] = buf[k, at, :] + jnp.where(sub8 == near, line, 0.0)

    def heat_out(k):
        return pltpu.make_async_copy(tb.at[k], t_out.at[k], sem.at[0, k])

    def east_out(k):
        return pltpu.make_async_copy(ub.at[k], u_out.at[k], sem.at[1, k])

    def north_out(k):
        return pltpu.make_async_copy(vb.at[k, middle], v_out.at[k, middle], sem.at[2, k])

    def north_ends(n):
        at = pl.ds((0, rows - 8)[n], 8)
        return pltpu.make_async_copy(vb.at[:, at], v_out.at[:, at], end_sem.at[n])

    dp0 = inward
    step = 1
    while step < levels:
        dp0 = dp0 + jnp.where(level_i >= step, sublanes(dp0, step), 0.0)
        step *= 2
    slope = jnp.where(lane < cols - 1, lanes(dp0, -1), 0.0) - jnp.where(lane > 0, lanes(dp0, 1), 0.0)
    ds = f0 * jnp.where(wet01, s1 - s0, 0.0) - 0.0125 * slope
    ds = jnp.where(wet0, ds, 0.0)
    tr[...] = inward[half:]
    ur[...] = ds[half:]
    turn_columns(turned_t, (inward[levels:half], inward[:levels], ds[levels:half], ds[:levels]))

    @pl.loop(0, levels, step=CHUNK)
    def first_out(begin):
        for i in range(CHUNK):
            k = begin + i
            add_columns(k, t_in, tb, turned_t, one, cols - 1)
            add_rows(k, tb, tr)
            heat_out(k).start()
            add_columns(k, v_in, vb, turned_t, one, cols - 1 - 2)
            north_out(k).start()

    before, after = (sw, se, sw, nw), (nw, ne, se, ne)

    def beyond(x, at):
        lo, hi = (
            jnp.concatenate(
                [jnp.broadcast_to(c[n : n + m], (levels, 1)) for c, (n, m) in zip(cells, at)], 0
            )
            for cells in (before, after)
        )
        lo, hi = jnp.broadcast_to(lo, four), jnp.broadcast_to(hi, four)
        return jnp.where(lane == 0, lo, lanes(x, 1)), jnp.where(lane == cols - 1, hi, lanes(x, -1))

    t_w, t_e = beyond(t1, ((0, levels),) * 4)
    k_w, k_e = beyond(k1, ((levels, levels),) * 4)
    s_w, s_e = beyond(s1, ((2 * levels, levels),) * 2 + ((3 * levels, levels),) * 2)
    d_w, d_e = beyond(d1, ((TAIL, 1),) * 4)
    flux_w = jnp.where(level < jnp.minimum(d_w, d1), face(1.0, s_w, s1, t_w, t1, k_w, k1), 0.0)
    flux_e = jnp.where(level < jnp.minimum(d1, d_e), face(1.0, s1, s_e, t1, t_e, k1, k_e), 0.0)
    rise = 0.125 * ((sublanes(k1, -1) + k1) * (sublanes(t1, -1) - t1))
    rise = jnp.where((level + 1.0 < d1) & (level_i < levels - 1), rise, 0.0)
    change = outer - inward + flux_w - flux_e + rise - sublanes(rise, 1)
    p1 = jnp.where(wet1, t1 + change, 0.0)
    step = 1
    while step < levels:
        p1 = p1 + jnp.where(level_i >= step, sublanes(p1, step), 0.0)
        step *= 2
    dn = 0.0125 * (side * p1) + f0 * jnp.where(wet01, n1 - n0, 0.0)
    dn = jnp.where(wet0, dn, 0.0)
    dn2 = jnp.where(level < d0b, 0.0125 * (side * dp0), 0.0)
    turn_columns(turned, (dn2[levels:half], dn[levels:half], dn[:levels], dn2[:levels]))
    for row, x in ((0, dn[half : half + levels]), (1, dn2[half : half + levels]),
                   (rows - 1, dn[half + levels :]), (rows - 2, dn2[half + levels :])):
        vb[:, row, :] = vb[:, row, :] + x
    for n in range(2):
        north_ends(n).start()

    @pl.loop(0, levels, step=CHUNK)
    def last_out(begin):
        for i in range(CHUNK):
            add_columns(begin + i, u_in, ub, turned, wide, cols - 2)
            add_rows(begin + i, ub, ur)
            east_out(begin + i).start()

    for n in range(2):
        north_ends(n).wait()

    @pl.loop(0, levels)
    def finish(k):
        for out in (heat_out, north_out, east_out):
            out(k).wait()


def on_device(t, u, v, kd, friction, water, strata):
    levels, rows, cols = t.shape
    lon_n, lat_n = lax.axis_size("lon"), lax.axis_size("lat")
    vmem = pl.BlockSpec(memory_space=pltpu.VMEM)
    hbm = pl.BlockSpec(memory_space=pltpu.HBM)
    params = pltpu.CompilerParams(vmem_limit_bytes=12 * 1024 * 1024)
    tall = levels * rows
    plane, message, stack = (rows, cols), (RIM, cols), (tall, cols)

    def in_hbm(*arrays):
        return [pltpu.with_memory_space_constraint(x, pltpu.HBM) for x in arrays]

    lat_a, lat_b, coriolis, drag = pl.pallas_call(
        functools.partial(rows_kernel, levels),
        out_shape=[pltpu.VMEM((RIM, 1, cols), F32)] * 2 + [pltpu.VMEM(plane, F32)] * 2,
        in_specs=[hbm] * 7,
        out_specs=[vmem] * 4,
        scratch_shapes=[pltpu.VMEM((2, 3, levels, 1, cols), F32)]
        + [pltpu.VMEM((4, 1, cols), jnp.int32)] * 2
        + [pltpu.SemaphoreType.DMA((2, 7)), pltpu.SemaphoreType.DMA((2, 2, 2)), pltpu.SemaphoreType.DMA],
        compiler_params=params,
        name="rows",
    )(
        *in_hbm(*[x.reshape(levels, rows, 1, cols) for x in (t, u, v, kd)]),
        *in_hbm(*[x.reshape(rows, 1, cols) for x in (water, strata)], friction),
    )
    lat_a, lat_b = lat_a.reshape(message), lat_b.reshape(message)
    lat_pairs = [(i, i ^ 1) for i in range(lat_n)]
    cross = []
    for m in range(lon_n):
        for i in range(1, lat_n - 1, 2):
            here, north = m * lat_n + i, m * lat_n + i + 1
            cross += [(here, north), (north, here)]
        cross.append((m * lat_n + lat_n - 1, (lon_n - 1 - m) * lat_n + lat_n - 1))
        cross.append((m * lat_n, (m ^ 1) * lat_n))
    rim_a = lax.ppermute(lat_a, "lat", lat_pairs)
    rim_b = lax.ppermute(lat_b, ("lon", "lat"), cross)

    fields = [x.reshape(stack) for x in (t, u, v, kd)]
    send_a, send_b, depth, drag_ends = pl.pallas_call(
        functools.partial(pack_kernel, levels),
        out_shape=[pltpu.VMEM(s, F32) for s in (message, message, plane, (8, cols))],
        in_specs=[vmem] * 7,
        out_specs=[vmem] * 4,
        scratch_shapes=[pltpu.VMEM((4, rows, cols), F32), pltpu.VMEM((2 * rows, cols), F32)],
        compiler_params=params,
        name="pack",
    )(*fields, water, strata, drag)
    padded, flat = pltpu.VMEM((rows + 2 * PAD, cols), F32), pltpu.VMEM(plane, F32)
    whole = pltpu.VMEM(stack, F32)
    work = [padded, padded, flat, padded] + [flat] * 4
    cost = pl.CostEstimate(flops=50 * tall * cols, bytes_accessed=1 << 20, transcendentals=0)
    *first, p_mid, up_mid = pl.pallas_call(
        functools.partial(low_kernel, levels, STRIP),
        out_shape=[whole] * 3 + [padded, flat],
        in_specs=[vmem] * 7,
        out_specs=[vmem] * 5,
        scratch_shapes=work,
        compiler_params=params,
        cost_estimate=cost,
        name="inner_low",
    )(*fields, depth, drag, coriolis)
    send_a, send_b = pl.pallas_call(
        functools.partial(corner_kernel, levels),
        out_shape=[pltpu.VMEM(message, F32)] * 2,
        in_specs=[vmem] * 5,
        out_specs=[vmem] * 2,
        compiler_params=params,
        name="corners",
    )(send_a, send_b, rim_b, rim_a, up_mid)
    lon_pairs = [(i, i ^ 1) for i in range(lon_n)]
    lon_cross = [(i, (i + 1) % lon_n if i % 2 else (i - 1) % lon_n) for i in range(lon_n)]
    recv_b = lax.ppermute(send_b, "lon", lon_cross)
    recv_a = lax.ppermute(send_a, "lon", lon_pairs)

    second = pl.pallas_call(
        functools.partial(high_kernel, levels, STRIP),
        out_shape=[whole] * 3,
        in_specs=[vmem] * 13,
        out_specs=[vmem] * 3,
        scratch_shapes=[padded, flat] + work,
        compiler_params=params,
        cost_estimate=cost,
        name="inner_high",
    )(*fields, depth, drag, coriolis, p_mid, up_mid, send_a, *first)

    rim_pair = pltpu.VMEM((2 * levels, cols), F32)
    outs = pl.pallas_call(
        functools.partial(border_kernel, levels),
        out_shape=[jax.ShapeDtypeStruct((levels, rows, cols), F32)] * 3,
        in_specs=[vmem] * 13,
        out_specs=[hbm] * 3,
        scratch_shapes=[pltpu.VMEM((levels, rows, cols), F32)] * 3
        + [rim_pair] * 2
        + [pltpu.VMEM(plane, F32)] * 2
        + [pltpu.SemaphoreType.DMA((3, levels)), pltpu.SemaphoreType.DMA((2,))],
        compiler_params=params,
        name="border",
    )(*second, send_a, send_b, recv_a, recv_b, lat_a, lat_b, rim_a, rim_b, drag, drag_ends)
    return tuple(outs)


def solution(mesh):
    stack, plane = P(None, "lat", "lon"), P("lat", "lon")
    return jax.shard_map(
        on_device,
        mesh=mesh,
        in_specs=(stack,) * 4 + (plane,) * 3,
        out_specs=(stack,) * 3,
        check_vma=False,
    )
```

```python
import functools

import jax
import jax.numpy as jnp
from jax import lax
from jax.experimental import pallas as pl
from jax.experimental.pallas import tpu as pltpu
from jax.sharding import PartitionSpec as P

DT = 0.25
GRAV = 0.1
F32 = jnp.float32
PAD = 8
RIM = 88
TAIL = 80
CHUNK = 8
STRIP = 32


def lanes(x, by):
    by %= x.shape[1]
    return x if by == 0 else pltpu.roll(x, by, 1)


def sublanes(x, by):
    by %= x.shape[0]
    return x if by == 0 else pltpu.roll(x, by, 0)


def iota(shape, dim):
    return lax.broadcasted_iota(jnp.int32, shape, dim)


def parity(axis):
    return lax.axis_index(axis) % 2 == 0


def face(side, ua, ub, ta, tb, ka, kb):
    return side * (0.0625 * ((ua + ub) * (ta + tb))) - 0.125 * ((ka + kb) * (tb - ta))


def square(x):
    rows, cols = x.shape
    return jnp.concatenate([x, jnp.zeros((cols - rows, cols), F32)], 0)


def rows_kernel(
    levels, t, u, v, kd, water, strata, friction, lat_a, lat_b, coriolis, drag,
    far_rows, water_rows, strata_rows, sem, plane_sem, drag_sem,
):
    rows, cols = coriolis.shape
    copies, planes = [], []
    lat_even = parity("lat")
    for side, message in enumerate((lat_a, lat_b)):
        north = lat_even if side == 0 else jnp.logical_not(lat_even)
        near = jnp.where(north, rows - 1, 0)
        far = jnp.where(north, rows - 2, 1)
        for n, row in enumerate((near, far)):
            for m, (src, dst) in enumerate(((water, water_rows), (strata, strata_rows))):
                at = dst.at[pl.ds(2 * side + n, 1)]
                planes.append(pltpu.make_async_copy(src.at[pl.ds(row, 1)], at, plane_sem.at[m, side, n]))
        for q, src in enumerate((t, kd, v, u)):
            at = message.at[pl.ds(q * levels, levels)]
            copies.append(pltpu.make_async_copy(src.at[:, near], at, sem.at[side, q]))
        for q, src in enumerate((t, kd, v)):
            copies.append(pltpu.make_async_copy(src.at[:, far], far_rows.at[side, q], sem.at[side, 4 + q]))
    whole = pltpu.make_async_copy(friction, drag, drag_sem)
    for copy in planes + copies + [whole]:
        copy.start()
    row = iota((8, rows), 1) + lax.axis_index("lat") * rows
    total = rows * lax.axis_size("lat")
    line = DT * jnp.sin(jnp.pi * ((row.astype(F32) + 0.5) / total - 0.5))
    coriolis[...] = jnp.broadcast_to(line[0:1], (cols, rows)).T
    for copy in planes:
        copy.wait()
    for side, message in enumerate((lat_a, lat_b)):
        message[pl.ds(TAIL + 2, RIM - TAIL - 2)] = jnp.zeros((RIM - TAIL - 2, 1, cols), F32)
        for n in range(2):
            at = pl.ds(2 * side + n, 1)
            message[pl.ds(TAIL + n, 1)] = (water_rows[at] * strata_rows[at]).astype(F32)
    whole.wait()
    drag[...] = DT * drag[...]
    for copy in copies:
        copy.wait()
    level = iota((levels, 1, cols), 0).astype(F32)
    for side, message in enumerate((lat_a, lat_b)):
        north = lat_even if side == 0 else jnp.logical_not(lat_even)
        t1, k1, v1 = (message[pl.ds(q * levels, levels)] for q in range(3))
        t2, k2, v2 = (far_rows[side, q] for q in range(3))
        wet = level < jnp.minimum(message[pl.ds(TAIL, 1)], message[pl.ds(TAIL + 1, 1)])
        flux = face(jnp.where(north, 1.0, -1.0), v2, v1, t2, t1, k2, k1)
        message[pl.ds(4 * levels, levels)] = jnp.where(wet, flux, 0.0)


def pack_kernel(
    levels, t, u, v, kd, water, strata, drag,
    send_a, send_b, depth, drag_ends, gathered, ends,
):
    rows, cols = depth.shape
    lane = iota((STRIP, cols), 1)
    edge = (lane < 2) | (lane >= cols - 2)
    for r in range(0, rows, STRIP):
        at = pl.ds(r, STRIP)
        d = (water[at, :] * strata[at, :]).astype(F32)
        depth[at, :] = d
        gathered[2, at, :] = lanes(d, 2)
        gathered[3, at, :] = lanes(drag[at, :], 2)
        gathered[0, at, :] = jnp.zeros((STRIP, cols), F32)
        gathered[1, at, :] = jnp.zeros((STRIP, cols), F32)

    @pl.loop(0, levels // CHUNK)
    def one_piece(part):
        begin = pl.multiple_of(part * CHUNK * rows, rows)
        for f, full in enumerate((t, kd, u, v)):
            for r in range(0, rows, STRIP):
                acc = gathered[f // 2, pl.ds(r, STRIP), :]
                for n in range(CHUNK):
                    x = jnp.where(edge, full[pl.ds(begin + n * rows + r, STRIP), :], 0.0)
                    to = 8 * (part * CHUNK + n) + 4 * (f % 2) + 2
                    acc = acc + pltpu.roll(x, to & (cols - 1), 1)
                gathered[f // 2, pl.ds(r, STRIP), :] = acc

    for n in range(2):
        ends[pl.ds(n * rows, rows), :] = gathered[n, :, :].T
    d = gathered[2, :, :].T
    drag_ends[...] = gathered[3, :, :].T[0:8]

    lon_even, lat_even = parity("lon"), parity("lat")

    def line_of(f, c):
        return ends[pl.ds((f // 2) * rows + 4 * (f % 2) + c, levels, stride=8), :]

    def side_of(side, near, far):
        t1, k1, u1, v1 = (line_of(f, near) for f in range(4))
        t2, k2, u2 = (line_of(f, far) for f in range(3))
        wet = iota((levels, cols), 0).astype(F32) < jnp.minimum(d[near : near + 1], d[far : far + 1])
        return t1, k1, u1, v1, jnp.where(wet, face(side, u2, u1, t2, t1, k2, k1), 0.0)

    for q, (east, west) in enumerate(zip(side_of(1.0, 1, 0), side_of(-1.0, 2, 3))):
        at = pl.ds(q * levels, levels)
        send_a[at, :] = jnp.where(lon_even, east, west)
        send_b[at, :] = jnp.where(lon_even, west, east)
    tail = (RIM - TAIL, cols)
    sub = iota(tail, 0)

    def tail_of(near, far):
        near, far = (jnp.broadcast_to(d[r : r + 1], tail) for r in (near, far))
        return jnp.where(sub == 0, near, jnp.where(sub == 1, far, 0.0))

    east, west = tail_of(1, 0), tail_of(2, 3)
    send_a[pl.ds(TAIL, RIM - TAIL), :] = jnp.where(lon_even, east, west)
    send_b[pl.ds(TAIL, RIM - TAIL), :] = jnp.where(lon_even, west, east)


def corner_kernel(levels, send_a, send_b, rim_b, rim_a, when, out_a, out_b):
    cols = send_a.shape[1]
    lon_even, lat_even = parity("lon"), parity("lat")
    a, b = rim_a[...], rim_b[...]
    b = jnp.where(lax.axis_index("lat") == 0, 0.0, b)
    south, north = square(jnp.where(lat_even, b, a)).T, square(jnp.where(lat_even, a, b)).T
    is_top = lax.axis_index("lat") == lax.axis_size("lat") - 1
    line = iota((1, cols), 1)
    turn = jnp.where((line >= 2 * levels) & (line < 4 * levels), -1.0, 1.0)
    first, last = north[0:1], north[cols - 1 : cols]
    first, last = jnp.where(is_top, turn * last, first), jnp.where(is_top, turn * first, last)
    tail = (RIM - TAIL, cols)
    sub = iota(tail, 0)
    for n, (main, out) in enumerate(((send_a, out_a), (send_b, out_b))):
        east = lon_even if n == 0 else jnp.logical_not(lon_even)
        s = jnp.broadcast_to(jnp.where(east, south[cols - 1 : cols], south[0:1]), tail)
        q = jnp.broadcast_to(jnp.where(east, last, first), tail)
        out[pl.ds(0, TAIL), :] = main[pl.ds(0, TAIL), :]
        depths = main[pl.ds(TAIL, RIM - TAIL), :]
        out[pl.ds(TAIL, RIM - TAIL), :] = jnp.where(sub == 2, s, jnp.where(sub == 3, q, depths))


def inner_kernel(
    levels, first, last, strip, t, u, v, kd, depth, drag, coriolis, p_in, up_in,
    t_out, u_out, v_out, p, up, de, dw, dn, dragn,
    fn, gu, gv, back,
):
    rows, cols = depth.shape
    zero = jnp.zeros((PAD, cols), F32)
    for ref in (fn, gu, back):
        ref[pl.ds(0, PAD), :] = zero

    shape = (strip, cols)
    lane = iota(shape, 1)
    row = iota(shape, 0)
    starts = range(0, rows, strip)
    for r in starts if p_in is None else ():
        here = pl.ds(r, strip)
        d, f = depth[here, :], drag[here, :]
        de[here, :] = jnp.where(lane < cols - 1, jnp.minimum(d, lanes(d, -1)), 0.0)
        dw[here, :] = jnp.where(lane > 0, jnp.minimum(d, lanes(d, 1)), 0.0)
        if r + strip < rows:
            north = pl.ds(r + 1, strip)
            dn[here, :] = jnp.minimum(d, depth[north, :])
            dragn[here, :] = drag[north, :]
        else:
            dn[here, :] = jnp.where(row < strip - 1, jnp.minimum(d, sublanes(d, -1)), 0.0)
            dragn[here, :] = sublanes(f, -1)

    up[...] = jnp.zeros(up.shape, F32) if p_in is None else up_in[...]
    p[...] = jnp.zeros(p.shape, F32) if p_in is None else p_in[...]

    def one_level(k):
        kf = k.astype(F32)
        base = pl.multiple_of(k * rows, rows)
        above = pl.multiple_of(jnp.minimum(k + 1, levels - 1) * rows, rows)
        for r in starts:
            here = out = pl.ds(base + r, strip)
            plane, padded, below = pl.ds(r, strip), pl.ds(PAD + r, strip), pl.ds(PAD + r - 1, strip)

            def north_of(ref, mid):
                return ref[pl.ds(base + r + 1, strip), :] if r + strip < rows else sublanes(mid, -1)

            d = depth[plane, :]
            t0, u0, v0, k0 = t[here, :], u[here, :], v[here, :], kd[here, :]
            wet, wet_e, wet_n = d > kf, de[plane, :] > kf, dn[plane, :] > kf

            t1, u1, k1 = lanes(t0, -1), lanes(u0, -1), lanes(k0, -1)
            flux = 0.0625 * ((u0 + u1) * (t0 + t1)) - 0.125 * ((k0 + k1) * (t1 - t0))
            flux = jnp.where(wet_e, flux, 0.0)
            change = lanes(flux, 1) - flux
            wet_w = dw[plane, :] > kf
            lap_u = jnp.where(wet_e, u1 - u0, 0.0) + jnp.where(wet_w, lanes(u0, 1) - u0, 0.0)
            lap_v = jnp.where(wet_e, lanes(v0, -1) - v0, 0.0) + jnp.where(wet_w, lanes(v0, 1) - v0, 0.0)

            t1, v1, k1 = north_of(t, t0), north_of(v, v0), north_of(kd, k0)
            flux = 0.0625 * ((v0 + v1) * (t0 + t1)) - 0.125 * ((k0 + k1) * (t1 - t0))
            flux = jnp.where(wet_n, flux, 0.0)
            lap = jnp.where(wet_n, north_of(u, u0) - u0, 0.0)
            lap2 = jnp.where(wet_n, v1 - v0, 0.0)
            fn[padded, :] = flux
            gu[padded, :] = lap
            gv[plane, :] = lap2
            change = change + (fn[below, :] - flux)
            lap_u = lap_u + (lap - gu[below, :])
            lap_v = lap_v + lap2

            higher = pl.ds(above + r, strip)
            rise = 0.125 * ((kd[higher, :] + k0) * (t[higher, :] - t0))
            rise = jnp.where(d > kf + 1.0, rise, 0.0)
            change = change + (rise - up[plane, :])
            up[plane, :] = rise

            t_next = jnp.where(wet, t0 + change, 0.0)
            t_out[out, :] = t_next
            p[padded, :] = p[padded, :] + t_next
            c, f = coriolis[plane, :], drag[plane, :]
            u_out[out, :] = u0 + (c * v0 + f * lap_u)
            v_out[out, :] = v0 + (f * lap_v - c * u0)

        middle = pl.ds(PAD, rows)
        back[middle, :] = 0.0125 * p[middle, :] - dragn[...] * gv[...]
        for r in starts:
            plane, out = pl.ds(r, strip), pl.ds(base + r, strip)
            wet = depth[plane, :] > kf
            mid = p[pl.ds(PAD + r, strip), :]
            slope = jnp.where(lane < cols - 1, lanes(mid, -1), 0.0) - jnp.where(lane > 0, lanes(mid, 1), 0.0)
            u_next = u_out[out, :] - 0.0125 * slope
            v_next = v_out[out, :] + back[pl.ds(PAD + r - 1, strip), :] - 0.0125 * p[pl.ds(PAD + r + 1, strip), :]
            u_out[out, :] = jnp.where(wet, u_next, 0.0)
            v_out[out, :] = jnp.where(wet, v_next, 0.0)

    @pl.loop(first, last)
    def each_level(k):
        one_level(k)


def levels_before(levels):
    lon, lat = lax.axis_index("lon"), lax.axis_index("lat")
    is_top = lat == lax.axis_size("lat") - 1
    is_last = lon == lax.axis_size("lon") - 1
    some = jnp.where(jnp.logical_not(is_top) & is_last, 0, levels // 2)
    some = jnp.where(is_top & (lon == 0), 3 * levels // 8, some)
    return jnp.where(is_top & (lon == 1), 5 * levels // 8, some)


def low_kernel(levels, strip, *refs):
    inner_kernel(levels, 0, levels_before(levels), strip, *refs[:7], None, None, *refs[7:])


def high_kernel(levels, strip, *refs):
    inputs, planes, (_, *low), outs, rest = refs[:9], refs[9:13], refs[13:17], refs[17:20], refs[20:]
    rows = refs[4].shape[0]
    split = levels_before(levels)

    @pl.loop(0, split)
    def hand_on(k):
        for src, dst in zip(low, outs):
            for r in range(0, rows, strip):
                at = pl.ds(pl.multiple_of(k * rows, rows) + r, strip)
                dst[at, :] = src[at, :]

    inner_kernel(levels, split, levels, strip, *inputs, *outs, *rest[:2], *planes, *rest[2:])


def border_kernel(
    levels, t_in, u_in, v_in,
    send_a, send_b, recv_a, recv_b, lat_a, lat_b, rim_a, rim_b, drag, drag_ends,
    t_out, u_out, v_out, tb, ub, vb, tr, ur, vr0, vr1, turned, turned_t, sem,
):
    rows, cols = drag.shape
    lon_even, lat_even = parity("lon"), parity("lat")
    is_top = lax.axis_index("lat") == lax.axis_size("lat") - 1

    def sides(even, a, b):
        a, b = a[...], b[...]
        return jnp.where(even, b, a), jnp.where(even, a, b)

    own_w, own_e = sides(lon_even, send_a, send_b)
    west, east = sides(lon_even, recv_a, recv_b)
    own_s, own_n = sides(lat_even, lat_a, lat_b)
    south, north = sides(lat_even, rim_a, rim_b)
    south = jnp.where(lax.axis_index("lat") == 0, 0.0, south)

    low, high = TAIL + 2, TAIL + 3
    ends_w, ends_e = square(west).T, square(east).T
    sw, nw = (ends_w[:, n : n + 1] for n in (low, high))
    se, ne = (ends_e[:, n : n + 1] for n in (low, high))
    line = iota((RIM, 1), 0)
    turn = jnp.where((line >= 2 * levels) & (line < 4 * levels), -1.0, 1.0)
    mirrored = turn * jnp.take_along_axis(north, cols - 1 - iota((RIM, cols), 1), axis=1)
    north = jnp.where(is_top, mirrored, north)

    four, half = (4 * levels, cols), 2 * levels

    def stack(q, blocks):
        return jnp.concatenate([x[q * levels : (q + 1) * levels] for x in blocks], 0)

    def lines(rows_of_one):
        return jnp.concatenate([jnp.broadcast_to(x, (levels, cols)) for x in rows_of_one], 0)

    outside, inside = (west, east, south, north), (own_w, own_e, own_s, own_n)
    t1, k1, n1, s1, outer = (stack(q, outside) for q in range(5))
    t0, k0, n0, s0 = (stack(q, inside) for q in range(4))
    d1 = lines([x[TAIL : TAIL + 1] for x in outside])
    d0, d0b = (lines([x[TAIL + n : TAIL + n + 1] for x in inside]) for n in (0, 1))
    f0 = lines([drag_ends[2:3, :], drag_ends[1:2, :], drag[0:1, :], drag[rows - 1 : rows, :]])
    sub, lane = iota(four, 0), iota(four, 1)
    level_i = sub & (levels - 1)
    level = level_i.astype(F32)
    side = jnp.where((sub & levels) == 0, 1.0, -1.0)
    wet0, wet1 = level < d0, level < d1
    wet01 = level < jnp.minimum(d0, d1)

    inward = jnp.where(wet01, face(side, n1, n0, t1, t0, k1, k0), 0.0)

    def turn_columns(ref, lines_of):
        for g, x in enumerate(lines_of):
            ref[pl.ds(g, levels, stride=8), :] = x
        ref[...] = ref[...].T

    tail = (8, cols)
    sub8, lane8 = iota(tail, 0), iota((STRIP, cols), 1)
    one, wide = (lane8 < 1) | (lane8 >= cols - 1), (lane8 < 2) | (lane8 >= cols - 2)
    spots = ((one, cols - 1), (wide, cols - 2), (one, cols - 1 - 4))
    bufs, outs = (tb, ub, vb), (t_out, u_out, v_out)

    def copy_out(n, k):
        at = pl.ds(k * rows, rows)
        return pltpu.make_async_copy(bufs[n].at[at], outs[n].at[at], sem.at[n, k])

    def one_level(k, n, part, inside):
        base, buf = k * rows, bufs[n]
        mask, to = spots[n]
        by = (to - 8 * k) & (cols - 1)
        for r in range(0, rows, STRIP):
            moved = pltpu.roll((turned_t if n == 0 else turned)[pl.ds(r, STRIP), :], by, 1)
            old = part[pl.ds(inside * rows + r, STRIP), :]
            buf[pl.ds(base + r, STRIP), :] = old + jnp.where(mask, moved, 0.0)

        def row_of(ref, s):
            return jnp.broadcast_to(ref[pl.ds(s * levels + k, 1), :], tail)

        for s, (near, far, begin) in enumerate(((0, 1, 0), (7, 6, rows - 8))):
            add = jnp.where(sub8 == near, row_of((tr, ur, vr0)[n], s), 0.0)
            if n == 2:
                add = jnp.where(sub8 == far, row_of(vr1, s), add)
            at = pl.ds(base + begin, 8)
            buf[at, :] = buf[at, :] + add
        copy_out(n, k).start()

    def all_levels(*which):
        for k in range(levels):
            for n in which:
                one_level(k, n, (t_in, u_in, v_in)[n], k)

    tr[...] = inward[half:]
    turn_columns(turned_t, (inward[levels:half], inward[:levels]))
    all_levels(0)

    before, after = (sw, se, sw, nw), (nw, ne, se, ne)

    def beyond(x, at):
        lo, hi = (
            jnp.concatenate(
                [jnp.broadcast_to(c[n : n + m], (levels, 1)) for c, (n, m) in zip(cells, at)], 0
            )
            for cells in (before, after)
        )
        lo, hi = jnp.broadcast_to(lo, four), jnp.broadcast_to(hi, four)
        return jnp.where(lane == 0, lo, lanes(x, 1)), jnp.where(lane == cols - 1, hi, lanes(x, -1))

    t_w, t_e = beyond(t1, ((0, levels),) * 4)
    k_w, k_e = beyond(k1, ((levels, levels),) * 4)
    s_w, s_e = beyond(s1, ((2 * levels, levels),) * 2 + ((3 * levels, levels),) * 2)
    d_w, d_e = beyond(d1, ((TAIL, 1),) * 4)
    flux_w = jnp.where(level < jnp.minimum(d_w, d1), face(1.0, s_w, s1, t_w, t1, k_w, k1), 0.0)
    flux_e = jnp.where(level < jnp.minimum(d1, d_e), face(1.0, s1, s_e, t1, t_e, k1, k_e), 0.0)
    rise = 0.125 * ((sublanes(k1, -1) + k1) * (sublanes(t1, -1) - t1))
    rise = jnp.where((level + 1.0 < d1) & (level_i < levels - 1), rise, 0.0)
    change = outer - inward + flux_w - flux_e + rise - sublanes(rise, 1)
    p1, dp0 = jnp.where(wet1, t1 + change, 0.0), inward
    step = 1
    while step < levels:
        p1 = p1 + jnp.where(level_i >= step, sublanes(p1, step), 0.0)
        dp0 = dp0 + jnp.where(level_i >= step, sublanes(dp0, step), 0.0)
        step *= 2
    dn = 0.0125 * (side * p1) + f0 * jnp.where(wet01, n1 - n0, 0.0)
    dn = jnp.where(wet0, dn, 0.0)
    dn2 = jnp.where(level < d0b, 0.0125 * (side * dp0), 0.0)
    slope = jnp.where(lane < cols - 1, lanes(dp0, -1), 0.0) - jnp.where(lane > 0, lanes(dp0, 1), 0.0)
    ds = f0 * jnp.where(wet01, s1 - s0, 0.0) - 0.0125 * slope
    ds = jnp.where(wet0, ds, 0.0)
    ur[...] = ds[half:]
    vr0[...] = dn[half:]
    vr1[...] = dn2[half:]

    turn_columns(
        turned, (dn2[levels:half], dn[levels:half], dn[:levels], dn2[:levels], ds[levels:half], ds[:levels])
    )
    all_levels(1, 2)

    for k in range(levels):
        for n in range(3):
            copy_out(n, k).wait()


def on_device(t, u, v, kd, friction, water, strata):
    levels, rows, cols = t.shape
    lon_n, lat_n = lax.axis_size("lon"), lax.axis_size("lat")
    vmem = pl.BlockSpec(memory_space=pltpu.VMEM)
    hbm = pl.BlockSpec(memory_space=pltpu.HBM)
    params = pltpu.CompilerParams(vmem_limit_bytes=12 * 1024 * 1024)
    tall = levels * rows
    plane, message, stack = (rows, cols), (RIM, cols), (tall, cols)

    def in_hbm(*arrays):
        return [pltpu.with_memory_space_constraint(x, pltpu.HBM) for x in arrays]

    lat_a, lat_b, coriolis, drag = pl.pallas_call(
        functools.partial(rows_kernel, levels),
        out_shape=[pltpu.VMEM((RIM, 1, cols), F32)] * 2 + [pltpu.VMEM(plane, F32)] * 2,
        in_specs=[hbm] * 7,
        out_specs=[vmem] * 4,
        scratch_shapes=[pltpu.VMEM((2, 3, levels, 1, cols), F32)]
        + [pltpu.VMEM((4, 1, cols), jnp.int32)] * 2
        + [pltpu.SemaphoreType.DMA((2, 7)), pltpu.SemaphoreType.DMA((2, 2, 2)), pltpu.SemaphoreType.DMA],
        compiler_params=params,
        name="rows",
    )(
        *in_hbm(*[x.reshape(levels, rows, 1, cols) for x in (t, u, v, kd)]),
        *in_hbm(*[x.reshape(rows, 1, cols) for x in (water, strata)], friction),
    )
    lat_a, lat_b = lat_a.reshape(message), lat_b.reshape(message)
    lat_pairs = [(i, i ^ 1) for i in range(lat_n)]
    cross = []
    for m in range(lon_n):
        for i in range(1, lat_n - 1, 2):
            here, north = m * lat_n + i, m * lat_n + i + 1
            cross += [(here, north), (north, here)]
        cross.append((m * lat_n + lat_n - 1, (lon_n - 1 - m) * lat_n + lat_n - 1))
        cross.append((m * lat_n, (m ^ 1) * lat_n))
    rim_a = lax.ppermute(lat_a, "lat", lat_pairs)
    rim_b = lax.ppermute(lat_b, ("lon", "lat"), cross)

    fields = [x.reshape(stack) for x in (t, u, v, kd)]
    send_a, send_b, depth, drag_ends = pl.pallas_call(
        functools.partial(pack_kernel, levels),
        out_shape=[pltpu.VMEM(s, F32) for s in (message, message, plane, (8, cols))],
        in_specs=[vmem] * 7,
        out_specs=[vmem] * 4,
        scratch_shapes=[pltpu.VMEM((4, rows, cols), F32), pltpu.VMEM((2 * rows, cols), F32)],
        compiler_params=params,
        name="pack",
    )(*fields, water, strata, drag)
    padded, flat = pltpu.VMEM((rows + 2 * PAD, cols), F32), pltpu.VMEM(plane, F32)
    whole = pltpu.VMEM(stack, F32)
    work = [padded, padded, flat, padded]
    cost = pl.CostEstimate(flops=50 * tall * cols, bytes_accessed=1 << 20, transcendentals=0)
    *first, p_mid, up_mid, de, dw, dn, dragn = pl.pallas_call(
        functools.partial(low_kernel, levels, STRIP),
        out_shape=[whole] * 3 + [padded] + [flat] * 5,
        in_specs=[vmem] * 7,
        out_specs=[vmem] * 9,
        scratch_shapes=work,
        compiler_params=params,
        cost_estimate=cost,
        name="inner_low",
    )(*fields, depth, drag, coriolis)
    send_a, send_b = pl.pallas_call(
        functools.partial(corner_kernel, levels),
        out_shape=[pltpu.VMEM(message, F32)] * 2,
        in_specs=[vmem] * 5,
        out_specs=[vmem] * 2,
        compiler_params=params,
        name="corners",
    )(send_a, send_b, rim_b, rim_a, up_mid)
    lon_pairs = [(i, i ^ 1) for i in range(lon_n)]
    lon_cross = [(i, (i + 1) % lon_n if i % 2 else (i - 1) % lon_n) for i in range(lon_n)]
    recv_b = lax.ppermute(send_b, "lon", lon_cross)
    recv_a = lax.ppermute(send_a, "lon", lon_pairs)

    second = pl.pallas_call(
        functools.partial(high_kernel, levels, STRIP),
        out_shape=[whole] * 3,
        in_specs=[vmem] * 17,
        out_specs=[vmem] * 3,
        scratch_shapes=[padded, flat] + work,
        compiler_params=params,
        cost_estimate=cost,
        name="inner_high",
    )(*fields, depth, drag, coriolis, p_mid, up_mid, de, dw, dn, dragn, send_a, *first)

    rim_pair = pltpu.VMEM((2 * levels, cols), F32)
    outs = pl.pallas_call(
        functools.partial(border_kernel, levels),
        out_shape=[jax.ShapeDtypeStruct(stack, F32)] * 3,
        in_specs=[vmem] * 13,
        out_specs=[hbm] * 3,
        scratch_shapes=[pltpu.VMEM(stack, F32)] * 3
        + [rim_pair] * 4
        + [pltpu.VMEM(plane, F32)] * 2
        + [pltpu.SemaphoreType.DMA((3, levels))],
        compiler_params=params,
        name="border",
    )(*second, send_a, send_b, recv_a, recv_b, lat_a, lat_b, rim_a, rim_b, drag, drag_ends)
    return tuple(x.reshape(levels, rows, cols) for x in outs)


def solution(mesh):
    stack, plane = P(None, "lat", "lon"), P("lat", "lon")
    return jax.shard_map(
        on_device,
        mesh=mesh,
        in_specs=(stack,) * 4 + (plane,) * 3,
        out_specs=(stack,) * 3,
        check_vma=False,
    )
```

```python
import functools

import jax
import jax.numpy as jnp
from jax import lax
from jax.experimental import pallas as pl
from jax.experimental.pallas import tpu as pltpu
from jax.sharding import PartitionSpec as P

DT = 0.25
GRAV = 0.1
F32 = jnp.float32
PAD = 8
RIM = 88
TAIL = 80
CHUNK = 8
STRIP = 32


def lanes(x, by):
    by %= x.shape[1]
    return x if by == 0 else pltpu.roll(x, by, 1)


def sublanes(x, by):
    by %= x.shape[0]
    return x if by == 0 else pltpu.roll(x, by, 0)


def iota(shape, dim):
    return lax.broadcasted_iota(jnp.int32, shape, dim)


def parity(axis):
    return lax.axis_index(axis) % 2 == 0


def face(side, ua, ub, ta, tb, ka, kb):
    return side * (0.0625 * ((ua + ub) * (ta + tb))) - 0.125 * ((ka + kb) * (tb - ta))


def square(x):
    rows, cols = x.shape
    return jnp.concatenate([x, jnp.zeros((cols - rows, cols), F32)], 0)


def rows_kernel(
    levels, t, u, v, kd, water, strata, friction, lat_a, lat_b, coriolis, drag,
    far_rows, water_rows, strata_rows, sem, plane_sem, drag_sem,
):
    rows, cols = coriolis.shape
    copies, planes = [], []
    lat_even = parity("lat")
    for side, message in enumerate((lat_a, lat_b)):
        north = lat_even if side == 0 else jnp.logical_not(lat_even)
        near = jnp.where(north, rows - 1, 0)
        far = jnp.where(north, rows - 2, 1)
        pair = pl.ds(jnp.where(north, rows - 2, 0), 2)
        for m, (src, dst) in enumerate(((water, water_rows), (strata, strata_rows))):
            planes.append(pltpu.make_async_copy(src.at[pair], dst.at[pl.ds(2 * side, 2)], plane_sem.at[m, side]))
        for q, src in enumerate((t, kd, v, u)):
            at = message.at[pl.ds(q * levels, levels)]
            copies.append(pltpu.make_async_copy(src.at[:, near], at, sem.at[side, q]))
        for q, src in enumerate((t, kd, v)):
            copies.append(pltpu.make_async_copy(src.at[:, far], far_rows.at[side, q], sem.at[side, 4 + q]))
    whole = pltpu.make_async_copy(friction, drag, drag_sem)
    for copy in planes + copies + [whole]:
        copy.start()
    row = iota((8, rows), 1) + lax.axis_index("lat") * rows
    total = rows * lax.axis_size("lat")
    line = DT * jnp.sin(jnp.pi * ((row.astype(F32) + 0.5) / total - 0.5))
    coriolis[...] = jnp.broadcast_to(line[0:1], (cols, rows)).T
    for copy in planes:
        copy.wait()
    for side, message in enumerate((lat_a, lat_b)):
        message[pl.ds(TAIL + 2, RIM - TAIL - 2)] = jnp.zeros((RIM - TAIL - 2, 1, cols), F32)
        north = lat_even if side == 0 else jnp.logical_not(lat_even)
        first, second = (
            (water_rows[pl.ds(2 * side + n, 1)] * strata_rows[pl.ds(2 * side + n, 1)]).astype(F32) for n in range(2)
        )
        message[pl.ds(TAIL, 1)] = jnp.where(north, second, first)
        message[pl.ds(TAIL + 1, 1)] = jnp.where(north, first, second)
    whole.wait()
    drag[...] = DT * drag[...]
    for copy in copies:
        copy.wait()
    level = iota((levels, 1, cols), 0).astype(F32)
    for side, message in enumerate((lat_a, lat_b)):
        north = lat_even if side == 0 else jnp.logical_not(lat_even)
        t1, k1, v1 = (message[pl.ds(q * levels, levels)] for q in range(3))
        t2, k2, v2 = (far_rows[side, q] for q in range(3))
        wet = level < jnp.minimum(message[pl.ds(TAIL, 1)], message[pl.ds(TAIL + 1, 1)])
        flux = face(jnp.where(north, 1.0, -1.0), v2, v1, t2, t1, k2, k1)
        message[pl.ds(4 * levels, levels)] = jnp.where(wet, flux, 0.0)


def pack_kernel(
    levels, t, u, v, kd, water, strata, drag,
    send_a, send_b, depth, drag_ends, gathered, ends,
):
    rows, cols = depth.shape
    lane = iota((STRIP, cols), 1)
    edge = (lane < 2) | (lane >= cols - 2)
    for r in range(0, rows, STRIP):
        at = pl.ds(r, STRIP)
        d = (water[at, :] * strata[at, :]).astype(F32)
        depth[at, :] = d
        gathered[2, at, :] = lanes(d, 2)
        gathered[3, at, :] = lanes(drag[at, :], 2)
        gathered[0, at, :] = jnp.zeros((STRIP, cols), F32)
        gathered[1, at, :] = jnp.zeros((STRIP, cols), F32)

    @pl.loop(0, levels // CHUNK)
    def one_piece(part):
        begin = pl.multiple_of(part * CHUNK * rows, rows)
        for f, full in enumerate((t, kd, u, v)):
            for r in range(0, rows, STRIP):
                acc = gathered[f // 2, pl.ds(r, STRIP), :]
                for n in range(CHUNK):
                    x = jnp.where(edge, full[pl.ds(begin + n * rows + r, STRIP), :], 0.0)
                    to = 8 * (part * CHUNK + n) + 4 * (f % 2) + 2
                    acc = acc + pltpu.roll(x, to & (cols - 1), 1)
                gathered[f // 2, pl.ds(r, STRIP), :] = acc

    for n in range(2):
        ends[pl.ds(n * rows, rows), :] = gathered[n, :, :].T
    d = gathered[2, :, :].T
    drag_ends[...] = gathered[3, :, :].T[0:8]

    lon_even, lat_even = parity("lon"), parity("lat")

    def line_of(f, c):
        return ends[pl.ds((f // 2) * rows + 4 * (f % 2) + c, levels, stride=8), :]

    def side_of(side, near, far):
        t1, k1, u1, v1 = (line_of(f, near) for f in range(4))
        t2, k2, u2 = (line_of(f, far) for f in range(3))
        wet = iota((levels, cols), 0).astype(F32) < jnp.minimum(d[near : near + 1], d[far : far + 1])
        return t1, k1, u1, v1, jnp.where(wet, face(side, u2, u1, t2, t1, k2, k1), 0.0)

    for q, (east, west) in enumerate(zip(side_of(1.0, 1, 0), side_of(-1.0, 2, 3))):
        at = pl.ds(q * levels, levels)
        send_a[at, :] = jnp.where(lon_even, east, west)
        send_b[at, :] = jnp.where(lon_even, west, east)
    tail = (RIM - TAIL, cols)
    sub = iota(tail, 0)

    def tail_of(near, far):
        near, far = (jnp.broadcast_to(d[r : r + 1], tail) for r in (near, far))
        return jnp.where(sub == 0, near, jnp.where(sub == 1, far, 0.0))

    east, west = tail_of(1, 0), tail_of(2, 3)
    send_a[pl.ds(TAIL, RIM - TAIL), :] = jnp.where(lon_even, east, west)
    send_b[pl.ds(TAIL, RIM - TAIL), :] = jnp.where(lon_even, west, east)


def corner_kernel(levels, send_a, send_b, rim_b, rim_a, when, out_a, out_b):
    cols = send_a.shape[1]
    lon_even, lat_even = parity("lon"), parity("lat")
    a, b = rim_a[...], rim_b[...]
    b = jnp.where(lax.axis_index("lat") == 0, 0.0, b)
    south, north = square(jnp.where(lat_even, b, a)).T, square(jnp.where(lat_even, a, b)).T
    is_top = lax.axis_index("lat") == lax.axis_size("lat") - 1
    line = iota((1, cols), 1)
    turn = jnp.where((line >= 2 * levels) & (line < 4 * levels), -1.0, 1.0)
    first, last = north[0:1], north[cols - 1 : cols]
    first, last = jnp.where(is_top, turn * last, first), jnp.where(is_top, turn * first, last)
    tail = (RIM - TAIL, cols)
    sub = iota(tail, 0)
    for n, (main, out) in enumerate(((send_a, out_a), (send_b, out_b))):
        east = lon_even if n == 0 else jnp.logical_not(lon_even)
        s = jnp.broadcast_to(jnp.where(east, south[cols - 1 : cols], south[0:1]), tail)
        q = jnp.broadcast_to(jnp.where(east, last, first), tail)
        out[pl.ds(0, TAIL), :] = main[pl.ds(0, TAIL), :]
        depths = main[pl.ds(TAIL, RIM - TAIL), :]
        out[pl.ds(TAIL, RIM - TAIL), :] = jnp.where(sub == 2, s, jnp.where(sub == 3, q, depths))


def inner_kernel(
    levels, first, last, strip, t, u, v, kd, depth, drag, coriolis, p_in, up_in,
    t_out, u_out, v_out, p, up, de, dw, dn, dragn,
    fn, gu, gv, back,
):
    rows, cols = depth.shape
    zero = jnp.zeros((PAD, cols), F32)
    for ref in (fn, gu, back):
        ref[pl.ds(0, PAD), :] = zero

    shape = (strip, cols)
    lane = iota(shape, 1)
    row = iota(shape, 0)
    starts = range(0, rows, strip)
    for r in starts if p_in is None else ():
        here = pl.ds(r, strip)
        d, f = depth[here, :], drag[here, :]
        de[here, :] = jnp.where(lane < cols - 1, jnp.minimum(d, lanes(d, -1)), 0.0)
        dw[here, :] = jnp.where(lane > 0, jnp.minimum(d, lanes(d, 1)), 0.0)
        if r + strip < rows:
            north = pl.ds(r + 1, strip)
            dn[here, :] = jnp.minimum(d, depth[north, :])
            dragn[here, :] = drag[north, :]
        else:
            dn[here, :] = jnp.where(row < strip - 1, jnp.minimum(d, sublanes(d, -1)), 0.0)
            dragn[here, :] = sublanes(f, -1)

    up[...] = jnp.zeros(up.shape, F32) if p_in is None else up_in[...]
    p[...] = jnp.zeros(p.shape, F32) if p_in is None else p_in[...]

    def one_level(k):
        kf = k.astype(F32)
        base = pl.multiple_of(k * rows, rows)
        above = pl.multiple_of(jnp.minimum(k + 1, levels - 1) * rows, rows)
        for r in starts:
            here = out = pl.ds(base + r, strip)
            plane, padded, below = pl.ds(r, strip), pl.ds(PAD + r, strip), pl.ds(PAD + r - 1, strip)

            def north_of(ref, mid):
                return ref[pl.ds(base + r + 1, strip), :] if r + strip < rows else sublanes(mid, -1)

            d = depth[plane, :]
            t0, u0, v0, k0 = t[here, :], u[here, :], v[here, :], kd[here, :]
            wet, wet_e, wet_n = d > kf, de[plane, :] > kf, dn[plane, :] > kf

            t1, u1, k1 = lanes(t0, -1), lanes(u0, -1), lanes(k0, -1)
            flux = 0.0625 * ((u0 + u1) * (t0 + t1)) - 0.125 * ((k0 + k1) * (t1 - t0))
            flux = jnp.where(wet_e, flux, 0.0)
            change = lanes(flux, 1) - flux
            wet_w = dw[plane, :] > kf
            lap_u = jnp.where(wet_e, u1 - u0, 0.0) + jnp.where(wet_w, lanes(u0, 1) - u0, 0.0)
            lap_v = jnp.where(wet_e, lanes(v0, -1) - v0, 0.0) + jnp.where(wet_w, lanes(v0, 1) - v0, 0.0)

            t1, v1, k1 = north_of(t, t0), north_of(v, v0), north_of(kd, k0)
            flux = 0.0625 * ((v0 + v1) * (t0 + t1)) - 0.125 * ((k0 + k1) * (t1 - t0))
            flux = jnp.where(wet_n, flux, 0.0)
            lap = jnp.where(wet_n, north_of(u, u0) - u0, 0.0)
            lap2 = jnp.where(wet_n, v1 - v0, 0.0)
            fn[padded, :] = flux
            gu[padded, :] = lap
            gv[plane, :] = lap2
            change = change + (fn[below, :] - flux)
            lap_u = lap_u + (lap - gu[below, :])
            lap_v = lap_v + lap2

            higher = pl.ds(above + r, strip)
            rise = 0.125 * ((kd[higher, :] + k0) * (t[higher, :] - t0))
            rise = jnp.where(d > kf + 1.0, rise, 0.0)
            change = change + (rise - up[plane, :])
            up[plane, :] = rise

            t_next = jnp.where(wet, t0 + change, 0.0)
            t_out[out, :] = t_next
            p[padded, :] = p[padded, :] + t_next
            c, f = coriolis[plane, :], drag[plane, :]
            u_out[out, :] = u0 + (c * v0 + f * lap_u)
            v_out[out, :] = v0 + (f * lap_v - c * u0)

        middle = pl.ds(PAD, rows)
        back[middle, :] = 0.0125 * p[middle, :] - dragn[...] * gv[...]
        for r in starts:
            plane, out = pl.ds(r, strip), pl.ds(base + r, strip)
            wet = depth[plane, :] > kf
            mid = p[pl.ds(PAD + r, strip), :]
            slope = jnp.where(lane < cols - 1, lanes(mid, -1), 0.0) - jnp.where(lane > 0, lanes(mid, 1), 0.0)
            u_next = u_out[out, :] - 0.0125 * slope
            v_next = v_out[out, :] + back[pl.ds(PAD + r - 1, strip), :] - 0.0125 * p[pl.ds(PAD + r + 1, strip), :]
            u_out[out, :] = jnp.where(wet, u_next, 0.0)
            v_out[out, :] = jnp.where(wet, v_next, 0.0)

    @pl.loop(first, last)
    def each_level(k):
        one_level(k)


def levels_before(levels):
    lon, lat = lax.axis_index("lon"), lax.axis_index("lat")
    is_top = lat == lax.axis_size("lat") - 1
    is_last = lon == lax.axis_size("lon") - 1
    some = jnp.where(jnp.logical_not(is_top) & is_last, 0, levels // 2)
    some = jnp.where(is_top & (lon == 0), 3 * levels // 8, some)
    return jnp.where(is_top & (lon == 1), 5 * levels // 8, some)


def low_kernel(levels, strip, *refs):
    inner_kernel(levels, 0, levels_before(levels), strip, *refs[:7], None, None, *refs[7:])


def high_kernel(levels, strip, *refs):
    inputs, planes, (_, *low), outs, rest = refs[:9], refs[9:13], refs[13:17], refs[17:20], refs[20:]
    rows = refs[4].shape[0]
    split = levels_before(levels)

    @pl.loop(0, split)
    def hand_on(k):
        for src, dst in zip(low, outs):
            for r in range(0, rows, strip):
                at = pl.ds(pl.multiple_of(k * rows, rows) + r, strip)
                dst[at, :] = src[at, :]

    inner_kernel(levels, split, levels, strip, *inputs, *outs, *rest[:2], *planes, *rest[2:])


def border_kernel(
    levels, t_in, u_in, v_in,
    send_a, send_b, recv_a, recv_b, lat_a, lat_b, rim_a, rim_b, drag, drag_ends,
    t_out, u_out, v_out, tb, ub, vb, tr, ur, vr0, vr1, turned, turned_t, sem,
):
    rows, cols = drag.shape
    lon_even, lat_even = parity("lon"), parity("lat")
    is_top = lax.axis_index("lat") == lax.axis_size("lat") - 1

    def sides(even, a, b):
        a, b = a[...], b[...]
        return jnp.where(even, b, a), jnp.where(even, a, b)

    own_w, own_e = sides(lon_even, send_a, send_b)
    west, east = sides(lon_even, recv_a, recv_b)
    own_s, own_n = sides(lat_even, lat_a, lat_b)
    south, north = sides(lat_even, rim_a, rim_b)
    south = jnp.where(lax.axis_index("lat") == 0, 0.0, south)

    line = iota((RIM, 1), 0)
    turn = jnp.where((line >= 2 * levels) & (line < 4 * levels), -1.0, 1.0)
    mirrored = turn * jnp.take_along_axis(north, cols - 1 - iota((RIM, cols), 1), axis=1)
    north = jnp.where(is_top, mirrored, north)

    four, half = (4 * levels, cols), 2 * levels

    def stack(q, blocks):
        return jnp.concatenate([x[q * levels : (q + 1) * levels] for x in blocks], 0)

    def lines(rows_of_one):
        return jnp.concatenate([jnp.broadcast_to(x, (levels, cols)) for x in rows_of_one], 0)

    outside, inside = (west, east, south, north), (own_w, own_e, own_s, own_n)
    t1, k1, n1, s1, outer = (stack(q, outside) for q in range(5))
    t0, k0, n0, s0 = (stack(q, inside) for q in range(4))
    d1 = lines([x[TAIL : TAIL + 1] for x in outside])
    d0, d0b = (lines([x[TAIL + n : TAIL + n + 1] for x in inside]) for n in (0, 1))
    f0 = lines([drag_ends[2:3, :], drag_ends[1:2, :], drag[0:1, :], drag[rows - 1 : rows, :]])
    sub, lane = iota(four, 0), iota(four, 1)
    level_i = sub & (levels - 1)
    level = level_i.astype(F32)
    side = jnp.where((sub & levels) == 0, 1.0, -1.0)
    wet0, wet1 = level < d0, level < d1
    wet01 = level < jnp.minimum(d0, d1)

    inward = jnp.where(wet01, face(side, n1, n0, t1, t0, k1, k0), 0.0)

    def turn_columns(ref, lines_of):
        for g, x in enumerate(lines_of):
            ref[pl.ds(g, levels, stride=8), :] = x
        ref[...] = ref[...].T

    tail = (8, cols)
    sub8, lane8 = iota(tail, 0), iota((STRIP, cols), 1)
    one, wide = (lane8 < 1) | (lane8 >= cols - 1), (lane8 < 2) | (lane8 >= cols - 2)
    spots = ((one, cols - 1), (wide, cols - 2), (one, cols - 1 - 4))
    bufs, outs = (tb, ub, vb), (t_out, u_out, v_out)

    def copy_out(n, k):
        at = pl.ds(pl.multiple_of(k * rows, rows), rows)
        return pltpu.make_async_copy(bufs[n].at[at], outs[n].at[at], sem.at[n, k])

    def one_level(k, n, part, inside):
        base, buf = pl.multiple_of(k * rows, rows), bufs[n]
        mask, to = spots[n]
        by = (to - 8 * k) & (cols - 1)
        for r in range(0, rows, STRIP):
            moved = pltpu.roll((turned_t if n == 0 else turned)[pl.ds(r, STRIP), :], by, 1)
            old = part[pl.ds(pl.multiple_of(inside * rows, rows) + r, STRIP), :]
            buf[pl.ds(base + r, STRIP), :] = old + jnp.where(mask, moved, 0.0)

        def row_of(ref, s):
            return jnp.broadcast_to(ref[pl.ds(s * levels + k, 1), :], tail)

        for s, (near, far, begin) in enumerate(((0, 1, 0), (7, 6, rows - 8))):
            add = jnp.where(sub8 == near, row_of((tr, ur, vr0)[n], s), 0.0)
            if n == 2:
                add = jnp.where(sub8 == far, row_of(vr1, s), add)
            at = pl.ds(base + begin, 8)
            buf[at, :] = buf[at, :] + add
        copy_out(n, k).start()

    def all_levels(*which):
        @pl.loop(0, levels, step=CHUNK)
        def some_of_them(k):
            for i in range(CHUNK):
                for n in which:
                    one_level(k + i, n, (t_in, u_in, v_in)[n], k + i)

    tr[...] = inward[half:]
    turn_columns(turned_t, (inward[levels:half], inward[:levels]))
    all_levels(0)

    low, high = TAIL + 2, TAIL + 3
    ends_w, ends_e = square(west).T, square(east).T
    sw, nw = (ends_w[:, n : n + 1] for n in (low, high))
    se, ne = (ends_e[:, n : n + 1] for n in (low, high))
    before, after = (sw, se, sw, nw), (nw, ne, se, ne)

    def beyond(x, at):
        lo, hi = (
            jnp.concatenate(
                [jnp.broadcast_to(c[n : n + m], (levels, 1)) for c, (n, m) in zip(cells, at)], 0
            )
            for cells in (before, after)
        )
        lo, hi = jnp.broadcast_to(lo, four), jnp.broadcast_to(hi, four)
        return jnp.where(lane == 0, lo, lanes(x, 1)), jnp.where(lane == cols - 1, hi, lanes(x, -1))

    t_w, t_e = beyond(t1, ((0, levels),) * 4)
    k_w, k_e = beyond(k1, ((levels, levels),) * 4)
    s_w, s_e = beyond(s1, ((2 * levels, levels),) * 2 + ((3 * levels, levels),) * 2)
    d_w, d_e = beyond(d1, ((TAIL, 1),) * 4)
    flux_w = jnp.where(level < jnp.minimum(d_w, d1), face(1.0, s_w, s1, t_w, t1, k_w, k1), 0.0)
    flux_e = jnp.where(level < jnp.minimum(d1, d_e), face(1.0, s1, s_e, t1, t_e, k1, k_e), 0.0)
    rise = 0.125 * ((sublanes(k1, -1) + k1) * (sublanes(t1, -1) - t1))
    rise = jnp.where((level + 1.0 < d1) & (level_i < levels - 1), rise, 0.0)
    change = outer - inward + flux_w - flux_e + rise - sublanes(rise, 1)
    p1, dp0 = jnp.where(wet1, t1 + change, 0.0), inward
    step = 1
    while step < levels:
        p1 = p1 + jnp.where(level_i >= step, sublanes(p1, step), 0.0)
        dp0 = dp0 + jnp.where(level_i >= step, sublanes(dp0, step), 0.0)
        step *= 2
    dn = 0.0125 * (side * p1) + f0 * jnp.where(wet01, n1 - n0, 0.0)
    dn = jnp.where(wet0, dn, 0.0)
    dn2 = jnp.where(level < d0b, 0.0125 * (side * dp0), 0.0)
    slope = jnp.where(lane < cols - 1, lanes(dp0, -1), 0.0) - jnp.where(lane > 0, lanes(dp0, 1), 0.0)
    ds = f0 * jnp.where(wet01, s1 - s0, 0.0) - 0.0125 * slope
    ds = jnp.where(wet0, ds, 0.0)
    ur[...] = ds[half:]
    vr0[...] = dn[half:]
    vr1[...] = dn2[half:]

    turn_columns(
        turned, (dn2[levels:half], dn[levels:half], dn[:levels], dn2[:levels], ds[levels:half], ds[:levels])
    )
    all_levels(1, 2)

    @pl.loop(0, levels)
    def finish(k):
        for n in range(3):
            copy_out(n, k).wait()


def on_device(t, u, v, kd, friction, water, strata):
    levels, rows, cols = t.shape
    lon_n, lat_n = lax.axis_size("lon"), lax.axis_size("lat")
    vmem = pl.BlockSpec(memory_space=pltpu.VMEM)
    hbm = pl.BlockSpec(memory_space=pltpu.HBM)
    params = pltpu.CompilerParams(vmem_limit_bytes=12 * 1024 * 1024)
    tall = levels * rows
    plane, message, stack = (rows, cols), (RIM, cols), (tall, cols)

    def in_hbm(*arrays):
        return [pltpu.with_memory_space_constraint(x, pltpu.HBM) for x in arrays]

    lat_a, lat_b, coriolis, drag = pl.pallas_call(
        functools.partial(rows_kernel, levels),
        out_shape=[pltpu.VMEM((RIM, 1, cols), F32)] * 2 + [pltpu.VMEM(plane, F32)] * 2,
        in_specs=[hbm] * 7,
        out_specs=[vmem] * 4,
        scratch_shapes=[pltpu.VMEM((2, 3, levels, 1, cols), F32)]
        + [pltpu.VMEM((4, 1, cols), jnp.int32)] * 2
        + [pltpu.SemaphoreType.DMA((2, 7)), pltpu.SemaphoreType.DMA((2, 2)), pltpu.SemaphoreType.DMA],
        compiler_params=params,
        name="rows",
    )(
        *in_hbm(*[x.reshape(levels, rows, 1, cols) for x in (t, u, v, kd)]),
        *in_hbm(*[x.reshape(rows, 1, cols) for x in (water, strata)], friction),
    )
    lat_a, lat_b = lat_a.reshape(message), lat_b.reshape(message)
    lat_pairs = [(i, i ^ 1) for i in range(lat_n)]
    cross = []
    for m in range(lon_n):
        for i in range(1, lat_n - 1, 2):
            here, north = m * lat_n + i, m * lat_n + i + 1
            cross += [(here, north), (north, here)]
        cross.append((m * lat_n + lat_n - 1, (lon_n - 1 - m) * lat_n + lat_n - 1))
        cross.append((m * lat_n, (m ^ 1) * lat_n))
    rim_a = lax.ppermute(lat_a, "lat", lat_pairs)
    rim_b = lax.ppermute(lat_b, ("lon", "lat"), cross)

    fields = [x.reshape(stack) for x in (t, u, v, kd)]
    send_a, send_b, depth, drag_ends = pl.pallas_call(
        functools.partial(pack_kernel, levels),
        out_shape=[pltpu.VMEM(s, F32) for s in (message, message, plane, (8, cols))],
        in_specs=[vmem] * 7,
        out_specs=[vmem] * 4,
        scratch_shapes=[pltpu.VMEM((4, rows, cols), F32), pltpu.VMEM((2 * rows, cols), F32)],
        compiler_params=params,
        name="pack",
    )(*fields, water, strata, drag)
    padded, flat = pltpu.VMEM((rows + 2 * PAD, cols), F32), pltpu.VMEM(plane, F32)
    whole = pltpu.VMEM(stack, F32)
    work = [padded, padded, flat, padded]
    cost = pl.CostEstimate(flops=50 * tall * cols, bytes_accessed=1 << 20, transcendentals=0)
    *first, p_mid, up_mid, de, dw, dn, dragn = pl.pallas_call(
        functools.partial(low_kernel, levels, STRIP),
        out_shape=[whole] * 3 + [padded] + [flat] * 5,
        in_specs=[vmem] * 7,
        out_specs=[vmem] * 9,
        scratch_shapes=work,
        compiler_params=params,
        cost_estimate=cost,
        name="inner_low",
    )(*fields, depth, drag, coriolis)
    send_a, send_b = pl.pallas_call(
        functools.partial(corner_kernel, levels),
        out_shape=[pltpu.VMEM(message, F32)] * 2,
        in_specs=[vmem] * 5,
        out_specs=[vmem] * 2,
        compiler_params=params,
        name="corners",
    )(send_a, send_b, rim_b, rim_a, up_mid)
    lon_pairs = [(i, i ^ 1) for i in range(lon_n)]
    lon_cross = [(i, (i + 1) % lon_n if i % 2 else (i - 1) % lon_n) for i in range(lon_n)]
    recv_b = lax.ppermute(send_b, "lon", lon_cross)
    recv_a = lax.ppermute(send_a, "lon", lon_pairs)

    second = pl.pallas_call(
        functools.partial(high_kernel, levels, STRIP),
        out_shape=[whole] * 3,
        in_specs=[vmem] * 17,
        out_specs=[vmem] * 3,
        scratch_shapes=[padded, flat] + work,
        compiler_params=params,
        cost_estimate=cost,
        name="inner_high",
    )(*fields, depth, drag, coriolis, p_mid, up_mid, de, dw, dn, dragn, send_a, *first)

    rim_pair = pltpu.VMEM((2 * levels, cols), F32)
    outs = pl.pallas_call(
        functools.partial(border_kernel, levels),
        out_shape=[jax.ShapeDtypeStruct(stack, F32)] * 3,
        in_specs=[vmem] * 13,
        out_specs=[hbm] * 3,
        scratch_shapes=[pltpu.VMEM(stack, F32)] * 3
        + [rim_pair] * 4
        + [pltpu.VMEM(plane, F32)] * 2
        + [pltpu.SemaphoreType.DMA((3, levels))],
        compiler_params=params,
        name="border",
    )(*second, send_a, send_b, recv_a, recv_b, lat_a, lat_b, rim_a, rim_b, drag, drag_ends)
    return tuple(x.reshape(levels, rows, cols) for x in outs)


def solution(mesh):
    stack, plane = P(None, "lat", "lon"), P("lat", "lon")
    return jax.shard_map(
        on_device,
        mesh=mesh,
        in_specs=(stack,) * 4 + (plane,) * 3,
        out_specs=(stack,) * 3,
        check_vma=False,
    )
```

```python
import functools

import jax
import jax.numpy as jnp
from jax import lax
from jax.experimental import pallas as pl
from jax.experimental.pallas import tpu as pltpu
from jax.sharding import PartitionSpec as P

DT = 0.25
GRAV = 0.1
F32 = jnp.float32
PAD = 8
RIM = 88
TAIL = 80
CHUNK = 8
STRIP = 32


def lanes(x, by):
    by %= x.shape[1]
    return x if by == 0 else pltpu.roll(x, by, 1)


def sublanes(x, by):
    by %= x.shape[0]
    return x if by == 0 else pltpu.roll(x, by, 0)


def iota(shape, dim):
    return lax.broadcasted_iota(jnp.int32, shape, dim)


def parity(axis):
    return lax.axis_index(axis) % 2 == 0


def face(side, ua, ub, ta, tb, ka, kb):
    return side * (0.0625 * ((ua + ub) * (ta + tb))) - 0.125 * ((ka + kb) * (tb - ta))


def square(x):
    rows, cols = x.shape
    return jnp.concatenate([x, jnp.zeros((cols - rows, cols), F32)], 0)


def rows_kernel(
    levels, t, u, v, kd, water, strata, friction, lat_a, lat_b, coriolis, drag,
    far_rows, water_rows, strata_rows, sem, plane_sem, drag_sem,
):
    rows, cols = coriolis.shape
    copies, planes = [], []
    lat_even = parity("lat")
    for side, message in enumerate((lat_a, lat_b)):
        north = lat_even if side == 0 else jnp.logical_not(lat_even)
        near = jnp.where(north, rows - 1, 0)
        far = jnp.where(north, rows - 2, 1)
        pair = pl.ds(jnp.where(north, rows - 2, 0), 2)
        for m, (src, dst) in enumerate(((water, water_rows), (strata, strata_rows))):
            planes.append(pltpu.make_async_copy(src.at[pair], dst.at[pl.ds(2 * side, 2)], plane_sem.at[m, side]))
        for q, src in enumerate((t, kd, v, u)):
            at = message.at[pl.ds(q * levels, levels)]
            copies.append(pltpu.make_async_copy(src.at[:, near], at, sem.at[side, q]))
        for q, src in enumerate((t, kd, v)):
            copies.append(pltpu.make_async_copy(src.at[:, far], far_rows.at[side, q], sem.at[side, 4 + q]))
    whole = pltpu.make_async_copy(friction, drag, drag_sem)
    for copy in planes + copies + [whole]:
        copy.start()
    row = iota((8, rows), 1) + lax.axis_index("lat") * rows
    total = rows * lax.axis_size("lat")
    line = DT * jnp.sin(jnp.pi * ((row.astype(F32) + 0.5) / total - 0.5))
    coriolis[...] = jnp.broadcast_to(line[0:1], (cols, rows)).T
    for copy in planes:
        copy.wait()
    for side, message in enumerate((lat_a, lat_b)):
        message[pl.ds(TAIL + 2, RIM - TAIL - 2)] = jnp.zeros((RIM - TAIL - 2, 1, cols), F32)
        north = lat_even if side == 0 else jnp.logical_not(lat_even)
        first, second = (
            (water_rows[pl.ds(2 * side + n, 1)] * strata_rows[pl.ds(2 * side + n, 1)]).astype(F32) for n in range(2)
        )
        message[pl.ds(TAIL, 1)] = jnp.where(north, second, first)
        message[pl.ds(TAIL + 1, 1)] = jnp.where(north, first, second)
    whole.wait()
    drag[...] = DT * drag[...]
    for copy in copies:
        copy.wait()
    level = iota((levels, 1, cols), 0).astype(F32)
    for side, message in enumerate((lat_a, lat_b)):
        north = lat_even if side == 0 else jnp.logical_not(lat_even)
        t1, k1, v1 = (message[pl.ds(q * levels, levels)] for q in range(3))
        t2, k2, v2 = (far_rows[side, q] for q in range(3))
        wet = level < jnp.minimum(message[pl.ds(TAIL, 1)], message[pl.ds(TAIL + 1, 1)])
        flux = face(jnp.where(north, 1.0, -1.0), v2, v1, t2, t1, k2, k1)
        message[pl.ds(4 * levels, levels)] = jnp.where(wet, flux, 0.0)


def pack_kernel(
    levels, t, u, v, kd, water, strata, drag,
    send_a, send_b, depth, drag_ends, gathered, ends,
):
    rows, cols = depth.shape
    lane = iota((STRIP, cols), 1)
    edge = (lane < 2) | (lane >= cols - 2)
    for r in range(0, rows, STRIP):
        at = pl.ds(r, STRIP)
        d = (water[at, :] * strata[at, :]).astype(F32)
        depth[at, :] = d
        gathered[2, at, :] = lanes(d, 2)
        gathered[3, at, :] = lanes(drag[at, :], 2)
        gathered[0, at, :] = jnp.zeros((STRIP, cols), F32)
        gathered[1, at, :] = jnp.zeros((STRIP, cols), F32)

    @pl.loop(0, levels // CHUNK)
    def one_piece(part):
        begin = pl.multiple_of(part * CHUNK * rows, rows)
        for f, full in enumerate((t, kd, u, v)):
            for r in range(0, rows, STRIP):
                acc = gathered[f // 2, pl.ds(r, STRIP), :]
                for n in range(CHUNK):
                    x = jnp.where(edge, full[pl.ds(begin + n * rows + r, STRIP), :], 0.0)
                    to = 8 * (part * CHUNK + n) + 4 * (f % 2) + 2
                    acc = acc + pltpu.roll(x, to & (cols - 1), 1)
                gathered[f // 2, pl.ds(r, STRIP), :] = acc

    for n in range(2):
        ends[pl.ds(n * rows, rows), :] = gathered[n, :, :].T
    d = gathered[2, :, :].T
    drag_ends[...] = gathered[3, :, :].T[0:8]

    lon_even, lat_even = parity("lon"), parity("lat")

    def line_of(f, c):
        return ends[pl.ds((f // 2) * rows + 4 * (f % 2) + c, levels, stride=8), :]

    def side_of(side, near, far):
        t1, k1, u1, v1 = (line_of(f, near) for f in range(4))
        t2, k2, u2 = (line_of(f, far) for f in range(3))
        wet = iota((levels, cols), 0).astype(F32) < jnp.minimum(d[near : near + 1], d[far : far + 1])
        return t1, k1, u1, v1, jnp.where(wet, face(side, u2, u1, t2, t1, k2, k1), 0.0)

    for q, (east, west) in enumerate(zip(side_of(1.0, 1, 0), side_of(-1.0, 2, 3))):
        at = pl.ds(q * levels, levels)
        send_a[at, :] = jnp.where(lon_even, east, west)
        send_b[at, :] = jnp.where(lon_even, west, east)
    tail = (RIM - TAIL, cols)
    sub = iota(tail, 0)

    def tail_of(near, far):
        near, far = (jnp.broadcast_to(d[r : r + 1], tail) for r in (near, far))
        return jnp.where(sub == 0, near, jnp.where(sub == 1, far, 0.0))

    east, west = tail_of(1, 0), tail_of(2, 3)
    send_a[pl.ds(TAIL, RIM - TAIL), :] = jnp.where(lon_even, east, west)
    send_b[pl.ds(TAIL, RIM - TAIL), :] = jnp.where(lon_even, west, east)


def corner_kernel(levels, send_a, send_b, rim_b, rim_a, when, out_a, out_b):
    cols = send_a.shape[1]
    lon_even, lat_even = parity("lon"), parity("lat")
    a, b = rim_a[...], rim_b[...]
    b = jnp.where(lax.axis_index("lat") == 0, 0.0, b)
    south, north = square(jnp.where(lat_even, b, a)).T, square(jnp.where(lat_even, a, b)).T
    is_top = lax.axis_index("lat") == lax.axis_size("lat") - 1
    line = iota((1, cols), 1)
    turn = jnp.where((line >= 2 * levels) & (line < 4 * levels), -1.0, 1.0)
    first, last = north[0:1], north[cols - 1 : cols]
    first, last = jnp.where(is_top, turn * last, first), jnp.where(is_top, turn * first, last)
    tail = (RIM - TAIL, cols)
    sub = iota(tail, 0)
    for n, (main, out) in enumerate(((send_a, out_a), (send_b, out_b))):
        east = lon_even if n == 0 else jnp.logical_not(lon_even)
        s = jnp.broadcast_to(jnp.where(east, south[cols - 1 : cols], south[0:1]), tail)
        q = jnp.broadcast_to(jnp.where(east, last, first), tail)
        out[pl.ds(0, TAIL), :] = main[pl.ds(0, TAIL), :]
        depths = main[pl.ds(TAIL, RIM - TAIL), :]
        out[pl.ds(TAIL, RIM - TAIL), :] = jnp.where(sub == 2, s, jnp.where(sub == 3, q, depths))


def inner_kernel(
    levels, first, last, strip, t, u, v, kd, depth, drag, coriolis, p_in, up_in,
    t_out, u_out, v_out, p, up, de, dw, dn, dragn,
    fn, gu, gv, back,
):
    rows, cols = depth.shape
    zero = jnp.zeros((PAD, cols), F32)
    for ref in (fn, gu, back):
        ref[pl.ds(0, PAD), :] = zero

    shape = (strip, cols)
    lane = iota(shape, 1)
    row = iota(shape, 0)
    starts = range(0, rows, strip)
    for r in starts if p_in is None else ():
        here = pl.ds(r, strip)
        d, f = depth[here, :], drag[here, :]
        de[here, :] = jnp.where(lane < cols - 1, jnp.minimum(d, lanes(d, -1)), 0.0)
        dw[here, :] = jnp.where(lane > 0, jnp.minimum(d, lanes(d, 1)), 0.0)
        if r + strip < rows:
            north = pl.ds(r + 1, strip)
            dn[here, :] = jnp.minimum(d, depth[north, :])
            dragn[here, :] = drag[north, :]
        else:
            dn[here, :] = jnp.where(row < strip - 1, jnp.minimum(d, sublanes(d, -1)), 0.0)
            dragn[here, :] = sublanes(f, -1)

    up[...] = jnp.zeros(up.shape, F32) if p_in is None else up_in[...]
    p[...] = jnp.zeros(p.shape, F32) if p_in is None else p_in[...]

    def one_level(k):
        kf = k.astype(F32)
        base = pl.multiple_of(k * rows, rows)
        above = pl.multiple_of(jnp.minimum(k + 1, levels - 1) * rows, rows)
        for r in starts:
            here = out = pl.ds(base + r, strip)
            plane, padded, below = pl.ds(r, strip), pl.ds(PAD + r, strip), pl.ds(PAD + r - 1, strip)

            def north_of(ref, mid):
                return ref[pl.ds(base + r + 1, strip), :] if r + strip < rows else sublanes(mid, -1)

            d = depth[plane, :]
            t0, u0, v0, k0 = t[here, :], u[here, :], v[here, :], kd[here, :]
            wet, wet_e, wet_n = d > kf, de[plane, :] > kf, dn[plane, :] > kf

            t1, u1, k1 = lanes(t0, -1), lanes(u0, -1), lanes(k0, -1)
            flux = 0.0625 * ((u0 + u1) * (t0 + t1)) - 0.125 * ((k0 + k1) * (t1 - t0))
            flux = jnp.where(wet_e, flux, 0.0)
            change = lanes(flux, 1) - flux
            wet_w = dw[plane, :] > kf
            lap_u = jnp.where(wet_e, u1 - u0, 0.0) + jnp.where(wet_w, lanes(u0, 1) - u0, 0.0)
            lap_v = jnp.where(wet_e, lanes(v0, -1) - v0, 0.0) + jnp.where(wet_w, lanes(v0, 1) - v0, 0.0)

            t1, v1, k1 = north_of(t, t0), north_of(v, v0), north_of(kd, k0)
            flux = 0.0625 * ((v0 + v1) * (t0 + t1)) - 0.125 * ((k0 + k1) * (t1 - t0))
            flux = jnp.where(wet_n, flux, 0.0)
            lap = jnp.where(wet_n, north_of(u, u0) - u0, 0.0)
            lap2 = jnp.where(wet_n, v1 - v0, 0.0)
            fn[padded, :] = flux
            gu[padded, :] = lap
            gv[plane, :] = lap2
            change = change + (fn[below, :] - flux)
            lap_u = lap_u + (lap - gu[below, :])
            lap_v = lap_v + lap2

            higher = pl.ds(above + r, strip)
            rise = 0.125 * ((kd[higher, :] + k0) * (t[higher, :] - t0))
            rise = jnp.where(d > kf + 1.0, rise, 0.0)
            change = change + (rise - up[plane, :])
            up[plane, :] = rise

            t_next = jnp.where(wet, t0 + change, 0.0)
            t_out[out, :] = t_next
            p[padded, :] = p[padded, :] + t_next
            c, f = coriolis[plane, :], drag[plane, :]
            u_out[out, :] = u0 + (c * v0 + f * lap_u)
            v_out[out, :] = v0 + (f * lap_v - c * u0)

        middle = pl.ds(PAD, rows)
        back[middle, :] = 0.0125 * p[middle, :] - dragn[...] * gv[...]
        for r in starts:
            plane, out = pl.ds(r, strip), pl.ds(base + r, strip)
            wet = depth[plane, :] > kf
            mid = p[pl.ds(PAD + r, strip), :]
            slope = jnp.where(lane < cols - 1, lanes(mid, -1), 0.0) - jnp.where(lane > 0, lanes(mid, 1), 0.0)
            u_next = u_out[out, :] - 0.0125 * slope
            v_next = v_out[out, :] + back[pl.ds(PAD + r - 1, strip), :] - 0.0125 * p[pl.ds(PAD + r + 1, strip), :]
            u_out[out, :] = jnp.where(wet, u_next, 0.0)
            v_out[out, :] = jnp.where(wet, v_next, 0.0)

    @pl.loop(first, last)
    def each_level(k):
        one_level(k)


def levels_before(levels):
    lon, lat = lax.axis_index("lon"), lax.axis_index("lat")
    is_top = lat == lax.axis_size("lat") - 1
    is_last = lon == lax.axis_size("lon") - 1
    some = jnp.where(jnp.logical_not(is_top) & is_last, 0, levels // 2)
    some = jnp.where(is_top & (lon == 0), 3 * levels // 8, some)
    return jnp.where(is_top & (lon == 1), 5 * levels // 8, some)


def low_kernel(levels, strip, *refs):
    inner_kernel(levels, 0, levels_before(levels), strip, *refs[:7], None, None, *refs[7:])


def high_kernel(levels, strip, *refs):
    inputs, planes, (_, *low), outs, rest = refs[:9], refs[9:13], refs[13:17], refs[17:20], refs[20:]
    rows = refs[4].shape[0]
    split = levels_before(levels)

    @pl.loop(0, split)
    def hand_on(k):
        for src, dst in zip(low, outs):
            for r in range(0, rows, strip):
                at = pl.ds(pl.multiple_of(k * rows, rows) + r, strip)
                dst[at, :] = src[at, :]

    inner_kernel(levels, split, levels, strip, *inputs, *outs, *rest[:2], *planes, *rest[2:])


def border_kernel(
    levels, t_in, u_in, v_in,
    send_a, send_b, recv_a, recv_b, lat_a, lat_b, rim_a, rim_b, drag, drag_ends,
    t_out, u_out, v_out, tb, ub, vb, tr, ur, vr0, vr1, turned, turned_t, sem,
):
    rows, cols = drag.shape
    lon_even, lat_even = parity("lon"), parity("lat")
    is_top = lax.axis_index("lat") == lax.axis_size("lat") - 1

    def sides(even, a, b):
        a, b = a[...], b[...]
        return jnp.where(even, b, a), jnp.where(even, a, b)

    own_w, own_e = sides(lon_even, send_a, send_b)
    west, east = sides(lon_even, recv_a, recv_b)
    own_s, own_n = sides(lat_even, lat_a, lat_b)
    south, north = sides(lat_even, rim_a, rim_b)
    south = jnp.where(lax.axis_index("lat") == 0, 0.0, south)

    line = iota((RIM, 1), 0)
    turn = jnp.where((line >= 2 * levels) & (line < 4 * levels), -1.0, 1.0)
    mirrored = turn * jnp.take_along_axis(north, cols - 1 - iota((RIM, cols), 1), axis=1)
    north = jnp.where(is_top, mirrored, north)

    four, half = (4 * levels, cols), 2 * levels

    def stack(q, blocks):
        return jnp.concatenate([x[q * levels : (q + 1) * levels] for x in blocks], 0)

    def lines(rows_of_one):
        return jnp.concatenate([jnp.broadcast_to(x, (levels, cols)) for x in rows_of_one], 0)

    outside, inside = (west, east, south, north), (own_w, own_e, own_s, own_n)
    t1, k1, n1, s1, outer = (stack(q, outside) for q in range(5))
    t0, k0, n0, s0 = (stack(q, inside) for q in range(4))
    d1 = lines([x[TAIL : TAIL + 1] for x in outside])
    d0, d0b = (lines([x[TAIL + n : TAIL + n + 1] for x in inside]) for n in (0, 1))
    f0 = lines([drag_ends[2:3, :], drag_ends[1:2, :], drag[0:1, :], drag[rows - 1 : rows, :]])
    sub, lane = iota(four, 0), iota(four, 1)
    level_i = sub & (levels - 1)
    level = level_i.astype(F32)
    side = jnp.where((sub & levels) == 0, 1.0, -1.0)
    wet0, wet1 = level < d0, level < d1
    wet01 = level < jnp.minimum(d0, d1)

    inward = jnp.where(wet01, face(side, n1, n0, t1, t0, k1, k0), 0.0)

    def turn_columns(ref, lines_of):
        for g, x in enumerate(lines_of):
            ref[pl.ds(g, levels, stride=8), :] = x
        ref[...] = ref[...].T

    tail = (8, cols)
    sub8, lane8 = iota(tail, 0), iota((STRIP, cols), 1)
    one, wide = (lane8 < 1) | (lane8 >= cols - 1), (lane8 < 2) | (lane8 >= cols - 2)
    spots = ((one, cols - 1), (wide, cols - 2), (one, cols - 1 - 4))
    bufs, outs = (tb, ub, vb), (t_out, u_out, v_out)

    def copy_out(n, k):
        at = pl.ds(pl.multiple_of(k * rows, rows), rows)
        return pltpu.make_async_copy(bufs[n].at[at], outs[n].at[at], sem.at[n, k])

    def one_level(k, n, part, inside):
        base, buf = pl.multiple_of(k * rows, rows), bufs[n]
        mask, to = spots[n]
        by = (to - 8 * k) & (cols - 1)
        for r in range(0, rows, STRIP):
            moved = pltpu.roll((turned_t if n == 0 else turned)[pl.ds(r, STRIP), :], by, 1)
            old = part[pl.ds(pl.multiple_of(inside * rows, rows) + r, STRIP), :]
            buf[pl.ds(base + r, STRIP), :] = old + jnp.where(mask, moved, 0.0)

        def row_of(ref, s):
            return jnp.broadcast_to(ref[pl.ds(s * levels + k, 1), :], tail)

        for s, (near, far, begin) in enumerate(((0, 1, 0), (7, 6, rows - 8))):
            add = jnp.where(sub8 == near, row_of((tr, ur, vr0)[n], s), 0.0)
            if n == 2:
                add = jnp.where(sub8 == far, row_of(vr1, s), add)
            at = pl.ds(base + begin, 8)
            buf[at, :] = buf[at, :] + add
        copy_out(n, k).start()

    def all_levels(*which):
        @pl.loop(0, levels, step=CHUNK)
        def some_of_them(k):
            for i in range(CHUNK):
                for n in which:
                    one_level(k + i, n, (t_in, u_in, v_in)[n], k + i)

    tr[...] = inward[half:]
    turn_columns(turned_t, (inward[levels:half], inward[:levels]))
    all_levels(0)

    low, high = TAIL + 2, TAIL + 3
    ends_w, ends_e = square(west).T, square(east).T
    sw, nw = (ends_w[:, n : n + 1] for n in (low, high))
    se, ne = (ends_e[:, n : n + 1] for n in (low, high))
    before, after = (sw, se, sw, nw), (nw, ne, se, ne)

    def beyond(x, at):
        lo, hi = (
            jnp.concatenate(
                [jnp.broadcast_to(c[n : n + m], (levels, 1)) for c, (n, m) in zip(cells, at)], 0
            )
            for cells in (before, after)
        )
        lo, hi = jnp.broadcast_to(lo, four), jnp.broadcast_to(hi, four)
        return jnp.where(lane == 0, lo, lanes(x, 1)), jnp.where(lane == cols - 1, hi, lanes(x, -1))

    t_w, t_e = beyond(t1, ((0, levels),) * 4)
    k_w, k_e = beyond(k1, ((levels, levels),) * 4)
    s_w, s_e = beyond(s1, ((2 * levels, levels),) * 2 + ((3 * levels, levels),) * 2)
    d_w, d_e = beyond(d1, ((TAIL, 1),) * 4)
    flux_w = jnp.where(level < jnp.minimum(d_w, d1), face(1.0, s_w, s1, t_w, t1, k_w, k1), 0.0)
    flux_e = jnp.where(level < jnp.minimum(d1, d_e), face(1.0, s1, s_e, t1, t_e, k1, k_e), 0.0)
    rise = 0.125 * ((sublanes(k1, -1) + k1) * (sublanes(t1, -1) - t1))
    rise = jnp.where((level + 1.0 < d1) & (level_i < levels - 1), rise, 0.0)
    change = outer - inward + flux_w - flux_e + rise - sublanes(rise, 1)
    p1, dp0 = jnp.where(wet1, t1 + change, 0.0), inward
    step = 1
    while step < levels:
        p1 = p1 + jnp.where(level_i >= step, sublanes(p1, step), 0.0)
        dp0 = dp0 + jnp.where(level_i >= step, sublanes(dp0, step), 0.0)
        step *= 2
    dn = 0.0125 * (side * p1) + f0 * jnp.where(wet01, n1 - n0, 0.0)
    dn = jnp.where(wet0, dn, 0.0)
    dn2 = jnp.where(level < d0b, 0.0125 * (side * dp0), 0.0)
    slope = jnp.where(lane < cols - 1, lanes(dp0, -1), 0.0) - jnp.where(lane > 0, lanes(dp0, 1), 0.0)
    ds = f0 * jnp.where(wet01, s1 - s0, 0.0) - 0.0125 * slope
    ds = jnp.where(wet0, ds, 0.0)
    ur[...] = ds[half:]
    vr0[...] = dn[half:]
    vr1[...] = dn2[half:]

    turn_columns(
        turned, (dn2[levels:half], dn[levels:half], dn[:levels], dn2[:levels], ds[levels:half], ds[:levels])
    )
    all_levels(1, 2)

    @pl.loop(0, levels)
    def finish(k):
        for n in range(3):
            copy_out(n, k).wait()


def on_device(t, u, v, kd, friction, water, strata):
    levels, rows, cols = t.shape
    lon_n, lat_n = lax.axis_size("lon"), lax.axis_size("lat")
    vmem = pl.BlockSpec(memory_space=pltpu.VMEM)
    hbm = pl.BlockSpec(memory_space=pltpu.HBM)
    params = pltpu.CompilerParams(vmem_limit_bytes=12 * 1024 * 1024)
    tall = levels * rows
    plane, message, stack = (rows, cols), (RIM, cols), (tall, cols)

    def in_hbm(*arrays):
        return [pltpu.with_memory_space_constraint(x, pltpu.HBM) for x in arrays]

    lat_a, lat_b, coriolis, drag = pl.pallas_call(
        functools.partial(rows_kernel, levels),
        out_shape=[pltpu.VMEM((RIM, 1, cols), F32)] * 2 + [pltpu.VMEM(plane, F32)] * 2,
        in_specs=[hbm] * 7,
        out_specs=[vmem] * 4,
        scratch_shapes=[pltpu.VMEM((2, 3, levels, 1, cols), F32)]
        + [pltpu.VMEM((4, 1, cols), jnp.int32)] * 2
        + [pltpu.SemaphoreType.DMA((2, 7)), pltpu.SemaphoreType.DMA((2, 2)), pltpu.SemaphoreType.DMA],
        compiler_params=params,
        name="rows",
    )(
        *in_hbm(*[x.reshape(levels, rows, 1, cols) for x in (t, u, v, kd)]),
        *in_hbm(*[x.reshape(rows, 1, cols) for x in (water, strata)], friction),
    )
    lat_a, lat_b = lat_a.reshape(message), lat_b.reshape(message)
    lat_pairs = [(i, i ^ 1) for i in range(lat_n)]
    cross = []
    for m in range(lon_n):
        for i in range(1, lat_n - 1, 2):
            here, north = m * lat_n + i, m * lat_n + i + 1
            cross += [(here, north), (north, here)]
        cross.append((m * lat_n + lat_n - 1, (lon_n - 1 - m) * lat_n + lat_n - 1))
        cross.append((m * lat_n, (m ^ 1) * lat_n))
    rim_a = lax.ppermute(lat_a, "lat", lat_pairs)
    rim_b = lax.ppermute(lat_b, ("lon", "lat"), cross)

    fields = [x.reshape(stack) for x in (t, u, v, kd)]
    send_a, send_b, depth, drag_ends = pl.pallas_call(
        functools.partial(pack_kernel, levels),
        out_shape=[pltpu.VMEM(s, F32) for s in (message, message, plane, (8, cols))],
        in_specs=[vmem] * 7,
        out_specs=[vmem] * 4,
        scratch_shapes=[pltpu.VMEM((4, rows, cols), F32), pltpu.VMEM((2 * rows, cols), F32)],
        compiler_params=params,
        name="pack",
    )(*fields, water, strata, drag)
    padded, flat = pltpu.VMEM((rows + 2 * PAD, cols), F32), pltpu.VMEM(plane, F32)
    whole = pltpu.VMEM(stack, F32)
    work = [padded, padded, flat, padded]
    cost = pl.CostEstimate(flops=50 * tall * cols, bytes_accessed=1 << 20, transcendentals=0)
    *first, p_mid, up_mid, de, dw, dn, dragn = pl.pallas_call(
        functools.partial(low_kernel, levels, STRIP // 2),
        out_shape=[whole] * 3 + [padded] + [flat] * 5,
        in_specs=[vmem] * 7,
        out_specs=[vmem] * 9,
        scratch_shapes=work,
        compiler_params=params,
        cost_estimate=cost,
        name="inner_low",
    )(*fields, depth, drag, coriolis)
    send_a, send_b = pl.pallas_call(
        functools.partial(corner_kernel, levels),
        out_shape=[pltpu.VMEM(message, F32)] * 2,
        in_specs=[vmem] * 5,
        out_specs=[vmem] * 2,
        compiler_params=params,
        name="corners",
    )(send_a, send_b, rim_b, rim_a, up_mid)
    lon_pairs = [(i, i ^ 1) for i in range(lon_n)]
    lon_cross = [(i, (i + 1) % lon_n if i % 2 else (i - 1) % lon_n) for i in range(lon_n)]
    recv_b = lax.ppermute(send_b, "lon", lon_cross)
    recv_a = lax.ppermute(send_a, "lon", lon_pairs)

    second = pl.pallas_call(
        functools.partial(high_kernel, levels, STRIP // 2),
        out_shape=[whole] * 3,
        in_specs=[vmem] * 17,
        out_specs=[vmem] * 3,
        scratch_shapes=[padded, flat] + work,
        compiler_params=params,
        cost_estimate=cost,
        name="inner_high",
    )(*fields, depth, drag, coriolis, p_mid, up_mid, de, dw, dn, dragn, send_a, *first)

    rim_pair = pltpu.VMEM((2 * levels, cols), F32)
    outs = pl.pallas_call(
        functools.partial(border_kernel, levels),
        out_shape=[jax.ShapeDtypeStruct(stack, F32)] * 3,
        in_specs=[vmem] * 13,
        out_specs=[hbm] * 3,
        scratch_shapes=[pltpu.VMEM(stack, F32)] * 3
        + [rim_pair] * 4
        + [pltpu.VMEM(plane, F32)] * 2
        + [pltpu.SemaphoreType.DMA((3, levels))],
        compiler_params=params,
        name="border",
    )(*second, send_a, send_b, recv_a, recv_b, lat_a, lat_b, rim_a, rim_b, drag, drag_ends)
    return tuple(x.reshape(levels, rows, cols) for x in outs)


def solution(mesh):
    stack, plane = P(None, "lat", "lon"), P("lat", "lon")
    return jax.shard_map(
        on_device,
        mesh=mesh,
        in_specs=(stack,) * 4 + (plane,) * 3,
        out_specs=(stack,) * 3,
        check_vma=False,
    )
```

```python
import functools

import jax
import jax.numpy as jnp
from jax import lax
from jax.experimental import pallas as pl
from jax.experimental.pallas import tpu as pltpu
from jax.sharding import PartitionSpec as P

DT = 0.25
GRAV = 0.1
F32 = jnp.float32
PAD = 8
RIM = 88
TAIL = 80
CHUNK = 8
STRIP = 32


def lanes(x, by):
    by %= x.shape[1]
    return x if by == 0 else pltpu.roll(x, by, 1)


def sublanes(x, by):
    by %= x.shape[0]
    return x if by == 0 else pltpu.roll(x, by, 0)


def iota(shape, dim):
    return lax.broadcasted_iota(jnp.int32, shape, dim)


def parity(axis):
    return lax.axis_index(axis) % 2 == 0


def face(side, ua, ub, ta, tb, ka, kb):
    return side * (0.0625 * ((ua + ub) * (ta + tb))) - 0.125 * ((ka + kb) * (tb - ta))


def square(x):
    rows, cols = x.shape
    return jnp.concatenate([x, jnp.zeros((cols - rows, cols), F32)], 0)


def rows_kernel(
    levels, t, u, v, kd, water, strata, friction, lat_a, lat_b, coriolis, drag,
    far_rows, water_rows, strata_rows, sem, plane_sem, drag_sem,
):
    rows, cols = coriolis.shape
    copies, planes = [], []
    lat_even = parity("lat")
    for side, message in enumerate((lat_a, lat_b)):
        north = lat_even if side == 0 else jnp.logical_not(lat_even)
        near = jnp.where(north, rows - 1, 0)
        far = jnp.where(north, rows - 2, 1)
        pair = pl.ds(jnp.where(north, rows - 2, 0), 2)
        for m, (src, dst) in enumerate(((water, water_rows), (strata, strata_rows))):
            planes.append(pltpu.make_async_copy(src.at[pair], dst.at[pl.ds(2 * side, 2)], plane_sem.at[m, side]))
        for q, src in enumerate((t, kd, v, u)):
            at = message.at[pl.ds(q * levels, levels)]
            copies.append(pltpu.make_async_copy(src.at[:, near], at, sem.at[side, q]))
        for q, src in enumerate((t, kd, v)):
            copies.append(pltpu.make_async_copy(src.at[:, far], far_rows.at[side, q], sem.at[side, 4 + q]))
    whole = pltpu.make_async_copy(friction, drag, drag_sem)
    for copy in planes + copies + [whole]:
        copy.start()
    row = iota((8, rows), 1) + lax.axis_index("lat") * rows
    total = rows * lax.axis_size("lat")
    line = DT * jnp.sin(jnp.pi * ((row.astype(F32) + 0.5) / total - 0.5))
    coriolis[...] = jnp.broadcast_to(line[0:1], (cols, rows)).T
    for copy in planes:
        copy.wait()
    for side, message in enumerate((lat_a, lat_b)):
        message[pl.ds(TAIL + 2, RIM - TAIL - 2)] = jnp.zeros((RIM - TAIL - 2, 1, cols), F32)
        north = lat_even if side == 0 else jnp.logical_not(lat_even)
        first, second = (
            (water_rows[pl.ds(2 * side + n, 1)] * strata_rows[pl.ds(2 * side + n, 1)]).astype(F32) for n in range(2)
        )
        message[pl.ds(TAIL, 1)] = jnp.where(north, second, first)
        message[pl.ds(TAIL + 1, 1)] = jnp.where(north, first, second)
    whole.wait()
    drag[...] = DT * drag[...]
    for copy in copies:
        copy.wait()
    level = iota((levels, 1, cols), 0).astype(F32)
    for side, message in enumerate((lat_a, lat_b)):
        north = lat_even if side == 0 else jnp.logical_not(lat_even)
        t1, k1, v1 = (message[pl.ds(q * levels, levels)] for q in range(3))
        t2, k2, v2 = (far_rows[side, q] for q in range(3))
        wet = level < jnp.minimum(message[pl.ds(TAIL, 1)], message[pl.ds(TAIL + 1, 1)])
        flux = face(jnp.where(north, 1.0, -1.0), v2, v1, t2, t1, k2, k1)
        message[pl.ds(4 * levels, levels)] = jnp.where(wet, flux, 0.0)


def pack_kernel(
    levels, t, u, v, kd, water, strata, drag,
    send_a, send_b, depth, drag_ends, gathered, ends,
):
    rows, cols = depth.shape
    lane = iota((STRIP, cols), 1)
    edge = (lane < 2) | (lane >= cols - 2)
    for r in range(0, rows, STRIP):
        at = pl.ds(r, STRIP)
        d = (water[at, :] * strata[at, :]).astype(F32)
        depth[at, :] = d
        gathered[2, at, :] = lanes(d, 2)
        gathered[3, at, :] = lanes(drag[at, :], 2)
        gathered[0, at, :] = jnp.zeros((STRIP, cols), F32)
        gathered[1, at, :] = jnp.zeros((STRIP, cols), F32)

    @pl.loop(0, levels // (2 * CHUNK))
    def one_piece(part):
        begin = pl.multiple_of(part * 2 * CHUNK * rows, rows)
        for f, full in enumerate((t, kd, u, v)):
            for r in range(0, rows, STRIP):
                acc = gathered[f // 2, pl.ds(r, STRIP), :]
                for n in range(2 * CHUNK):
                    x = jnp.where(edge, full[pl.ds(begin + n * rows + r, STRIP), :], 0.0)
                    to = 8 * (part * 2 * CHUNK + n) + 4 * (f % 2) + 2
                    acc = acc + pltpu.roll(x, to & (cols - 1), 1)
                gathered[f // 2, pl.ds(r, STRIP), :] = acc

    for n in range(2):
        ends[pl.ds(n * rows, rows), :] = gathered[n, :, :].T
    d = gathered[2, :, :].T
    drag_ends[...] = gathered[3, :, :].T[0:8]

    lon_even, lat_even = parity("lon"), parity("lat")

    def line_of(f, c):
        return ends[pl.ds((f // 2) * rows + 4 * (f % 2) + c, levels, stride=8), :]

    def side_of(side, near, far):
        t1, k1, u1, v1 = (line_of(f, near) for f in range(4))
        t2, k2, u2 = (line_of(f, far) for f in range(3))
        wet = iota((levels, cols), 0).astype(F32) < jnp.minimum(d[near : near + 1], d[far : far + 1])
        return t1, k1, u1, v1, jnp.where(wet, face(side, u2, u1, t2, t1, k2, k1), 0.0)

    for q, (east, west) in enumerate(zip(side_of(1.0, 1, 0), side_of(-1.0, 2, 3))):
        at = pl.ds(q * levels, levels)
        send_a[at, :] = jnp.where(lon_even, east, west)
        send_b[at, :] = jnp.where(lon_even, west, east)
    tail = (RIM - TAIL, cols)
    sub = iota(tail, 0)

    def tail_of(near, far):
        near, far = (jnp.broadcast_to(d[r : r + 1], tail) for r in (near, far))
        return jnp.where(sub == 0, near, jnp.where(sub == 1, far, 0.0))

    east, west = tail_of(1, 0), tail_of(2, 3)
    send_a[pl.ds(TAIL, RIM - TAIL), :] = jnp.where(lon_even, east, west)
    send_b[pl.ds(TAIL, RIM - TAIL), :] = jnp.where(lon_even, west, east)


def corner_kernel(levels, send_a, send_b, rim_b, rim_a, when, out_a, out_b):
    cols = send_a.shape[1]
    lon_even, lat_even = parity("lon"), parity("lat")
    a, b = rim_a[...], rim_b[...]
    b = jnp.where(lax.axis_index("lat") == 0, 0.0, b)
    south, north = square(jnp.where(lat_even, b, a)).T, square(jnp.where(lat_even, a, b)).T
    is_top = lax.axis_index("lat") == lax.axis_size("lat") - 1
    line = iota((1, cols), 1)
    turn = jnp.where((line >= 2 * levels) & (line < 4 * levels), -1.0, 1.0)
    first, last = north[0:1], north[cols - 1 : cols]
    first, last = jnp.where(is_top, turn * last, first), jnp.where(is_top, turn * first, last)
    tail = (RIM - TAIL, cols)
    sub = iota(tail, 0)
    for n, (main, out) in enumerate(((send_a, out_a), (send_b, out_b))):
        east = lon_even if n == 0 else jnp.logical_not(lon_even)
        s = jnp.broadcast_to(jnp.where(east, south[cols - 1 : cols], south[0:1]), tail)
        q = jnp.broadcast_to(jnp.where(east, last, first), tail)
        out[pl.ds(0, TAIL), :] = main[pl.ds(0, TAIL), :]
        depths = main[pl.ds(TAIL, RIM - TAIL), :]
        out[pl.ds(TAIL, RIM - TAIL), :] = jnp.where(sub == 2, s, jnp.where(sub == 3, q, depths))


def inner_kernel(
    levels, first, last, strip, t, u, v, kd, depth, drag, coriolis, p_in, up_in,
    t_out, u_out, v_out, p, up, de, dw, dn, dragn,
    fn, gu, gv, back,
):
    rows, cols = depth.shape
    zero = jnp.zeros((PAD, cols), F32)
    for ref in (fn, gu, back):
        ref[pl.ds(0, PAD), :] = zero

    shape = (strip, cols)
    lane = iota(shape, 1)
    row = iota(shape, 0)
    starts = range(0, rows, strip)
    for r in starts if p_in is None else ():
        here = pl.ds(r, strip)
        d, f = depth[here, :], drag[here, :]
        de[here, :] = jnp.where(lane < cols - 1, jnp.minimum(d, lanes(d, -1)), 0.0)
        dw[here, :] = jnp.where(lane > 0, jnp.minimum(d, lanes(d, 1)), 0.0)
        if r + strip < rows:
            north = pl.ds(r + 1, strip)
            dn[here, :] = jnp.minimum(d, depth[north, :])
            dragn[here, :] = drag[north, :]
        else:
            dn[here, :] = jnp.where(row < strip - 1, jnp.minimum(d, sublanes(d, -1)), 0.0)
            dragn[here, :] = sublanes(f, -1)

    up[...] = jnp.zeros(up.shape, F32) if p_in is None else up_in[...]
    p[...] = jnp.zeros(p.shape, F32) if p_in is None else p_in[...]

    def one_level(k):
        kf = k.astype(F32)
        base = pl.multiple_of(k * rows, rows)
        above = pl.multiple_of(jnp.minimum(k + 1, levels - 1) * rows, rows)
        for r in starts:
            here = out = pl.ds(base + r, strip)
            plane, padded, below = pl.ds(r, strip), pl.ds(PAD + r, strip), pl.ds(PAD + r - 1, strip)

            def north_of(ref, mid):
                return ref[pl.ds(base + r + 1, strip), :] if r + strip < rows else sublanes(mid, -1)

            d = depth[plane, :]
            t0, u0, v0, k0 = t[here, :], u[here, :], v[here, :], kd[here, :]
            wet, wet_e, wet_n = d > kf, de[plane, :] > kf, dn[plane, :] > kf

            t1, u1, k1 = lanes(t0, -1), lanes(u0, -1), lanes(k0, -1)
            flux = 0.0625 * ((u0 + u1) * (t0 + t1)) - 0.125 * ((k0 + k1) * (t1 - t0))
            flux = jnp.where(wet_e, flux, 0.0)
            change = lanes(flux, 1) - flux
            wet_w = dw[plane, :] > kf
            lap_u = jnp.where(wet_e, u1 - u0, 0.0) + jnp.where(wet_w, lanes(u0, 1) - u0, 0.0)
            lap_v = jnp.where(wet_e, lanes(v0, -1) - v0, 0.0) + jnp.where(wet_w, lanes(v0, 1) - v0, 0.0)

            t1, v1, k1 = north_of(t, t0), north_of(v, v0), north_of(kd, k0)
            flux = 0.0625 * ((v0 + v1) * (t0 + t1)) - 0.125 * ((k0 + k1) * (t1 - t0))
            flux = jnp.where(wet_n, flux, 0.0)
            lap = jnp.where(wet_n, north_of(u, u0) - u0, 0.0)
            lap2 = jnp.where(wet_n, v1 - v0, 0.0)
            fn[padded, :] = flux
            gu[padded, :] = lap
            gv[plane, :] = lap2
            change = change + (fn[below, :] - flux)
            lap_u = lap_u + (lap - gu[below, :])
            lap_v = lap_v + lap2

            higher = pl.ds(above + r, strip)
            rise = 0.125 * ((kd[higher, :] + k0) * (t[higher, :] - t0))
            rise = jnp.where(d > kf + 1.0, rise, 0.0)
            change = change + (rise - up[plane, :])
            up[plane, :] = rise

            t_next = jnp.where(wet, t0 + change, 0.0)
            t_out[out, :] = t_next
            p[padded, :] = p[padded, :] + t_next
            c, f = coriolis[plane, :], drag[plane, :]
            u_out[out, :] = u0 + (c * v0 + f * lap_u)
            v_out[out, :] = v0 + (f * lap_v - c * u0)

        middle = pl.ds(PAD, rows)
        back[middle, :] = 0.0125 * p[middle, :] - dragn[...] * gv[...]
        for r in starts:
            plane, out = pl.ds(r, strip), pl.ds(base + r, strip)
            wet = depth[plane, :] > kf
            mid = p[pl.ds(PAD + r, strip), :]
            slope = jnp.where(lane < cols - 1, lanes(mid, -1), 0.0) - jnp.where(lane > 0, lanes(mid, 1), 0.0)
            u_next = u_out[out, :] - 0.0125 * slope
            v_next = v_out[out, :] + back[pl.ds(PAD + r - 1, strip), :] - 0.0125 * p[pl.ds(PAD + r + 1, strip), :]
            u_out[out, :] = jnp.where(wet, u_next, 0.0)
            v_out[out, :] = jnp.where(wet, v_next, 0.0)

    @pl.loop(first, last)
    def each_level(k):
        one_level(k)


def levels_before(levels):
    lon, lat = lax.axis_index("lon"), lax.axis_index("lat")
    is_top = lat == lax.axis_size("lat") - 1
    is_last = lon == lax.axis_size("lon") - 1
    some = jnp.where(jnp.logical_not(is_top) & is_last, 0, levels // 2)
    some = jnp.where(is_top & (lon == 0), 3 * levels // 8, some)
    return jnp.where(is_top & (lon == 1), 5 * levels // 8, some)


def low_kernel(levels, strip, *refs):
    inner_kernel(levels, 0, levels_before(levels), strip, *refs[:7], None, None, *refs[7:])


def high_kernel(levels, strip, *refs):
    inputs, planes, (_, *low), outs, rest = refs[:9], refs[9:13], refs[13:17], refs[17:20], refs[20:]
    rows = refs[4].shape[0]
    split = levels_before(levels)

    @pl.loop(0, split)
    def hand_on(k):
        for src, dst in zip(low, outs):
            for r in range(0, rows, strip):
                at = pl.ds(pl.multiple_of(k * rows, rows) + r, strip)
                dst[at, :] = src[at, :]

    inner_kernel(levels, split, levels, strip, *inputs, *outs, *rest[:2], *planes, *rest[2:])


def border_kernel(
    levels, t_in, u_in, v_in,
    send_a, send_b, recv_a, recv_b, lat_a, lat_b, rim_a, rim_b, drag, drag_ends,
    t_out, u_out, v_out, tb, ub, vb, tr, ur, vr0, vr1, turned, turned_t, sem,
):
    rows, cols = drag.shape
    lon_even, lat_even = parity("lon"), parity("lat")
    is_top = lax.axis_index("lat") == lax.axis_size("lat") - 1

    def sides(even, a, b):
        a, b = a[...], b[...]
        return jnp.where(even, b, a), jnp.where(even, a, b)

    own_w, own_e = sides(lon_even, send_a, send_b)
    west, east = sides(lon_even, recv_a, recv_b)
    own_s, own_n = sides(lat_even, lat_a, lat_b)
    south, north = sides(lat_even, rim_a, rim_b)
    south = jnp.where(lax.axis_index("lat") == 0, 0.0, south)

    line = iota((RIM, 1), 0)
    turn = jnp.where((line >= 2 * levels) & (line < 4 * levels), -1.0, 1.0)
    mirrored = turn * jnp.take_along_axis(north, cols - 1 - iota((RIM, cols), 1), axis=1)
    north = jnp.where(is_top, mirrored, north)

    four, half = (4 * levels, cols), 2 * levels

    def stack(q, blocks):
        return jnp.concatenate([x[q * levels : (q + 1) * levels] for x in blocks], 0)

    def lines(rows_of_one):
        return jnp.concatenate([jnp.broadcast_to(x, (levels, cols)) for x in rows_of_one], 0)

    outside, inside = (west, east, south, north), (own_w, own_e, own_s, own_n)
    t1, k1, n1, s1, outer = (stack(q, outside) for q in range(5))
    t0, k0, n0, s0 = (stack(q, inside) for q in range(4))
    d1 = lines([x[TAIL : TAIL + 1] for x in outside])
    d0, d0b = (lines([x[TAIL + n : TAIL + n + 1] for x in inside]) for n in (0, 1))
    f0 = lines([drag_ends[2:3, :], drag_ends[1:2, :], drag[0:1, :], drag[rows - 1 : rows, :]])
    sub, lane = iota(four, 0), iota(four, 1)
    level_i = sub & (levels - 1)
    level = level_i.astype(F32)
    side = jnp.where((sub & levels) == 0, 1.0, -1.0)
    wet0, wet1 = level < d0, level < d1
    wet01 = level < jnp.minimum(d0, d1)

    inward = jnp.where(wet01, face(side, n1, n0, t1, t0, k1, k0), 0.0)

    def turn_columns(ref, lines_of):
        for g, x in enumerate(lines_of):
            ref[pl.ds(g, levels, stride=8), :] = x
        ref[...] = ref[...].T

    tail = (8, cols)
    sub8, lane8 = iota(tail, 0), iota((STRIP, cols), 1)
    one, wide = (lane8 < 1) | (lane8 >= cols - 1), (lane8 < 2) | (lane8 >= cols - 2)
    spots = ((one, cols - 1), (wide, cols - 2), (one, cols - 1 - 4))
    bufs, outs = (tb, ub, vb), (t_out, u_out, v_out)

    def copy_out(n, k):
        at = pl.ds(pl.multiple_of(k * rows, rows), rows)
        return pltpu.make_async_copy(bufs[n].at[at], outs[n].at[at], sem.at[n, k])

    def one_level(k, n, part, inside):
        base, buf = pl.multiple_of(k * rows, rows), bufs[n]
        mask, to = spots[n]
        by = (to - 8 * k) & (cols - 1)
        for r in range(0, rows, STRIP):
            moved = pltpu.roll((turned_t if n == 0 else turned)[pl.ds(r, STRIP), :], by, 1)
            old = part[pl.ds(pl.multiple_of(inside * rows, rows) + r, STRIP), :]
            buf[pl.ds(base + r, STRIP), :] = old + jnp.where(mask, moved, 0.0)

        def row_of(ref, s):
            return jnp.broadcast_to(ref[pl.ds(s * levels + k, 1), :], tail)

        for s, (near, far, begin) in enumerate(((0, 1, 0), (7, 6, rows - 8))):
            add = jnp.where(sub8 == near, row_of((tr, ur, vr0)[n], s), 0.0)
            if n == 2:
                add = jnp.where(sub8 == far, row_of(vr1, s), add)
            at = pl.ds(base + begin, 8)
            buf[at, :] = buf[at, :] + add
        copy_out(n, k).start()

    def all_levels(*which):
        @pl.loop(0, levels, step=CHUNK)
        def some_of_them(k):
            for i in range(CHUNK):
                for n in which:
                    one_level(k + i, n, (t_in, u_in, v_in)[n], k + i)

    tr[...] = inward[half:]
    turn_columns(turned_t, (inward[levels:half], inward[:levels]))
    all_levels(0)

    low, high = TAIL + 2, TAIL + 3
    ends_w, ends_e = square(west).T, square(east).T
    sw, nw = (ends_w[:, n : n + 1] for n in (low, high))
    se, ne = (ends_e[:, n : n + 1] for n in (low, high))
    before, after = (sw, se, sw, nw), (nw, ne, se, ne)

    def beyond(x, at):
        lo, hi = (
            jnp.concatenate(
                [jnp.broadcast_to(c[n : n + m], (levels, 1)) for c, (n, m) in zip(cells, at)], 0
            )
            for cells in (before, after)
        )
        lo, hi = jnp.broadcast_to(lo, four), jnp.broadcast_to(hi, four)
        return jnp.where(lane == 0, lo, lanes(x, 1)), jnp.where(lane == cols - 1, hi, lanes(x, -1))

    t_w, t_e = beyond(t1, ((0, levels),) * 4)
    k_w, k_e = beyond(k1, ((levels, levels),) * 4)
    s_w, s_e = beyond(s1, ((2 * levels, levels),) * 2 + ((3 * levels, levels),) * 2)
    d_w, d_e = beyond(d1, ((TAIL, 1),) * 4)
    flux_w = jnp.where(level < jnp.minimum(d_w, d1), face(1.0, s_w, s1, t_w, t1, k_w, k1), 0.0)
    flux_e = jnp.where(level < jnp.minimum(d1, d_e), face(1.0, s1, s_e, t1, t_e, k1, k_e), 0.0)
    rise = 0.125 * ((sublanes(k1, -1) + k1) * (sublanes(t1, -1) - t1))
    rise = jnp.where((level + 1.0 < d1) & (level_i < levels - 1), rise, 0.0)
    change = outer - inward + flux_w - flux_e + rise - sublanes(rise, 1)
    p1, dp0 = jnp.where(wet1, t1 + change, 0.0), inward
    step = 1
    while step < levels:
        p1 = p1 + jnp.where(level_i >= step, sublanes(p1, step), 0.0)
        dp0 = dp0 + jnp.where(level_i >= step, sublanes(dp0, step), 0.0)
        step *= 2
    dn = 0.0125 * (side * p1) + f0 * jnp.where(wet01, n1 - n0, 0.0)
    dn = jnp.where(wet0, dn, 0.0)
    dn2 = jnp.where(level < d0b, 0.0125 * (side * dp0), 0.0)
    slope = jnp.where(lane < cols - 1, lanes(dp0, -1), 0.0) - jnp.where(lane > 0, lanes(dp0, 1), 0.0)
    ds = f0 * jnp.where(wet01, s1 - s0, 0.0) - 0.0125 * slope
    ds = jnp.where(wet0, ds, 0.0)
    ur[...] = ds[half:]
    vr0[...] = dn[half:]
    vr1[...] = dn2[half:]

    turn_columns(
        turned, (dn2[levels:half], dn[levels:half], dn[:levels], dn2[:levels], ds[levels:half], ds[:levels])
    )
    all_levels(1, 2)

    @pl.loop(0, levels)
    def finish(k):
        for n in range(3):
            copy_out(n, k).wait()


def on_device(t, u, v, kd, friction, water, strata):
    levels, rows, cols = t.shape
    lon_n, lat_n = lax.axis_size("lon"), lax.axis_size("lat")
    vmem = pl.BlockSpec(memory_space=pltpu.VMEM)
    hbm = pl.BlockSpec(memory_space=pltpu.HBM)
    params = pltpu.CompilerParams(vmem_limit_bytes=12 * 1024 * 1024)
    tall = levels * rows
    plane, message, stack = (rows, cols), (RIM, cols), (tall, cols)

    def in_hbm(*arrays):
        return [pltpu.with_memory_space_constraint(x, pltpu.HBM) for x in arrays]

    lat_a, lat_b, coriolis, drag = pl.pallas_call(
        functools.partial(rows_kernel, levels),
        out_shape=[pltpu.VMEM((RIM, 1, cols), F32)] * 2 + [pltpu.VMEM(plane, F32)] * 2,
        in_specs=[hbm] * 7,
        out_specs=[vmem] * 4,
        scratch_shapes=[pltpu.VMEM((2, 3, levels, 1, cols), F32)]
        + [pltpu.VMEM((4, 1, cols), jnp.int32)] * 2
        + [pltpu.SemaphoreType.DMA((2, 7)), pltpu.SemaphoreType.DMA((2, 2)), pltpu.SemaphoreType.DMA],
        compiler_params=params,
        name="rows",
    )(
        *in_hbm(*[x.reshape(levels, rows, 1, cols) for x in (t, u, v, kd)]),
        *in_hbm(*[x.reshape(rows, 1, cols) for x in (water, strata)], friction),
    )
    lat_a, lat_b = lat_a.reshape(message), lat_b.reshape(message)
    lat_pairs = [(i, i ^ 1) for i in range(lat_n)]
    cross = []
    for m in range(lon_n):
        for i in range(1, lat_n - 1, 2):
            here, north = m * lat_n + i, m * lat_n + i + 1
            cross += [(here, north), (north, here)]
        cross.append((m * lat_n + lat_n - 1, (lon_n - 1 - m) * lat_n + lat_n - 1))
        cross.append((m * lat_n, (m ^ 1) * lat_n))
    rim_a = lax.ppermute(lat_a, "lat", lat_pairs)
    rim_b = lax.ppermute(lat_b, ("lon", "lat"), cross)

    fields = [x.reshape(stack) for x in (t, u, v, kd)]
    send_a, send_b, depth, drag_ends = pl.pallas_call(
        functools.partial(pack_kernel, levels),
        out_shape=[pltpu.VMEM(s, F32) for s in (message, message, plane, (8, cols))],
        in_specs=[vmem] * 7,
        out_specs=[vmem] * 4,
        scratch_shapes=[pltpu.VMEM((4, rows, cols), F32), pltpu.VMEM((2 * rows, cols), F32)],
        compiler_params=params,
        name="pack",
    )(*fields, water, strata, drag)
    padded, flat = pltpu.VMEM((rows + 2 * PAD, cols), F32), pltpu.VMEM(plane, F32)
    whole = pltpu.VMEM(stack, F32)
    work = [padded, padded, flat, padded]
    cost = pl.CostEstimate(flops=50 * tall * cols, bytes_accessed=1 << 20, transcendentals=0)
    *first, p_mid, up_mid, de, dw, dn, dragn = pl.pallas_call(
        functools.partial(low_kernel, levels, STRIP),
        out_shape=[whole] * 3 + [padded] + [flat] * 5,
        in_specs=[vmem] * 7,
        out_specs=[vmem] * 9,
        scratch_shapes=work,
        compiler_params=params,
        cost_estimate=cost,
        name="inner_low",
    )(*fields, depth, drag, coriolis)
    send_a, send_b = pl.pallas_call(
        functools.partial(corner_kernel, levels),
        out_shape=[pltpu.VMEM(message, F32)] * 2,
        in_specs=[vmem] * 5,
        out_specs=[vmem] * 2,
        compiler_params=params,
        name="corners",
    )(send_a, send_b, rim_b, rim_a, up_mid)
    lon_pairs = [(i, i ^ 1) for i in range(lon_n)]
    lon_cross = [(i, (i + 1) % lon_n if i % 2 else (i - 1) % lon_n) for i in range(lon_n)]
    recv_b = lax.ppermute(send_b, "lon", lon_cross)
    recv_a = lax.ppermute(send_a, "lon", lon_pairs)

    second = pl.pallas_call(
        functools.partial(high_kernel, levels, STRIP),
        out_shape=[whole] * 3,
        in_specs=[vmem] * 17,
        out_specs=[vmem] * 3,
        scratch_shapes=[padded, flat] + work,
        compiler_params=params,
        cost_estimate=cost,
        name="inner_high",
    )(*fields, depth, drag, coriolis, p_mid, up_mid, de, dw, dn, dragn, send_a, *first)

    rim_pair = pltpu.VMEM((2 * levels, cols), F32)
    outs = pl.pallas_call(
        functools.partial(border_kernel, levels),
        out_shape=[jax.ShapeDtypeStruct(stack, F32)] * 3,
        in_specs=[vmem] * 13,
        out_specs=[hbm] * 3,
        scratch_shapes=[pltpu.VMEM(stack, F32)] * 3
        + [rim_pair] * 4
        + [pltpu.VMEM(plane, F32)] * 2
        + [pltpu.SemaphoreType.DMA((3, levels))],
        compiler_params=params,
        name="border",
    )(*second, send_a, send_b, recv_a, recv_b, lat_a, lat_b, rim_a, rim_b, drag, drag_ends)
    return tuple(x.reshape(levels, rows, cols) for x in outs)


def solution(mesh):
    stack, plane = P(None, "lat", "lon"), P("lat", "lon")
    return jax.shard_map(
        on_device,
        mesh=mesh,
        in_specs=(stack,) * 4 + (plane,) * 3,
        out_specs=(stack,) * 3,
        check_vma=False,
    )
```
